32 devices in a mesh: dp: 2 (over x), row: 4 (over z), col: 4 (over y, core).
Axes of the slice: x: 2, y: 2, z: 4, core: 2. Of those that a mesh axis runs over, the one named last changes fastest.
Arguments:
- inputs: bfloat16 [8192, 1024], P(('dp', 'row', 'col')), may hold values from -6 to 6
- lengths: int32 [2, 8], P('dp'), may hold values from 1 to 1024, 4096 in all within a row
- routes: int32 [8192, 8], P(('dp', 'row', 'col')), may hold values from 0 to 31, all different within a row; in each aligned block of 256 rows (0 to 255, 256 to 511, ...) at most 96 rows name the same one
- norm1_gain: float32 [1024], replicated, may hold values from 0.25 to 1.75
- w_query: bfloat16 [1024, 1024], P('row', 'col'), may hold values from -0.1875 to 0.1875
- key_weight: bfloat16 [1024, 512], P('row', 'col'), may hold values from -0.1875 to 0.1875
- value_weight: bfloat16 [1024, 512], P('row', 'col'), may hold values from -0.1875 to 0.1875
- w_output: bfloat16 [1024, 1024], P('col', 'row'), may hold values from -1.5 to 1.5
- norm2_gain: float32 [1024], replicated, may hold values from 0.25 to 1.75
- router: bfloat16 [1024, 32], replicated, may hold values from -0.09375 to 0.09375
- w_gate: bfloat16 [32, 1024, 512], P('dp'), may hold values from -0.1875 to 0.1875
- w_up: bfloat16 [32, 1024, 512], P('dp'), may hold values from -0.1875 to 0.1875
- w_down: bfloat16 [32, 512, 1024], P('dp'), may hold values from -1 to 1
- d_output: bfloat16 [8192, 1024], P(('dp', 'row', 'col')), may hold values from -6 to 6
Outputs:
- output: bfloat16 [8192, 1024], P(('dp', 'row', 'col'))
- d_inputs: float32 [8192, 1024], P(('dp', 'row', 'col'))
- d_norm1_gain: float32 [1024], replicated
- d_w_query: float32 [1024, 1024], P('row', 'col')
- d_w_key: float32 [1024, 512], P('row', 'col')
- d_w_value: float32 [1024, 512], P('row', 'col')
- d_w_output: float32 [1024, 1024], P('col', 'row')
- d_norm2_gain: float32 [1024], replicated
- d_router: float32 [1024, 32], replicated
- d_w_gate: float32 [32, 1024, 512], P('dp', ('row', 'col'))
- d_w_up: float32 [32, 1024, 512], P('dp', ('row', 'col'))
- d_w_down: float32 [32, 512, 1024], P('dp', None, ('row', 'col'))
The draws below stay inside these ranges and needn't reach their ends.
Inputs may be any that keep to these rules, and one draw needn't show every extreme that they name: Row g gives the lengths of group g's sequences in order; each row sums to 4096, and its largest entry is 1024. `routes`: each row names 8 different experts. In each aligned block of 256 rows no expert is named more than 96 times.
All inputs are finite; a program needn't handle non-finite values.
Results may differ from the reference program's by a relative error of at most 0.018.
Values may be sent and summed in bfloat16 or wider, within the bound.
No kernel may reach another device: no remote copies, remote signals or barrier semaphores. Data moves between devices by JAX's collectives and lax.ppermute only.
A program may use at most 320 MiB of HBM per device.

```python
import math
from functools import partial
import jax
import jax.numpy as jnp
import numpy as np
from jax import lax

MODEL_WIDTH = 1024
QUERY_HEADS = 16
KEY_VALUE_HEADS = 8
HEAD_SIZE = 64
FF = 512
EXPERTS = 32
TOPK = 8
TOK_DEV = 256
MAX_LEN = 1024
GROUP_TOKENS = 4096
TOKENS = 8192
SEQS = 8
CAP = 96
N_DP = 2


def level_of(stream_key, extent, pieces, smallest, top_value):
    level, own = 1.0, jax.random.fold_in(stream_key, 6)
    for dim, blocks in pieces:
        heights = jnp.exp(jax.random.uniform(jax.random.fold_in(own, dim), (blocks,), jnp.float32, smallest / len(pieces), top_value / len(pieces)))
        level = level * jnp.repeat(heights, extent[dim] // blocks).reshape([-1 if axis == dim else 1 for axis in range(len(extent))])
    return level


def length_profile(amount, total, most, lean):
    portions = [(1 << 20) // math.isqrt(grade ** lean) + 1 for grade in range(2, amount + 1)]
    surplus, counts = total - most - (amount - 1), [1] * (amount - 1)
    while surplus > 0:
        candidates = [i for i in range(amount - 1) if counts[i] < most]
        pool, remaining = sum([portions[i] for i in candidates]), surplus
        for i in candidates:
            addition = min(most - counts[i], max(1, remaining * portions[i] // pool), surplus)
            counts[i] = counts[i] + addition
            surplus = surplus - addition
    return np.array([most] + counts)


def uneven(own_key, count, total, bound, skew):
    if count == 2:
        one = jax.random.randint(own_key, (), max(1, total - bound), min(bound, total - 1) + 1)
        return jnp.stack([one, total - one])
    sizes = jnp.asarray(length_profile(count, total, bound, skew), jnp.int32)
    couples = (count - 1) // 2
    giver, taker = sizes[1:1 + 2 * couples:2], sizes[2:2 + 2 * couples:2]
    room = jnp.minimum(giver - 1, bound - taker)
    shifted = jax.random.randint(jax.random.fold_in(own_key, 1), (couples,), 0, 1 << 20) % (room + 1)
    sizes = sizes.at[1:1 + 2 * couples:2].set(giver - shifted).at[2:2 + 2 * couples:2].set(taker + shifted)
    return sizes[jax.random.permutation(jax.random.fold_in(own_key, 2), count)]


def deal_out(stream_key, own, number, rows, count, top, most, lean):
    order = jax.random.permutation(stream_key, count)
    heavy_load, usual = shares(count, rows * top, most, lean, True), shares(count, rows * top, most, lean, False)
    places = jnp.arange(count)

    def named(tallies, rotation):
        used = int((tallies > 0).sum())
        fixed = max(1, used // 4)
        moved = fixed + (places - fixed + rotation * (used - fixed)) % max(1, count - fixed)
        return jnp.zeros((count,), jnp.int32).at[order[jnp.where(places < fixed, places, moved)]].set(jnp.asarray(tallies, jnp.int32))

    tallies = jnp.where(number % 4 == 0, named(heavy_load, number // 4), named(usual, number - number // 4 - 1))
    mixed = jax.random.permutation(jax.random.fold_in(own, 3), count)
    giver, sink = mixed[0:count // 2 * 2:2], mixed[1:count // 2 * 2:2]
    slack = jnp.minimum(tallies[giver] - 1, most - tallies[sink]) // 2
    slack = jnp.where((giver == order[0]) | (sink == order[0]) | (tallies[sink] == 0), 0, jnp.maximum(slack, 0))
    moved = jax.random.randint(jax.random.fold_in(own, 4), (count // 2,), 0, 1 << 20) % (slack + 1)
    tallies = tallies.at[giver].add(-moved).at[sink].add(moved)
    labels = jnp.searchsorted(jnp.cumsum(tallies), jnp.arange(rows * top), side="right").astype(jnp.int32)
    listing = labels.reshape(top, rows).T
    listing = listing[jax.random.permutation(jax.random.fold_in(own, 1), rows)]
    rotation = jax.random.randint(jax.random.fold_in(own, 2), (rows, 1), 0, top)
    return jnp.take_along_axis(listing, (jnp.arange(top)[None, :] + rotation) % top, axis=1)


def shares(number_of, total, reach, lean, full):
    weights = [(1 << 20) // math.isqrt(rank ** lean) + 1 for rank in range(1, number_of + 1)]
    largest = reach if full else min(reach, max(-(-total // number_of), total * weights[0] // sum(weights)))
    least = 1 if total - largest >= number_of - 1 else 0
    given, spare = [largest] + [least] * (number_of - 1), total - largest - least * (number_of - 1)
    while spare > 0:
        movable = [i for i in range(1, number_of) if given[i] < largest] or [i for i in range(1, number_of) if given[i] < reach]
        mass, remaining = sum([weights[i] for i in movable]), spare
        for i in movable:
            addition = min(reach - given[i], max(1, remaining * weights[i] // mass), spare)
            given[i] = given[i] + addition
            spare = spare - addition
    return np.array(given)


def scatter_about(own_key, dims, deviation, limit, pieces=(), kind=jnp.bfloat16):
    entries = jax.random.normal(own_key, dims, jnp.float32) * deviation
    if len(pieces) > 0:
        entries = level_of(own_key, dims, pieces, -0.22, 0.18) * entries
    return jnp.clip(entries, min=-limit, max=limit).astype(kind)


def setup_inputs(seed: int = 0) -> dict:
    key_of = jax.random.split(jax.random.key(seed), 15)
    inputs = scatter_about(key_of[0], (TOKENS, MODEL_WIDTH), 1.0, 6.0, ((0, 32),))
    lengths = jax.vmap(lambda own: uneven(own, SEQS, GROUP_TOKENS, MAX_LEN, 2))(jax.random.split(key_of[1], N_DP)).reshape((N_DP, SEQS)).astype(jnp.int32)
    routes_keys = jax.random.split(jax.random.fold_in(key_of[2], 1), TOKENS // TOK_DEV)
    routes_turns = jax.random.permutation(jax.random.fold_in(key_of[2], 3), TOKENS // TOK_DEV)
    routes = jax.vmap(lambda own, number: deal_out(jax.random.fold_in(key_of[2], 2), own, number, TOK_DEV, EXPERTS, TOPK, CAP, 1))(routes_keys, routes_turns).reshape((TOKENS, TOPK))
    norm1_gain = jnp.clip(1.0 + 0.15 * jax.random.normal(key_of[3], (MODEL_WIDTH,), jnp.float32), 0.25, 1.75)
    w_query = scatter_about(key_of[4], (MODEL_WIDTH, QUERY_HEADS * HEAD_SIZE), MODEL_WIDTH ** -0.5, 0.1875, ((0, 4), (1, 4)))
    key_weight = scatter_about(key_of[5], (MODEL_WIDTH, KEY_VALUE_HEADS * HEAD_SIZE), MODEL_WIDTH ** -0.5, 0.1875, ((0, 4), (1, 4)))
    value_weight = scatter_about(key_of[6], (MODEL_WIDTH, KEY_VALUE_HEADS * HEAD_SIZE), MODEL_WIDTH ** -0.5, 0.1875, ((0, 4), (1, 4)))
    w_output = scatter_about(key_of[7], (QUERY_HEADS * HEAD_SIZE, MODEL_WIDTH), (QUERY_HEADS * HEAD_SIZE // 64) ** -0.5, 1.5, ((0, 4), (1, 4)))
    norm2_gain = jnp.clip(1.0 + 0.15 * jax.random.normal(key_of[8], (MODEL_WIDTH,), jnp.float32), 0.25, 1.75)
    router = scatter_about(key_of[9], (MODEL_WIDTH, EXPERTS), (4 * MODEL_WIDTH) ** -0.5, 0.09375)
    w_gate = scatter_about(key_of[10], (EXPERTS, MODEL_WIDTH, FF), MODEL_WIDTH ** -0.5, 0.1875, ((0, 2),))
    w_up = scatter_about(key_of[11], (EXPERTS, MODEL_WIDTH, FF), MODEL_WIDTH ** -0.5, 0.1875, ((0, 2),))
    w_down = scatter_about(key_of[12], (EXPERTS, FF, MODEL_WIDTH), (FF // 16) ** -0.5, 1.0, ((0, 2),))
    d_output = scatter_about(key_of[13], (TOKENS, MODEL_WIDTH), 1.0, 6.0, ((0, 32),))
    return {"inputs": inputs, "lengths": lengths, "routes": routes, "norm1_gain": norm1_gain, "w_query": w_query, "key_weight": key_weight, "value_weight": value_weight, "w_output": w_output, "norm2_gain": norm2_gain, "router": router, "w_gate": w_gate, "w_up": w_up, "w_down": w_down, "d_output": d_output}


EPSILON = 1e-06
MASKED_SCORE = -1e+30
ROPE_BASE = 10000.0
HIGHEST_PRECISION = lax.Precision.HIGHEST

@jax.custom_vjp
def low(v):
    return lax.optimization_barrier(v.astype(jnp.bfloat16)).astype(jnp.float32)

@jax.custom_vjp
def low_back(v):
    return v

def low_keep(v):
    return (low(v), None)

def low_pass(kept, grad):
    return (grad,)

def back_keep(v):
    return (v, None)

def back_low(kept, grad):
    return (low(grad),)
low.defvjp(low_keep, low_pass)
low_back.defvjp(back_keep, back_low)

def places(seq_lengths, total_rows):
    seq_ends = jnp.cumsum(seq_lengths).astype(jnp.int32)
    row_spots = jnp.arange(total_rows, dtype=jnp.int32)
    passed = (row_spots[:, None] >= seq_ends[None, :]).astype(jnp.int32)
    segment_ids = lax.optimization_barrier(jnp.sum(passed, axis=1)).astype(jnp.int32)
    seq_starts = lax.optimization_barrier(jnp.sum(passed * seq_lengths[None, :], axis=1)).astype(jnp.int32)
    return (segment_ids, row_spots - seq_starts)

def angle_tables(positions, half_dim):
    frequency = jnp.exp(-math.log(ROPE_BASE) * jnp.arange(half_dim, dtype=jnp.float32) / half_dim)
    angles = positions.astype(jnp.float32)[:, None] * frequency[None, :]
    return (jnp.cos(angles), jnp.sin(angles))

def rotate_pairs(value_rows, cos_table, sin_table, sign_value):
    row_total = value_rows.shape[0]
    half_dim = cos_table.shape[1]
    shaped = value_rows.reshape(row_total, -1, 2, half_dim)
    first_half = shaped[:, :, 0]
    second_half = shaped[:, :, 1]
    cos_part = cos_table[:, None, :]
    sin_part = sign_value * sin_table[:, None, :]
    turned = jnp.stack([first_half * cos_part - second_half * sin_part, second_half * cos_part + first_half * sin_part], axis=2)
    return turned.reshape(row_total, -1)

def attention(query_rows, key_rows, value_rows, segment_ids):
    block_rows = TOK_DEV
    rows_returned_back = -(-(MAX_LEN - 1) // block_rows) * block_rows
    window = rows_returned_back + block_rows
    group_blocks = GROUP_TOKENS // block_rows
    group_portion = QUERY_HEADS // KEY_VALUE_HEADS
    score_scale = 1.0 / math.sqrt(HEAD_SIZE)
    grouped_queries = query_rows.reshape(N_DP, GROUP_TOKENS, KEY_VALUE_HEADS, group_portion, HEAD_SIZE)
    grouped_keys = jnp.pad(key_rows.reshape(N_DP, GROUP_TOKENS, KEY_VALUE_HEADS, HEAD_SIZE), ((0, 0), (rows_returned_back, 0), (0, 0), (0, 0)))
    grouped_values = jnp.pad(value_rows.reshape(N_DP, GROUP_TOKENS, KEY_VALUE_HEADS, HEAD_SIZE), ((0, 0), (rows_returned_back, 0), (0, 0), (0, 0)))
    segment_pad = jnp.pad(segment_ids, ((0, 0), (rows_returned_back, 0)), constant_values=-1)

    def one_block(block_index):
        group_index = block_index // group_blocks
        first_row = block_index % group_blocks * block_rows
        query_group = lax.dynamic_index_in_dim(grouped_queries, group_index, 0, keepdims=False)
        key_group = lax.dynamic_index_in_dim(grouped_keys, group_index, 0, keepdims=False)
        value_group = lax.dynamic_index_in_dim(grouped_values, group_index, 0, keepdims=False)
        seg_group = lax.dynamic_index_in_dim(segment_ids, group_index, 0, keepdims=False)
        seg_padded = lax.dynamic_index_in_dim(segment_pad, group_index, 0, keepdims=False)
        query_block = lax.dynamic_slice_in_dim(query_group, first_row, block_rows, 0)
        key_block = lax.dynamic_slice_in_dim(key_group, first_row, window, 0)
        value_block = lax.dynamic_slice_in_dim(value_group, first_row, window, 0)
        query_seg = lax.dynamic_slice_in_dim(seg_group, first_row, block_rows, 0)
        key_seg = lax.dynamic_slice_in_dim(seg_padded, first_row, window, 0)
        query_at = first_row + jnp.arange(block_rows, dtype=jnp.int32)
        key_at = first_row - rows_returned_back + jnp.arange(window, dtype=jnp.int32)
        allowed = (query_seg[:, None] == key_seg[None, :]) & (key_at[None, :] <= query_at[:, None])
        scores = low_back(jnp.einsum('bkgd,skd->kbgs', query_block, key_block, precision=HIGHEST_PRECISION) * score_scale)
        scores = jnp.where(allowed[None, :, None, :], scores, MASKED_SCORE)
        row_top = lax.optimization_barrier(jnp.max(scores, axis=3, keepdims=True))
        exp_scores = jnp.exp(scores - row_top)
        probabilities = exp_scores / lax.optimization_barrier(jnp.sum(exp_scores, axis=3, keepdims=True))
        mixed_heads = jnp.einsum('kbgs,skd->bkgd', low(probabilities), value_block, precision=HIGHEST_PRECISION)
        return mixed_heads.reshape(block_rows, QUERY_HEADS * HEAD_SIZE)
    blocks_out = lax.map(jax.checkpoint(one_block), jnp.arange(N_DP * group_blocks, dtype=jnp.int32))
    return blocks_out.reshape(TOKENS, QUERY_HEADS * HEAD_SIZE)

def expert_block(w_gate, w_up, w_down, block_items):
    normed_rows, gate_rows, route_rows = block_items
    assign_total = TOK_DEV * TOPK
    flat_routes = route_rows.reshape(-1)
    expert_ids = jnp.arange(EXPERTS, dtype=jnp.int32)
    flat_hot = (flat_routes[:, None] == expert_ids[None, :]).astype(jnp.int32)
    running = jnp.cumsum(flat_hot, axis=0).astype(jnp.int32)
    slot_rank = (lax.optimization_barrier(jnp.sum(flat_hot * running, axis=1)) - 1).astype(jnp.int32)
    slot_index = flat_routes * CAP + slot_rank
    slot_owner = jnp.full((EXPERTS * CAP,), assign_total, jnp.int32).at[slot_index].set(jnp.arange(assign_total, dtype=jnp.int32))
    owner_row = jnp.where(slot_owner < assign_total, slot_owner // TOPK, TOK_DEV)
    padded_rows = jnp.concatenate([normed_rows, jnp.zeros((1, MODEL_WIDTH), jnp.float32)], axis=0)
    expert_in = low_back(padded_rows[owner_row]).reshape(EXPERTS, CAP, MODEL_WIDTH)
    gate_vals = low_back(jnp.einsum('ecd,edf->ecf', expert_in, w_gate, precision=HIGHEST_PRECISION))
    up_vals = low_back(jnp.einsum('ecd,edf->ecf', expert_in, w_up, precision=HIGHEST_PRECISION))
    inner_vals = low(jax.nn.silu(gate_vals) * up_vals)
    expert_out = low(low_back(jnp.einsum('ecf,efd->ecd', inner_vals, w_down, precision=HIGHEST_PRECISION)))
    picked = expert_out.reshape(EXPERTS * CAP, MODEL_WIDTH)[slot_index].reshape(TOK_DEV, TOPK, MODEL_WIDTH)
    return lax.optimization_barrier(jnp.sum(gate_rows[:, :, None] * picked, axis=1))

def layer(lengths, routes, inputs, norm1_gain, w_query, key_weight, value_weight, w_output, norm2_gain, router, w_gate, w_up, w_down):
    rinv_one = lax.rsqrt(lax.optimization_barrier(jnp.mean(inputs * inputs, axis=1, keepdims=True)) + EPSILON)
    normed_one = low(inputs * rinv_one * norm1_gain)
    query_raw = low_back(jnp.dot(normed_one, w_query, precision=HIGHEST_PRECISION))
    key_raw = low_back(jnp.dot(normed_one, key_weight, precision=HIGHEST_PRECISION))
    value_raw = low_back(jnp.dot(normed_one, value_weight, precision=HIGHEST_PRECISION))
    segment_ids, positions = jax.vmap(partial(places, total_rows=GROUP_TOKENS))(lengths)
    cos_table, sin_table = angle_tables(positions.reshape(-1), HEAD_SIZE // 2)
    query_rows = low(rotate_pairs(query_raw, cos_table, sin_table, 1.0))
    key_rows = low(rotate_pairs(key_raw, cos_table, sin_table, 1.0))
    value_rows = low(value_raw)
    heads = low(low_back(attention(query_rows, key_rows, value_rows, segment_ids)))
    attn = low_back(jnp.dot(heads, w_output, precision=HIGHEST_PRECISION))
    hidden = inputs + attn
    rinv_two = lax.rsqrt(lax.optimization_barrier(jnp.mean(hidden * hidden, axis=1, keepdims=True)) + EPSILON)
    normed_two = low(hidden * rinv_two * norm2_gain)
    logits = low_back(jnp.dot(normed_two, router, precision=HIGHEST_PRECISION))
    chosen = jnp.take_along_axis(logits, routes, axis=1)
    gates = jax.nn.softmax(chosen, axis=1)
    device_blocks = TOKENS // TOK_DEV
    mixture = lax.map(jax.checkpoint(partial(expert_block, w_gate, w_up, w_down)), (normed_two.reshape(device_blocks, TOK_DEV, MODEL_WIDTH), gates.reshape(device_blocks, TOK_DEV, TOPK), routes.reshape(device_blocks, TOK_DEV, TOPK)))
    return hidden + mixture.reshape(TOKENS, MODEL_WIDTH)

def reference(inputs, lengths, routes, norm1_gain, w_query, key_weight, value_weight, w_output, norm2_gain, router, w_gate, w_up, w_down, d_output):
    floats = tuple((item.astype(jnp.float32) for item in (inputs, norm1_gain, w_query, key_weight, value_weight, w_output, norm2_gain, router, w_gate, w_up, w_down)))
    forward_fn = partial(layer, lengths, routes)
    result, pull_back = jax.vjp(forward_fn, *floats)
    grads = pull_back(d_output.astype(jnp.float32))
    return (result.astype(jnp.bfloat16), grads[0], grads[1], grads[2], grads[3], grads[4], grads[5], grads[6], grads[7], grads[8], grads[9], grads[10])
```

```python
import functools
import math

import jax
import jax.numpy as jnp
from jax import lax
from jax.experimental import pallas as pl
from jax.experimental.pallas import tpu as pltpu
from jax.sharding import PartitionSpec as P

HEAD_SIZE = 64
EXPERTS = 32
TOPK = 8
MAX_LEN = 1024
CAP = 96

EPSILON = 1e-06
MASKED_SCORE = -1e30
ROPE_BASE = 10000.0
LANES = 128
MIB = 1024 * 1024


def nt_dot(left, right):
    return lax.dot_general(
        left, right, (((1,), (1,)), ((), ())), preferred_element_type=jnp.float32
    )


def tn_dot(left, right):
    return lax.dot_general(
        left, right, (((0,), (0,)), ((), ())), preferred_element_type=jnp.float32
    )


def nn_dot(left, right):
    return jnp.dot(left, right, preferred_element_type=jnp.float32)


def xor_perm(size, step):
    return [(i, i ^ step) for i in range(size)]


def swap(value, axis, step):
    return lax.ppermute(value, axis, xor_perm(lax.axis_size(axis), step))


def place(blocks, indices):
    out = jnp.zeros((len(blocks),) + blocks[0].shape, blocks[0].dtype)
    for block, index in zip(blocks, indices):
        out = lax.dynamic_update_index_in_dim(out, block, index, 0)
    return out


def gather_col(value):
    mine = lax.axis_index("col")
    if lax.axis_size("col") != 4:
        return lax.all_gather(value, "col")
    far = swap(value, "col", 2)
    near = swap(value, "col", 1)
    cross = swap(far, "col", 1)
    return place([value, near, far, cross], [mine, mine ^ 1, mine ^ 2, mine ^ 3])


def exchange_col(blocks):
    mine = lax.axis_index("col")
    size = lax.axis_size("col")
    if size & (size - 1):
        return lax.all_to_all(blocks, "col", split_axis=0, concat_axis=0, tiled=True)

    def pick(index):
        return lax.dynamic_index_in_dim(blocks, index, 0, keepdims=False)

    got = [pick(mine)]
    for step in range(1, size):
        got.append(swap(pick(mine ^ step), "col", step))
    return place(got, [mine ^ step for step in range(size)])


def scatter_col(blocks):
    mine = lax.axis_index("col")
    if lax.axis_size("col") != 4:
        return lax.psum_scatter(
            blocks.astype(jnp.float32), "col", scatter_dimension=0, tiled=False
        )

    def pick(index):
        return lax.dynamic_index_in_dim(blocks, index, 0, keepdims=False)

    def wide(value):
        return value.astype(jnp.float32)

    away = jnp.stack([pick(mine ^ 1), pick(mine ^ 3)])
    came = swap(away, "col", 1)
    far_sum = (wide(pick(mine ^ 2)) + wide(came[1])).astype(jnp.bfloat16)
    far = swap(far_sum, "col", 2)
    return wide(pick(mine)) + wide(came[0]) + wide(far)


def gather_row(value):
    size = lax.axis_size("row")
    mine = lax.axis_index("row")
    blocks = [value]
    for step in range(1, size):
        blocks.append(lax.ppermute(value, "row", [(i, (i + step) % size) for i in range(size)]))
    return place(blocks, [lax.rem(mine - step + size, size) for step in range(size)])


def scatter_row(blocks):
    size = lax.axis_size("row")
    mine = lax.axis_index("row")
    total = None
    for step in range(size):
        block = lax.dynamic_index_in_dim(blocks, lax.rem(mine + step, size), 0, keepdims=False)
        if step:
            block = lax.ppermute(block, "row", [(i, (i + step) % size) for i in range(size)])
        block = block.astype(jnp.float32)
        total = block if total is None else total + block
    return total


def sum_over(value, axis):
    size = lax.axis_size(axis)
    if size & (size - 1):
        return lax.psum(value, axis)
    step = 1
    while step < size:
        value = value + swap(value, axis, step)
        step *= 2
    return value


def gather_tokens(value, axes):
    if axes != ("dp", "col") or lax.axis_size("dp") != 2 or lax.axis_size("col") != 4:
        return lax.all_gather(value, axes)
    mine_dp, mine_col = lax.axis_index("dp"), lax.axis_index("col")
    half = value.shape[0] // 2
    along_x = swap(value, "dp", 1)
    along_y = swap(value, "col", 2)
    near = swap(value, "col", 1)
    cross_low = swap(along_x[:half], "col", 2)
    cross_high = swap(along_y[half:], "dp", 1)
    near_x = swap(along_x, "col", 1)
    near_y = swap(along_y, "col", 1)
    cross = jnp.concatenate([cross_low, cross_high], axis=0)
    near_cross = swap(cross, "col", 1)
    here, there = mine_dp * 4, (1 - mine_dp) * 4
    return place(
        [value, near, along_y, near_y, along_x, near_x, cross, near_cross],
        [here + (mine_col ^ s) for s in range(4)] + [there + (mine_col ^ s) for s in range(4)],
    )


def scatter_tokens(blocks, axes):
    if axes != ("dp", "col") or lax.axis_size("dp") != 2 or lax.axis_size("col") != 4:
        return lax.psum_scatter(blocks, axes, scatter_dimension=0, tiled=False).astype(jnp.float32)
    mine_dp, mine_col = lax.axis_index("dp"), lax.axis_index("col")
    half = blocks.shape[1] // 2

    def pick(flip_dp, flip_col):
        index = (mine_dp ^ flip_dp) * 4 + (mine_col ^ flip_col)
        return lax.dynamic_index_in_dim(blocks, index, 0, keepdims=False)

    def wide(value):
        return value.astype(jnp.float32)

    def low(value):
        return value.astype(jnp.bfloat16)

    spots = [(0, 0), (0, 2), (1, 0), (1, 2)]
    away = jnp.stack([pick(d, c ^ 1) for d, c in spots])
    came = swap(away, "col", 1)
    own, over_y, over_x, over_xy = [wide(pick(d, c)) + wide(came[i]) for i, (d, c) in enumerate(spots)]
    low_part = swap(low(jnp.stack([over_x[:half], over_xy[:half]])), "dp", 1)
    high_part = swap(low(jnp.stack([over_y[half:], over_xy[half:]])), "col", 2)
    last_low = swap(low(over_y[:half] + wide(low_part[1])), "col", 2)
    last_high = swap(low(over_x[half:] + wide(high_part[1])), "dp", 1)
    return jnp.concatenate(
        [
            own[:half] + wide(low_part[0]) + wide(last_low),
            own[half:] + wide(high_part[0]) + wide(last_high),
        ],
        axis=0,
    )


def swap_halves(value):
    lane = lax.broadcasted_iota(jnp.int32, value.shape, 1)
    first = (lane % HEAD_SIZE) < HEAD_SIZE // 2
    half = HEAD_SIZE // 2
    return jnp.where(first, pltpu.roll(value, LANES - half, 1), pltpu.roll(value, half, 1))


def turn(value, cos_part, sin_part):
    return value * cos_part + swap_halves(value) * sin_part


def spread_heads(pairs):
    lane = lax.broadcasted_iota(jnp.int32, pairs[0].shape, 1)
    low_lane = lane < HEAD_SIZE
    return [
        jnp.where(low_lane, pairs[0], 0.0),
        jnp.where(low_lane, pltpu.roll(pairs[0], HEAD_SIZE, 1), 0.0),
        jnp.where(low_lane, 0.0, pltpu.roll(pairs[1], HEAD_SIZE, 1)),
        jnp.where(low_lane, 0.0, pairs[1]),
    ]


def join_heads(heads):
    lane = lax.broadcasted_iota(jnp.int32, heads[0].shape, 1)
    low_lane = lane < HEAD_SIZE
    return [
        jnp.where(low_lane, heads[0], pltpu.roll(heads[1], HEAD_SIZE, 1)),
        jnp.where(low_lane, pltpu.roll(heads[2], HEAD_SIZE, 1), heads[3]),
    ]


def project_kernel(x_ref, gain_ref, w_ref, cos_ref, sin_ref, xn_ref, q_ref, kv_ref):
    x = x_ref[...].astype(jnp.float32)
    rinv = lax.rsqrt(jnp.mean(x * x, axis=1, keepdims=True) + EPSILON)
    xn = (x * rinv * gain_ref[...]).astype(jnp.bfloat16)
    xn_ref[...] = xn
    joined = nn_dot(xn, w_ref[...])
    cos_part, sin_part = cos_ref[...], sin_ref[...]
    scale = 1.0 / math.sqrt(HEAD_SIZE)
    pairs = [
        turn(joined[:, i * LANES : (i + 1) * LANES], cos_part, sin_part) * scale for i in range(2)
    ]
    for h, head in enumerate(spread_heads(pairs)):
        q_ref[h] = head.astype(jnp.bfloat16)
    kv_ref[:, :LANES] = turn(joined[:, 2 * LANES : 3 * LANES], cos_part, sin_part).astype(
        jnp.bfloat16
    )
    kv_ref[:, LANES:] = joined[:, 3 * LANES :].astype(jnp.bfloat16)


def project(x_plane, gain, w_joined, cos_table, sin_table, block):
    rows, width = x_plane.shape
    cols = w_joined.shape[1]
    return pl.pallas_call(
        project_kernel,
        grid=(rows // block,),
        in_specs=[
            pl.BlockSpec((block, width), lambda i: (i, 0)),
            pl.BlockSpec((1, width), lambda i: (0, 0)),
            pl.BlockSpec((width, cols), lambda i: (0, 0)),
            pl.BlockSpec((block, LANES), lambda i: (i, 0)),
            pl.BlockSpec((block, LANES), lambda i: (i, 0)),
        ],
        out_specs=[
            pl.BlockSpec((block, width), lambda i: (i, 0)),
            pl.BlockSpec((4, block, LANES), lambda i: (0, i, 0)),
            pl.BlockSpec((block, 2 * LANES), lambda i: (i, 0)),
        ],
        out_shape=[
            jax.ShapeDtypeStruct((rows, width), jnp.bfloat16),
            jax.ShapeDtypeStruct((4, rows, LANES), jnp.bfloat16),
            jax.ShapeDtypeStruct((rows, 2 * LANES), jnp.bfloat16),
        ],
        compiler_params=pltpu.CompilerParams(vmem_limit_bytes=32 * MIB),
        name="project",
    )(x_plane, gain, w_joined, cos_table, sin_table)


def project_back_kernel(dq_ref, own_ref, came_ref, cos_ref, sin_ref, w_ref, dqkv_ref, dx_ref):
    total = own_ref[...] + came_ref[...].astype(jnp.float32)
    dk = turn(total[:, :LANES], cos_ref[...], -sin_ref[...])
    dqkv_ref[:, : 2 * LANES] = dq_ref[...]
    dqkv_ref[:, 2 * LANES : 3 * LANES] = dk.astype(jnp.bfloat16)
    dqkv_ref[:, 3 * LANES :] = total[:, LANES:].astype(jnp.bfloat16)
    dx_ref[...] = nt_dot(dqkv_ref[...], w_ref[...]).astype(jnp.bfloat16)


def project_back(dq, own, came, cos_table, sin_table, w_joined, block):
    rows = dq.shape[0]
    width, cols = w_joined.shape
    return pl.pallas_call(
        project_back_kernel,
        grid=(rows // block,),
        in_specs=[
            pl.BlockSpec((block, 2 * LANES), lambda i: (i, 0)),
            pl.BlockSpec((block, 2 * LANES), lambda i: (i, 0)),
            pl.BlockSpec((block, 2 * LANES), lambda i: (i, 0)),
            pl.BlockSpec((block, LANES), lambda i: (i, 0)),
            pl.BlockSpec((block, LANES), lambda i: (i, 0)),
            pl.BlockSpec((width, cols), lambda i: (0, 0)),
        ],
        out_specs=[
            pl.BlockSpec((block, cols), lambda i: (i, 0)),
            pl.BlockSpec((block, width), lambda i: (i, 0)),
        ],
        out_shape=[
            jax.ShapeDtypeStruct((rows, cols), jnp.bfloat16),
            jax.ShapeDtypeStruct((rows, width), jnp.bfloat16),
        ],
        compiler_params=pltpu.CompilerParams(vmem_limit_bytes=32 * MIB),
        name="project_back",
    )(dq, own, came, cos_table, sin_table, w_joined)


def window_bias(start, first_key, window, block, plane):
    key_at = first_key + lax.broadcasted_iota(jnp.int32, (window, block), 0)
    query_at = first_key + plane + lax.broadcasted_iota(jnp.int32, (window, block), 1)
    allowed = (key_at >= start) & (key_at <= query_at)
    return jnp.where(allowed, 0.0, MASKED_SCORE)


def attend_kernel(q_ref, kv_ref, start_ref, o_ref, lse_ref, *, plane, block):
    window = plane + block
    first_key = pl.multiple_of(pl.program_id(0) * block, block)
    keys = kv_ref[pl.ds(first_key, window), :LANES]
    values = kv_ref[pl.ds(first_key, window), LANES:]
    values_t = values.astype(jnp.float32).T.astype(jnp.bfloat16)
    bias = window_bias(start_ref[...], first_key, window, block, plane)
    heads = []
    for h in range(4):
        scores = nt_dot(keys, q_ref[h]) + bias
        top = jnp.max(scores, axis=0, keepdims=True)
        weights = jnp.exp(scores - top)
        total = jnp.sum(weights, axis=0, keepdims=True)
        mixed = nn_dot(values_t, weights.astype(jnp.bfloat16)) / total
        lse_ref[h : h + 1, :] = top + jnp.log(total)
        heads.append(mixed.T)
    pairs = join_heads(heads)
    o_ref[:, :LANES] = pairs[0].astype(jnp.bfloat16)
    o_ref[:, LANES:] = pairs[1].astype(jnp.bfloat16)


def attend(q4, kv, start, block):
    plane = q4.shape[1]
    return pl.pallas_call(
        functools.partial(attend_kernel, plane=plane, block=block),
        grid=(plane // block,),
        in_specs=[
            pl.BlockSpec((4, block, LANES), lambda i: (0, i, 0)),
            pl.BlockSpec((2 * plane, 2 * LANES), lambda i: (0, 0)),
            pl.BlockSpec((1, block), lambda i: (0, i)),
        ],
        out_specs=[
            pl.BlockSpec((block, 2 * LANES), lambda i: (i, 0)),
            pl.BlockSpec((4, block), lambda i: (0, i)),
        ],
        out_shape=[
            jax.ShapeDtypeStruct((plane, 2 * LANES), jnp.bfloat16),
            jax.ShapeDtypeStruct((4, plane), jnp.float32),
        ],
        compiler_params=pltpu.CompilerParams(vmem_limit_bytes=48 * MIB),
        name="attend",
    )(q4, kv, start)


def attend_back_kernel(
    q_ref, kv_ref, start_ref, lse_ref, do_ref, cos_ref, sin_ref, dq_ref, dkv_ref, *, plane, block
):
    window = plane + block

    @pl.when(pl.program_id(0) == 0)
    def _():
        dkv_ref[...] = jnp.zeros_like(dkv_ref)

    first_key = pl.multiple_of(pl.program_id(0) * block, block)
    keys = kv_ref[pl.ds(first_key, window), :LANES]
    values = kv_ref[pl.ds(first_key, window), LANES:]
    keys_t = keys.astype(jnp.float32).T.astype(jnp.bfloat16)
    bias = window_bias(start_ref[...], first_key, window, block, plane)
    grad = do_ref[...].astype(jnp.float32)
    grads = [g.astype(jnp.bfloat16) for g in spread_heads([grad[:, :LANES], grad[:, LANES:]])]
    heads = []
    dk_total, dv_total = None, None
    for h in range(4):
        q = q_ref[h]
        weights = jnp.exp(nt_dot(keys, q) + bias - lse_ref[h : h + 1, :])
        dv = nn_dot(weights.astype(jnp.bfloat16), grads[h])
        product = weights * nt_dot(values, grads[h])
        centre = jnp.sum(product, axis=0, keepdims=True)
        ds = (product - weights * centre).astype(jnp.bfloat16)
        dk = nn_dot(ds, q)
        heads.append(nn_dot(keys_t, ds).T)
        dk_total = dk if dk_total is None else dk_total + dk
        dv_total = dv if dv_total is None else dv_total + dv
    dkv_ref[pl.ds(first_key, window), :LANES] += dk_total
    dkv_ref[pl.ds(first_key, window), LANES:] += dv_total
    scale = 1.0 / math.sqrt(HEAD_SIZE)
    for i, pair in enumerate(join_heads(heads)):
        dq_ref[:, i * LANES : (i + 1) * LANES] = turn(
            pair * scale, cos_ref[...], -sin_ref[...]
        ).astype(jnp.bfloat16)


def attend_back(q4, kv, start, lse, do, cos_table, sin_table, block):
    plane = q4.shape[1]
    return pl.pallas_call(
        functools.partial(attend_back_kernel, plane=plane, block=block),
        grid=(plane // block,),
        in_specs=[
            pl.BlockSpec((4, block, LANES), lambda i: (0, i, 0)),
            pl.BlockSpec((2 * plane, 2 * LANES), lambda i: (0, 0)),
            pl.BlockSpec((1, block), lambda i: (0, i)),
            pl.BlockSpec((4, block), lambda i: (0, i)),
            pl.BlockSpec((block, 2 * LANES), lambda i: (i, 0)),
            pl.BlockSpec((block, LANES), lambda i: (i, 0)),
            pl.BlockSpec((block, LANES), lambda i: (i, 0)),
        ],
        out_specs=[
            pl.BlockSpec((block, 2 * LANES), lambda i: (i, 0)),
            pl.BlockSpec((2 * plane, 2 * LANES), lambda i: (0, 0)),
        ],
        out_shape=[
            jax.ShapeDtypeStruct((plane, 2 * LANES), jnp.bfloat16),
            jax.ShapeDtypeStruct((2 * plane, 2 * LANES), jnp.float32),
        ],
        compiler_params=pltpu.CompilerParams(vmem_limit_bytes=48 * MIB),
        name="attend_back",
    )(q4, kv, start, lse, do, cos_table, sin_table)


def expert_kernel(
    hn_ref,
    go_ref,
    pos_ref,
    gate_ref,
    wg_ref,
    wu_ref,
    wd_ref,
    y_ref,
    dx_ref,
    dgate_ref,
    grad_ref,
    x_all,
    go_all,
    slot_gate,
    sums,
    *,
    sources,
    tok,
    chunks,
):
    chunk = pl.program_id(1)
    for s in range(sources):
        spot = lax.broadcasted_iota(jnp.int32, (CAP, tok), 0)
        hot = spot == pos_ref[0, :, s * tok : (s + 1) * tok]
        hot_low = hot.astype(jnp.bfloat16)
        rows = slice(s * CAP, (s + 1) * CAP)
        x_all[rows, :] = nn_dot(hot_low, hn_ref[s]).astype(jnp.bfloat16)
        go_all[rows, :] = nn_dot(hot_low, go_ref[s]).astype(jnp.bfloat16)
        slot_gate[rows, :] = jnp.sum(
            jnp.where(hot, gate_ref[0, :, s * tok : (s + 1) * tok], 0.0), axis=1, keepdims=True
        )
    x = x_all[...]
    go = go_all[...]
    gate = slot_gate[...]
    a = nn_dot(x, wg_ref[0])
    b = nn_dot(x, wu_ref[0])
    dz = nt_dot(go, wd_ref[0])
    sig = 1.0 / (1.0 + jnp.exp(-a))
    silu = a * sig
    z = silu * b
    z_low = z.astype(jnp.bfloat16)
    dgate = jnp.sum(z_low.astype(jnp.float32) * dz, axis=1, keepdims=True)
    dz = dz * gate
    da = (dz * b * sig * (1.0 + a * (1.0 - sig))).astype(jnp.bfloat16)
    db = (dz * silu).astype(jnp.bfloat16)
    y = (nn_dot(z_low, wd_ref[0]) * gate).astype(jnp.bfloat16)
    dx = (nt_dot(da, wg_ref[0]) + nt_dot(db, wu_ref[0])).astype(jnp.bfloat16)
    for s in range(sources):
        rows = slice(s * CAP, (s + 1) * CAP)
        y_ref[s, 0] = y[rows]
        dx_ref[s, 0] = dx[rows]
        spot = lax.broadcasted_iota(jnp.int32, (CAP, tok), 0)
        hot = spot == pos_ref[0, :, s * tok : (s + 1) * tok]
        dgate_ref[0, :, s * tok : (s + 1) * tok] = jnp.sum(
            jnp.where(hot, dgate[rows], 0.0), axis=0, keepdims=True
        )
    gz = (z * gate).astype(jnp.bfloat16)
    out_shape = grad_ref.shape[:2] + grad_ref.shape[4:]
    for i, term in enumerate([tn_dot(x, da), tn_dot(x, db), tn_dot(go, gz)]):
        if chunks == 1:
            grad_ref[:, :, 0, i] = term.astype(jnp.bfloat16).reshape(out_shape)
        else:

            @pl.when(chunk == 0)
            def _(i=i, term=term):
                sums[i] = term

            @pl.when(chunk > 0)
            def _(i=i, term=term):
                sums[i] += term

            @pl.when(chunk == chunks - 1)
            def _(i=i):
                grad_ref[:, :, 0, i] = sums[i].astype(jnp.bfloat16).reshape(out_shape)


def experts(hn_all, go_all, pos, gate, w_gate, w_up, w_down, first, row_count, col_count):
    total, tok, width = hn_all.shape
    count = pos.shape[0]
    hidden = w_gate.shape[2]
    sources = 8 if total % 8 == 0 else total
    chunks = total // sources
    part = width // (row_count * col_count)
    slots = sources * CAP

    def weight(shape):
        return pl.BlockSpec((1,) + shape, lambda e, c, f: (f[0] + e, 0, 0))

    return pl.pallas_call(
        lambda f, *refs: expert_kernel(*refs, sources=sources, tok=tok, chunks=chunks),
        grid_spec=pltpu.PrefetchScalarGridSpec(
            num_scalar_prefetch=1,
            grid=(count, chunks),
            in_specs=[
                pl.BlockSpec((sources, tok, width), lambda e, c, f: (c, 0, 0)),
                pl.BlockSpec((sources, tok, width), lambda e, c, f: (c, 0, 0)),
                pl.BlockSpec((1, 1, sources * tok), lambda e, c, f: (e, 0, c)),
                pl.BlockSpec((1, 1, sources * tok), lambda e, c, f: (e, 0, c)),
                weight((width, hidden)),
                weight((width, hidden)),
                weight((hidden, width)),
            ],
            out_specs=[
                pl.BlockSpec((sources, 1, CAP, width), lambda e, c, f: (c, e, 0, 0)),
                pl.BlockSpec((sources, 1, CAP, width), lambda e, c, f: (c, e, 0, 0)),
                pl.BlockSpec((1, 1, sources * tok), lambda e, c, f: (e, 0, c)),
                pl.BlockSpec(
                    (row_count, col_count, 1, 3, part, hidden),
                    lambda e, c, f: (0, 0, e, 0, 0, 0),
                ),
            ],
            scratch_shapes=[
                pltpu.VMEM((slots, width), jnp.bfloat16),
                pltpu.VMEM((slots, width), jnp.bfloat16),
                pltpu.VMEM((slots, 1), jnp.float32),
                pltpu.VMEM((3, width, hidden) if chunks > 1 else (1, 8, LANES), jnp.float32),
            ],
        ),
        out_shape=[
            jax.ShapeDtypeStruct((total, count, CAP, width), jnp.bfloat16),
            jax.ShapeDtypeStruct((total, count, CAP, width), jnp.bfloat16),
            jax.ShapeDtypeStruct((count, 1, total * tok), jnp.float32),
            jax.ShapeDtypeStruct(
                (row_count, col_count, count, 3, part, hidden), jnp.bfloat16
            ),
        ],
        compiler_params=pltpu.CompilerParams(vmem_limit_bytes=60 * MIB),
        name="experts",
    )(first, hn_all, go_all, pos, gate, w_gate, w_up, w_down)


def combine_kernel(pos_ref, y_ref, dx_ref, out_ref, dhn_ref, *, count, tok):
    spot = lax.broadcasted_iota(jnp.int32, (CAP, tok), 0)
    hots = [
        (spot == pos_ref[e]).astype(jnp.float32).astype(jnp.bfloat16) for e in range(count)
    ]
    hot = jnp.concatenate(hots, axis=0)
    width = out_ref.shape[2]
    out_ref[0] = tn_dot(hot, y_ref[0].reshape(count * CAP, width)).astype(jnp.bfloat16)
    dhn_ref[0] = tn_dot(hot, dx_ref[0].reshape(count * CAP, width)).astype(jnp.bfloat16)


def combine(pos, y, dx, tok):
    total, count, _, width = y.shape
    return pl.pallas_call(
        functools.partial(combine_kernel, count=count, tok=tok),
        grid=(total,),
        in_specs=[
            pl.BlockSpec((count, 1, tok), lambda s: (0, 0, s)),
            pl.BlockSpec((1, count, CAP, width), lambda s: (s, 0, 0, 0)),
            pl.BlockSpec((1, count, CAP, width), lambda s: (s, 0, 0, 0)),
        ],
        out_specs=[
            pl.BlockSpec((1, tok, width), lambda s: (s, 0, 0)),
            pl.BlockSpec((1, tok, width), lambda s: (s, 0, 0)),
        ],
        out_shape=[
            jax.ShapeDtypeStruct((total, tok, width), jnp.bfloat16),
            jax.ShapeDtypeStruct((total, tok, width), jnp.bfloat16),
        ],
        compiler_params=pltpu.CompilerParams(vmem_limit_bytes=32 * MIB),
        name="combine",
    )(pos, y, dx)


def places(seq_lengths, first_row, total_rows):
    seq_ends = jnp.cumsum(seq_lengths)
    spots = first_row + jnp.arange(total_rows, dtype=jnp.int32)
    passed = (spots[:, None] >= seq_ends[None, :]).astype(jnp.int32)
    starts = jnp.sum(passed * seq_lengths[None, :], axis=1)
    return spots, starts


def route_mask(routes_t):
    ids = lax.broadcasted_iota(jnp.int32, (EXPERTS, 1, 1), 0)
    return jnp.any(routes_t[None, :, :] == ids, axis=1)


def dense_gates(logits_t, mask):
    shown = jnp.where(mask, logits_t, MASKED_SCORE)
    top = jnp.max(shown, axis=0, keepdims=True)
    raised = jnp.where(mask, jnp.exp(shown - top), 0.0)
    return raised / jnp.sum(raised, axis=0, keepdims=True)


def on_device(
    inputs,
    lengths,
    routes,
    norm1_gain,
    w_query,
    key_weight,
    value_weight,
    w_output,
    norm2_gain,
    router,
    w_gate,
    w_up,
    w_down,
    d_output,
):
    row_count = lax.axis_size("row")
    col_count = lax.axis_size("col")
    dp_count = lax.axis_size("dp")
    my_row, my_col = lax.axis_index("row"), lax.axis_index("col")
    tok, width = inputs.shape
    plane = tok * col_count
    block = tok
    query_cols, key_cols = w_query.shape[1], key_weight.shape[1]
    assert plane >= MAX_LEN - 1 and query_cols == 2 * LANES and key_cols == LANES
    local_experts = w_gate.shape[0]
    split = local_experts % col_count == 0
    axes = ("dp", "col") if split else ("dp",)
    mine_experts = local_experts // col_count if split else local_experts
    first_local = my_col * mine_experts if split else jnp.int32(0)
    sources = dp_count * (col_count if split else 1)

    x_plane = gather_col(inputs).reshape(plane, width)
    w_mine = jnp.concatenate([w_query, key_weight, value_weight], axis=1)
    w_joined = gather_row(w_mine).reshape(width, 2 * query_cols)
    routes_all = gather_tokens(routes.reshape(-1, LANES), axes).reshape(sources * tok, TOPK)
    go_all = gather_tokens(d_output, axes)

    spots, starts = places(lengths[0], my_row * plane, plane)
    frequency = jnp.exp(
        -math.log(ROPE_BASE) * jnp.arange(HEAD_SIZE // 2, dtype=jnp.float32) / (HEAD_SIZE // 2)
    )
    angles = (spots - starts).astype(jnp.float32)[:, None] * frequency[None, :]
    cos_table = jnp.tile(jnp.cos(angles), (1, 4))
    sin_table = jnp.sin(angles)
    sin_table = jnp.tile(jnp.concatenate([-sin_table, sin_table], axis=1), (1, 2))
    start = (starts - (my_row - 1) * plane)[None, :]
    mask_all = route_mask(routes_all.T)
    first_expert = lax.axis_index("dp") * local_experts + first_local
    mask_mine = lax.dynamic_slice_in_dim(mask_all, first_expert, mine_experts, 0)
    before = jnp.triu(jnp.ones((tok, tok), jnp.bfloat16), 1)
    rank = jnp.dot(
        mask_mine.reshape(mine_experts * sources, tok).astype(jnp.bfloat16),
        before,
        preferred_element_type=jnp.float32,
    ).astype(jnp.int32)
    pos = jnp.where(mask_mine, rank.reshape(mine_experts, sources * tok), -1)
    pos = pos.reshape(mine_experts, 1, sources * tok)
    mask_own = route_mask(routes.T)

    xn1, q4, kv = project(
        x_plane, norm1_gain[None, :], w_joined, cos_table, sin_table, block
    )
    kv_before = lax.ppermute(kv, "row", [(i, i + 1) for i in range(row_count - 1)])
    kv_all = jnp.concatenate([kv_before, kv], axis=0)
    heads, lse = attend(q4, kv_all, start, block)
    wo_rows = jnp.swapaxes(gather_row(w_output), 0, 1).reshape(query_cols, width)
    wo_full = gather_col(wo_rows).reshape(col_count * query_cols, width)
    heads_tok = jnp.swapaxes(exchange_col(heads.reshape(col_count, tok, query_cols)), 0, 1)
    heads_tok = heads_tok.reshape(tok, col_count * query_cols)
    inputs_f = inputs.astype(jnp.float32)
    rinv_one = lax.rsqrt(jnp.mean(inputs_f * inputs_f, axis=1, keepdims=True) + EPSILON)
    hidden = inputs_f + jnp.dot(heads_tok, wo_full, preferred_element_type=jnp.float32)
    rinv_two = lax.rsqrt(jnp.mean(hidden * hidden, axis=1, keepdims=True) + EPSILON)
    hn = (hidden * rinv_two * norm2_gain).astype(jnp.bfloat16)

    hn_all = gather_tokens(hn, axes)
    logits_t = lax.dot_general(
        router,
        hn_all.reshape(sources * tok, width),
        (((0,), (1,)), ((), ())),
        preferred_element_type=jnp.float32,
    )
    gate_all = dense_gates(logits_t, mask_all)
    gate_mine = lax.dynamic_slice_in_dim(gate_all, first_expert, mine_experts, 0)
    y, dx, dgate, expert_grads = experts(
        hn_all,
        go_all,
        pos,
        gate_mine.reshape(mine_experts, 1, sources * tok),
        w_gate,
        w_up,
        w_down,
        first_local.reshape(1),
        row_count,
        col_count,
    )
    out_terms, dhn_terms = combine(pos, y, dx, tok)
    dgate_blocks = jnp.zeros((EXPERTS, sources * tok), jnp.float32)
    dgate_blocks = lax.dynamic_update_slice_in_dim(
        dgate_blocks, dgate.reshape(mine_experts, sources * tok), first_expert, 0
    )
    dgate_blocks = jnp.swapaxes(dgate_blocks.reshape(EXPERTS, sources, tok), 0, 1)
    dgate_blocks = dgate_blocks.reshape(sources, EXPERTS * tok // width, width)
    dgate_high = dgate_blocks.astype(jnp.bfloat16)
    dgate_low = (dgate_blocks - dgate_high.astype(jnp.float32)).astype(jnp.bfloat16)
    dhn_sum = scatter_tokens(
        jnp.concatenate([dgate_high, dhn_terms, dgate_low], axis=1), axes
    )
    extra = EXPERTS * tok // width
    dgate_own = (dhn_sum[:extra] + dhn_sum[extra + tok :]).reshape(EXPERTS, tok)
    dhn = dhn_sum[extra : extra + tok]

    logits_own = lax.dot_general(
        router, hn, (((0,), (1,)), ((), ())), preferred_element_type=jnp.float32
    )
    gate_own = dense_gates(logits_own, mask_own)
    dlogits = gate_own * (dgate_own - jnp.sum(gate_own * dgate_own, axis=0, keepdims=True))
    dlogits = dlogits.astype(jnp.bfloat16)
    dhn = dhn + lax.dot_general(
        dlogits, router, (((0,), (1,)), ((), ())), preferred_element_type=jnp.float32
    )
    d_router_part = lax.dot_general(
        hn, dlogits, (((0,), (1,)), ((), ())), preferred_element_type=jnp.float32
    )
    grad_out = d_output.astype(jnp.float32)
    scaled_two = norm2_gain * dhn
    gain_two_part = jnp.sum(dhn * hidden * rinv_two, axis=0)
    dh = (
        grad_out
        + rinv_two * scaled_two
        - hidden * rinv_two**3 * jnp.mean(scaled_two * hidden, axis=1, keepdims=True)
    )
    dattn = dh.astype(jnp.bfloat16)

    do_tok = nt_dot(dattn, wo_full).astype(jnp.bfloat16)
    do_blocks = jnp.swapaxes(do_tok.reshape(tok, col_count, query_cols), 0, 1)
    do = exchange_col(do_blocks).reshape(plane, query_cols)
    dq, dkv = attend_back(q4, kv_all, start, lse, do, cos_table, sin_table, block)
    dkv_after = lax.ppermute(
        dkv[:plane].astype(jnp.bfloat16), "row", [(i + 1, i) for i in range(row_count - 1)]
    )
    dqkv, dxn1_part = project_back(dq, dkv[plane:], dkv_after, cos_table, sin_table, w_joined, block)
    dxn1 = scatter_col(dxn1_part.reshape(col_count, tok, width))
    scaled_one = norm1_gain * dxn1
    gain_one_part = jnp.sum(dxn1 * inputs_f * rinv_one, axis=0)
    d_inputs = (
        dh
        + rinv_one * scaled_one
        - inputs_f * rinv_one**3 * jnp.mean(scaled_one * inputs_f, axis=1, keepdims=True)
    )

    dattn_plane = gather_col(dattn).reshape(plane, width)
    wo_part = tn_dot(heads, dattn_plane).astype(jnp.bfloat16)
    wo_part = jnp.swapaxes(wo_part.reshape(query_cols, row_count, -1), 0, 1)
    d_w_output = scatter_row(wo_part).astype(jnp.bfloat16)
    d_w_output = sum_over_low(d_w_output, "dp")
    qkv_part = tn_dot(xn1, dqkv).astype(jnp.bfloat16).reshape(row_count, -1, 2 * query_cols)
    d_w_qkv = sum_over_low(scatter_row(qkv_part).astype(jnp.bfloat16), "dp")

    output = (hidden + scatter_tokens(out_terms, axes)).astype(jnp.bfloat16)
    if split:
        sums = lax.psum_scatter(expert_grads, "row", scatter_dimension=0, tiled=False)
        sums = exchange_col(sums)
    else:
        sums = lax.psum_scatter(
            expert_grads.reshape((row_count * col_count,) + expert_grads.shape[2:]),
            ("row", "col"),
            scatter_dimension=0,
            tiled=False,
        )
    sums = sums.reshape((local_experts, 3) + sums.shape[-2:])
    d_w_gate = sums[:, 0].astype(jnp.float32)
    d_w_up = sums[:, 1].astype(jnp.float32)
    d_w_down = jnp.swapaxes(sums[:, 2], 1, 2).astype(jnp.float32)

    small = jnp.concatenate([d_router_part.reshape(-1, width), gain_two_part[None, :]], axis=0)
    gain_one = gain_one_part.reshape(-1, LANES)
    for axis in ("col", "dp", "row"):
        small = sum_over(small, axis)
        gain_one = sum_over(gain_one, axis)
    d_router = small[:-1].reshape(width, EXPERTS)
    return (
        output,
        d_inputs,
        gain_one.reshape(-1),
        d_w_qkv[:, :query_cols],
        d_w_qkv[:, query_cols : query_cols + key_cols],
        d_w_qkv[:, query_cols + key_cols :],
        d_w_output,
        small[-1],
        d_router,
        d_w_gate,
        d_w_up,
        d_w_down,
    )


def sum_over_low(value, axis):
    size = lax.axis_size(axis)
    if size == 2:
        return value.astype(jnp.float32) + swap(value, axis, 1).astype(jnp.float32)
    return lax.psum(value, axis).astype(jnp.float32)


def solution(mesh):
    return jax.shard_map(
        on_device,
        mesh=mesh,
        in_specs=(
            P(("dp", "row", "col"), None),
            P("dp", None),
            P(("dp", "row", "col"), None),
            P(),
            P("row", "col"),
            P("row", "col"),
            P("row", "col"),
            P("col", "row"),
            P(),
            P(),
            P("dp", None, None),
            P("dp", None, None),
            P("dp", None, None),
            P(("dp", "row", "col"), None),
        ),
        out_specs=(
            P(("dp", "row", "col"), None),
            P(("dp", "row", "col"), None),
            P(),
            P("row", "col"),
            P("row", "col"),
            P("row", "col"),
            P("col", "row"),
            P(),
            P(),
            P("dp", ("row", "col"), None),
            P("dp", ("row", "col"), None),
            P("dp", None, ("row", "col")),
        ),
        check_vma=False,
    )
```

```python
import functools
import math

import jax
import jax.numpy as jnp
from jax import lax
from jax.experimental import pallas as pl
from jax.experimental.pallas import tpu as pltpu
from jax.sharding import PartitionSpec as P

HEAD_SIZE = 64
EXPERTS = 32
TOPK = 8
MAX_LEN = 1024
CAP = 96

EPSILON = 1e-06
MASKED_SCORE = -1e30
ROPE_BASE = 10000.0
LANES = 128
MIB = 1024 * 1024


def nt_dot(left, right):
    return lax.dot_general(
        left, right, (((1,), (1,)), ((), ())), preferred_element_type=jnp.float32
    )


def tn_dot(left, right):
    return lax.dot_general(
        left, right, (((0,), (0,)), ((), ())), preferred_element_type=jnp.float32
    )


def nn_dot(left, right):
    return jnp.dot(left, right, preferred_element_type=jnp.float32)


def swap(value, axis, step):
    return lax.ppermute(value, axis, [(i, i ^ step) for i in range(lax.axis_size(axis))])


def after(value, *others):
    return lax.optimization_barrier((value,) + others)[0]


def gather_col(value):
    far = swap(value, "col", 2)
    near = swap(value, "col", 1)
    return [value, near, far, swap(far, "col", 1)]


def exchange_col(blocks):
    return [blocks[0]] + [swap(blocks[s], "col", s) for s in (1, 2, 3)]


def shift_row(value, step):
    size = lax.axis_size("row")
    return lax.ppermute(value, "row", [(i, (i + step) % size) for i in range(size)])


def gather_row(value):
    return [value] + [shift_row(value, s) for s in range(1, lax.axis_size("row"))]


def scatter_row(blocks):
    total = blocks[0].astype(jnp.float32)
    for step in range(1, len(blocks)):
        total = total + shift_row(blocks[step], step).astype(jnp.float32)
    return total


def sum_over(value, axis):
    size = lax.axis_size(axis)
    if size & (size - 1):
        return lax.psum(value, axis)
    step = 1
    while step < size:
        value = value + swap(value, axis, step)
        step *= 2
    return value


def sum_over_low(value, axis):
    if lax.axis_size(axis) == 2:
        return value.astype(jnp.float32) + swap(value, axis, 1).astype(jnp.float32)
    return lax.psum(value, axis).astype(jnp.float32)


def two_way(axes):
    return axes == ("dp", "col") and lax.axis_size("dp") == 2


def gather_tokens(value, axes):
    if not two_way(axes):
        every = lax.all_gather(value, axes)
        return [every[s] for s in range(every.shape[0])]
    half = value.shape[0] // 2
    along_x = swap(value, "dp", 1)
    along_y = swap(value, "col", 2)
    near = swap(value, "col", 1)
    cross_low = swap(along_x[:half], "col", 2)
    cross_high = swap(along_y[half:], "dp", 1)
    near_x = swap(along_x, "col", 1)
    near_y = swap(along_y, "col", 1)
    cross = jnp.concatenate([cross_low, cross_high], axis=0)
    near_cross = swap(cross, "col", 1)
    return [value, along_y, along_x, cross, near, near_y, near_x, near_cross]


def add_first_kernel(keep_ref, came_ref, x_ref, y_ref, *, low):
    def total(spot, rows):
        return (
            keep_ref[spot, rows].astype(jnp.float32) + came_ref[spot, rows].astype(jnp.float32)
        ).astype(jnp.bfloat16)

    x_ref[0], x_ref[1] = total(2, slice(0, low)), total(3, slice(0, low))
    y_ref[0], y_ref[1] = total(1, slice(low, None)), total(3, slice(low, None))


def add_second_kernel(keep_ref, came_ref, x_ref, y_ref, low_ref, high_ref, *, low):
    def total(spot, rows, extra):
        return (
            keep_ref[spot, rows].astype(jnp.float32)
            + came_ref[spot, rows].astype(jnp.float32)
            + extra.astype(jnp.float32)
        ).astype(jnp.bfloat16)

    low_ref[...] = total(1, slice(0, low), x_ref[1])
    high_ref[...] = total(2, slice(low, None), y_ref[1])


def scatter_tokens(keep, away, low):
    rows, width = keep.shape[1:]
    high = rows - low
    came = swap(away, "col", 1)
    params = pltpu.CompilerParams(vmem_limit_bytes=32 * MIB)
    send_x, send_y = pl.pallas_call(
        functools.partial(add_first_kernel, low=low),
        out_shape=[
            jax.ShapeDtypeStruct((2, low, width), jnp.bfloat16),
            jax.ShapeDtypeStruct((2, high, width), jnp.bfloat16),
        ],
        compiler_params=params,
        name="add_first",
    )(keep, came)
    by_x, by_y = swap(send_x, "dp", 1), swap(send_y, "col", 2)
    last_low, last_high = pl.pallas_call(
        functools.partial(add_second_kernel, low=low),
        out_shape=[
            jax.ShapeDtypeStruct((low, width), jnp.bfloat16),
            jax.ShapeDtypeStruct((high, width), jnp.bfloat16),
        ],
        compiler_params=params,
        name="add_second",
    )(keep, came, by_x, by_y)
    return [keep, came, by_x, by_y, swap(last_low, "col", 2), swap(last_high, "dp", 1)]


def whole_sum(parts, low):
    keep, came, by_x, by_y, last_low, last_high = [p[...].astype(jnp.float32) for p in parts]
    return jnp.concatenate(
        [
            keep[0, :low] + came[0, :low] + by_x[0] + last_low,
            keep[0, low:] + came[0, low:] + by_y[0] + last_high,
        ],
        axis=0,
    )


def swap_halves(value):
    lane = lax.broadcasted_iota(jnp.int32, value.shape, 1)
    first = (lane % HEAD_SIZE) < HEAD_SIZE // 2
    half = HEAD_SIZE // 2
    return jnp.where(first, pltpu.roll(value, LANES - half, 1), pltpu.roll(value, half, 1))


def turn(value, cos_part, sin_part):
    return value * cos_part + swap_halves(value) * sin_part


def spread_heads(pairs):
    lane = lax.broadcasted_iota(jnp.int32, pairs[0].shape, 1)
    low_lane = lane < HEAD_SIZE
    return [
        jnp.where(low_lane, pairs[0], 0.0),
        jnp.where(low_lane, pltpu.roll(pairs[0], HEAD_SIZE, 1), 0.0),
        jnp.where(low_lane, 0.0, pltpu.roll(pairs[1], HEAD_SIZE, 1)),
        jnp.where(low_lane, 0.0, pairs[1]),
    ]


def join_heads(heads):
    lane = lax.broadcasted_iota(jnp.int32, heads[0].shape, 1)
    low_lane = lane < HEAD_SIZE
    return [
        jnp.where(low_lane, heads[0], pltpu.roll(heads[1], HEAD_SIZE, 1)),
        jnp.where(low_lane, pltpu.roll(heads[2], HEAD_SIZE, 1), heads[3]),
    ]


SMEM_SPEC = pl.BlockSpec(memory_space=pltpu.SMEM)
VMEM_SPEC = pl.BlockSpec(memory_space=pltpu.VMEM)


def place_rows(index, block):
    return pl.ds(pl.multiple_of(index * block, block), block)


def project_kernel(*refs, rows, block):
    me_ref, gain_ref, cos_ref, sin_ref = refs[:4]
    x_refs, w_refs = refs[4:8], refs[8 : 8 + rows]
    xn_ref, q_ref, kv_ref, w_ref = refs[8 + rows :]
    my_col, my_row = me_ref[0], me_ref[1]
    part = w_refs[0].shape[0]
    for s in range(rows):
        w_ref[place_rows(lax.rem(my_row - s + rows, rows), part), :] = w_refs[s][...]
    w_joined = w_ref[...]
    scale = 1.0 / math.sqrt(HEAD_SIZE)
    for s in range(4):
        at = place_rows(my_col ^ s, block)
        x = x_refs[s][...].astype(jnp.float32)
        rinv = lax.rsqrt(jnp.mean(x * x, axis=1, keepdims=True) + EPSILON)
        xn = (x * rinv * gain_ref[...]).astype(jnp.bfloat16)
        xn_ref[at, :] = xn
        joined = nn_dot(xn, w_joined)
        cos_part, sin_part = cos_ref[at, :], sin_ref[at, :]
        pairs = [
            turn(joined[:, i * LANES : (i + 1) * LANES], cos_part, sin_part) * scale
            for i in range(2)
        ]
        for h, head in enumerate(spread_heads(pairs)):
            q_ref[h, at, :] = head.astype(jnp.bfloat16)
        kv_ref[at, :LANES] = turn(joined[:, 2 * LANES : 3 * LANES], cos_part, sin_part).astype(
            jnp.bfloat16
        )
        kv_ref[at, LANES:] = joined[:, 3 * LANES :].astype(jnp.bfloat16)


def project(me, gain, cos_table, sin_table, x_list, w_list):
    block, width = x_list[0].shape
    rows = len(w_list)
    plane = 4 * block
    return pl.pallas_call(
        functools.partial(project_kernel, rows=rows, block=block),
        in_specs=[SMEM_SPEC] + [VMEM_SPEC] * (7 + rows),
        out_specs=[VMEM_SPEC] * 4,
        out_shape=[
            jax.ShapeDtypeStruct((plane, width), jnp.bfloat16),
            jax.ShapeDtypeStruct((4, plane, LANES), jnp.bfloat16),
            jax.ShapeDtypeStruct((plane, 2 * LANES), jnp.bfloat16),
            jax.ShapeDtypeStruct((width, 4 * LANES), jnp.bfloat16),
        ],
        compiler_params=pltpu.CompilerParams(vmem_limit_bytes=40 * MIB),
        name="project",
    )(me, gain, cos_table, sin_table, *x_list, *w_list)


def project_back_kernel(
    me_ref, dq_ref, own_ref, came_ref, cos_ref, sin_ref, w_ref, dqkv_ref, keep_ref, away_ref, *, block
):
    my_col = me_ref[0]
    for s in (1, 3, 0, 2):
        at = place_rows(my_col ^ s, block)
        total = own_ref[at, :] + came_ref[at, :].astype(jnp.float32)
        dk = turn(total[:, :LANES], cos_ref[at, :], -sin_ref[at, :]).astype(jnp.bfloat16)
        dqkv = jnp.concatenate([dq_ref[at, :], dk, total[:, LANES:].astype(jnp.bfloat16)], axis=1)
        dqkv_ref[at, :] = dqkv
        target = away_ref if s % 2 else keep_ref
        target[s // 2] = nt_dot(dqkv, w_ref[...]).astype(jnp.bfloat16)


def project_back(me, dq, own, came, cos_table, sin_table, w_joined, block):
    width = w_joined.shape[0]
    return pl.pallas_call(
        functools.partial(project_back_kernel, block=block),
        in_specs=[SMEM_SPEC] + [VMEM_SPEC] * 6,
        out_specs=[VMEM_SPEC] * 3,
        out_shape=[
            jax.ShapeDtypeStruct((dq.shape[0], 4 * LANES), jnp.bfloat16),
            jax.ShapeDtypeStruct((2, block, width), jnp.bfloat16),
            jax.ShapeDtypeStruct((2, block, width), jnp.bfloat16),
        ],
        compiler_params=pltpu.CompilerParams(vmem_limit_bytes=40 * MIB),
        name="project_back",
    )(me, dq, own, came, cos_table, sin_table, w_joined)


def qkv_grad_kernel(me_ref, xn_ref, dqkv_ref, *refs, rows):
    scratch = refs[rows]
    scratch[...] = tn_dot(xn_ref[...], dqkv_ref[...])
    part = refs[0].shape[0]
    for s in range(rows):
        at = place_rows(lax.rem(me_ref[1] + s, rows), part)
        refs[s][...] = scratch[at, :].astype(jnp.bfloat16)


def qkv_grad(me, xn, dqkv, rows):
    width, cols = xn.shape[1], dqkv.shape[1]
    return pl.pallas_call(
        functools.partial(qkv_grad_kernel, rows=rows),
        in_specs=[SMEM_SPEC, VMEM_SPEC, VMEM_SPEC],
        out_specs=[VMEM_SPEC] * rows,
        out_shape=[jax.ShapeDtypeStruct((width // rows, cols), jnp.bfloat16)] * rows,
        scratch_shapes=[pltpu.VMEM((width, cols), jnp.float32)],
        compiler_params=pltpu.CompilerParams(vmem_limit_bytes=40 * MIB),
        name="qkv_grad",
    )(me, xn, dqkv)


def wo_grad_kernel(me_ref, *refs, rows):
    scratch = refs[8 + rows]
    total = None
    for s in range(4):
        term = tn_dot(refs[s][...], refs[4 + s][...])
        total = term if total is None else total + term
    scratch[...] = total
    part = refs[8].shape[1]
    for s in range(rows):
        at = place_rows(lax.rem(me_ref[1] + s, rows), part)
        refs[8 + s][...] = scratch[:, at].astype(jnp.bfloat16)


def wo_grad(me, heads, dattn, rows):
    cols, width = heads[0].shape[1], dattn[0].shape[1]
    return pl.pallas_call(
        functools.partial(wo_grad_kernel, rows=rows),
        in_specs=[SMEM_SPEC] + [VMEM_SPEC] * 8,
        out_specs=[VMEM_SPEC] * rows,
        out_shape=[jax.ShapeDtypeStruct((cols, width // rows), jnp.bfloat16)] * rows,
        scratch_shapes=[pltpu.VMEM((cols, width), jnp.float32)],
        compiler_params=pltpu.CompilerParams(vmem_limit_bytes=40 * MIB),
        name="wo_grad",
    )(me, *heads, *dattn)


def window_bias(start, first_key, window, block, plane):
    key_at = first_key + lax.broadcasted_iota(jnp.int32, (window, block), 0)
    query_at = first_key + plane + lax.broadcasted_iota(jnp.int32, (window, block), 1)
    allowed = (key_at >= start) & (key_at <= query_at)
    return jnp.where(allowed, 0.0, MASKED_SCORE)


def attend_kernel(
    me_ref, q_ref, before_ref, kv_ref, start_ref, o0, o1, o2, o3, lse_ref, kv_all, *, plane, block
):
    window = plane + block
    step = pl.program_id(0)

    @pl.when(step == 0)
    def _():
        kv_all[:plane] = before_ref[...]
        kv_all[plane:] = kv_ref[...]

    first_key = pl.multiple_of((me_ref[0] ^ step) * block, block)
    keys = kv_all[pl.ds(first_key, window), :LANES]
    values = kv_all[pl.ds(first_key, window), LANES:]
    values_t = values.astype(jnp.float32).T.astype(jnp.bfloat16)
    bias = window_bias(start_ref[...], first_key, window, block, plane)
    heads = []
    for h in range(4):
        scores = nt_dot(keys, q_ref[h]) + bias
        top = jnp.max(scores, axis=0, keepdims=True)
        weights = jnp.exp(scores - top)
        total = jnp.sum(weights, axis=0, keepdims=True)
        mixed = nn_dot(values_t, weights.astype(jnp.bfloat16)) / total
        lse_ref[h : h + 1, :] = top + jnp.log(total)
        heads.append(mixed.T)
    pairs = jnp.concatenate([p.astype(jnp.bfloat16) for p in join_heads(heads)], axis=1)
    for s, o_ref in enumerate((o0, o1, o2, o3)):

        @pl.when(step == s)
        def _(o_ref=o_ref):
            o_ref[...] = pairs


def attend(me, q4, before, kv, start, block):
    plane = q4.shape[1]
    whole = pl.BlockSpec((plane, 2 * LANES), lambda i, m: (0, 0))
    return pl.pallas_call(
        functools.partial(attend_kernel, plane=plane, block=block),
        grid_spec=pltpu.PrefetchScalarGridSpec(
            num_scalar_prefetch=1,
            grid=(4,),
            in_specs=[
                pl.BlockSpec((4, block, LANES), lambda i, m: (0, m[0] ^ i, 0)),
                whole,
                whole,
                pl.BlockSpec((1, block), lambda i, m: (0, m[0] ^ i)),
            ],
            out_specs=[pl.BlockSpec((block, 2 * LANES), lambda i, m: (0, 0))] * 4
            + [pl.BlockSpec((4, block), lambda i, m: (0, m[0] ^ i))],
            scratch_shapes=[pltpu.VMEM((2 * plane, 2 * LANES), jnp.bfloat16)],
        ),
        out_shape=[jax.ShapeDtypeStruct((block, 2 * LANES), jnp.bfloat16)] * 4
        + [jax.ShapeDtypeStruct((4, plane), jnp.float32)],
        compiler_params=pltpu.CompilerParams(vmem_limit_bytes=48 * MIB),
        name="attend",
    )(me, q4, before, kv, start)


def attend_back_kernel(
    me_ref,
    q_ref,
    before_ref,
    kv_ref,
    start_ref,
    lse_ref,
    do0,
    do1,
    do2,
    do3,
    cos_ref,
    sin_ref,
    dq_ref,
    dbefore_ref,
    dkv_ref,
    kv_all,
    sums,
    do_now,
    *,
    plane,
    block,
):
    window = plane + block
    step = pl.program_id(0)

    @pl.when(step == 0)
    def _():
        kv_all[:plane] = before_ref[...]
        kv_all[plane:] = kv_ref[...]
        sums[...] = jnp.zeros_like(sums)

    for s, do_ref in enumerate((do0, do1, do2, do3)):

        @pl.when(step == s)
        def _(do_ref=do_ref):
            do_now[...] = do_ref[...]

    first_key = pl.multiple_of((me_ref[0] ^ step) * block, block)
    keys = kv_all[pl.ds(first_key, window), :LANES]
    values = kv_all[pl.ds(first_key, window), LANES:]
    keys_t = keys.astype(jnp.float32).T.astype(jnp.bfloat16)
    bias = window_bias(start_ref[...], first_key, window, block, plane)
    grad = do_now[...].astype(jnp.float32)
    grads = [g.astype(jnp.bfloat16) for g in spread_heads([grad[:, :LANES], grad[:, LANES:]])]
    heads = []
    dk_total, dv_total = None, None
    for h in range(4):
        q = q_ref[h]
        weights = jnp.exp(nt_dot(keys, q) + bias - lse_ref[h : h + 1, :])
        dv = nn_dot(weights.astype(jnp.bfloat16), grads[h])
        product = weights * nt_dot(values, grads[h])
        centre = jnp.sum(product, axis=0, keepdims=True)
        ds = (product - weights * centre).astype(jnp.bfloat16)
        dk = nn_dot(ds, q)
        heads.append(nn_dot(keys_t, ds).T)
        dk_total = dk if dk_total is None else dk_total + dk
        dv_total = dv if dv_total is None else dv_total + dv
    sums[pl.ds(first_key, window), :LANES] += dk_total
    sums[pl.ds(first_key, window), LANES:] += dv_total
    scale = 1.0 / math.sqrt(HEAD_SIZE)
    for i, pair in enumerate(join_heads(heads)):
        dq_ref[:, i * LANES : (i + 1) * LANES] = turn(
            pair * scale, cos_ref[...], -sin_ref[...]
        ).astype(jnp.bfloat16)

    @pl.when(step == 3)
    def _():
        dbefore_ref[...] = sums[:plane].astype(jnp.bfloat16)
        dkv_ref[...] = sums[plane:]


def attend_back(me, q4, before, kv, start, lse, do_list, cos_table, sin_table, block):
    plane = q4.shape[1]
    whole = pl.BlockSpec((plane, 2 * LANES), lambda i, m: (0, 0))
    small = pl.BlockSpec((block, 2 * LANES), lambda i, m: (0, 0))
    table = pl.BlockSpec((block, LANES), lambda i, m: (m[0] ^ i, 0))
    return pl.pallas_call(
        functools.partial(attend_back_kernel, plane=plane, block=block),
        grid_spec=pltpu.PrefetchScalarGridSpec(
            num_scalar_prefetch=1,
            grid=(4,),
            in_specs=[
                pl.BlockSpec((4, block, LANES), lambda i, m: (0, m[0] ^ i, 0)),
                whole,
                whole,
                pl.BlockSpec((1, block), lambda i, m: (0, m[0] ^ i)),
                pl.BlockSpec((4, block), lambda i, m: (0, m[0] ^ i)),
            ]
            + [small] * 4
            + [table, table],
            out_specs=[
                pl.BlockSpec((block, 2 * LANES), lambda i, m: (m[0] ^ i, 0)),
                whole,
                whole,
            ],
            scratch_shapes=[
                pltpu.VMEM((2 * plane, 2 * LANES), jnp.bfloat16),
                pltpu.VMEM((2 * plane, 2 * LANES), jnp.float32),
                pltpu.VMEM((block, 2 * LANES), jnp.bfloat16),
            ],
        ),
        out_shape=[
            jax.ShapeDtypeStruct((plane, 2 * LANES), jnp.bfloat16),
            jax.ShapeDtypeStruct((plane, 2 * LANES), jnp.bfloat16),
            jax.ShapeDtypeStruct((plane, 2 * LANES), jnp.float32),
        ],
        compiler_params=pltpu.CompilerParams(vmem_limit_bytes=48 * MIB),
        name="attend_back",
    )(me, q4, before, kv, start, lse, *do_list, cos_table, sin_table)


def hidden_kernel(x_ref, gain_ref, o0, o1, o2, o3, w0, w1, w2, w3, hidden_ref, hn_ref):
    hidden = x_ref[...].astype(jnp.float32)
    for o_ref, w_ref in ((o0, w0), (o1, w1), (o2, w2), (o3, w3)):
        hidden = hidden + nn_dot(o_ref[...], w_ref[...])
    hidden_ref[...] = hidden
    rinv = lax.rsqrt(jnp.mean(hidden * hidden, axis=1, keepdims=True) + EPSILON)
    hn_ref[...] = (hidden * rinv * gain_ref[...]).astype(jnp.bfloat16)


def second_norm(x, gain, o_list, wo_list):
    return pl.pallas_call(
        hidden_kernel,
        out_shape=[
            jax.ShapeDtypeStruct(x.shape, jnp.float32),
            jax.ShapeDtypeStruct(x.shape, jnp.bfloat16),
        ],
        compiler_params=pltpu.CompilerParams(vmem_limit_bytes=32 * MIB),
        name="second_norm",
    )(x, gain, *o_list, *wo_list)


def masked_softmax(logits, mask):
    shown = jnp.where(mask, logits, MASKED_SCORE)
    top = jnp.max(shown, axis=0, keepdims=True)
    raised = jnp.where(mask, jnp.exp(shown - top), 0.0)
    return raised / jnp.sum(raised, axis=0, keepdims=True)


def second_norm_back_kernel(*refs, low, tok, parts):
    hidden_ref, hn_ref, go_ref, router_ref, mask_ref, gain_ref = refs[:6]
    wo_refs = refs[6:10]
    part_refs = refs[10 : 10 + parts]
    dh_ref, dattn_ref, do0, do1, do2, do3, small_ref = refs[10 + parts :]
    if parts == 1:
        total = part_refs[0][...].astype(jnp.float32)
    else:
        total = whole_sum(part_refs, low)
    width = hidden_ref.shape[1]
    group = EXPERTS * tok // width
    spare = total[tok : tok + group] + total[tok + group :]
    dgate = jnp.concatenate(
        [spare[:, b * tok : (b + 1) * tok] for b in range(width // tok)], axis=0
    )
    hn = hn_ref[...]
    router = router_ref[...]
    gate = masked_softmax(nt_dot(router, hn), mask_ref[...] > 0)
    dlogits = gate * (dgate - jnp.sum(gate * dgate, axis=0, keepdims=True))
    dlogits = dlogits.astype(jnp.bfloat16)
    dhn = total[:tok] + tn_dot(dlogits, router)
    small_ref[:EXPERTS, :] = nn_dot(dlogits, hn)
    hidden = hidden_ref[...]
    rinv = lax.rsqrt(jnp.mean(hidden * hidden, axis=1, keepdims=True) + EPSILON)
    unit = hidden * rinv
    small_ref[EXPERTS:, :] = jnp.broadcast_to(
        jnp.sum(dhn * unit, axis=0, keepdims=True), (8, width)
    )
    scaled = dhn * gain_ref[...]
    dh = go_ref[...].astype(jnp.float32) + rinv * (
        scaled - unit * jnp.mean(scaled * unit, axis=1, keepdims=True)
    )
    dh_ref[...] = dh
    dattn = dh.astype(jnp.bfloat16)
    dattn_ref[...] = dattn
    for w_ref, do_ref in zip(wo_refs, (do0, do1, do2, do3)):
        do_ref[...] = nt_dot(dattn, w_ref[...]).astype(jnp.bfloat16)


def second_norm_back(hidden, hn, go, router, mask, gain, wo_list, parts, low):
    tok, width = hidden.shape
    first = pl.BlockSpec((1,) + parts[0].shape[1:], lambda i: (0, 0, 0))
    specs = [
        pl.BlockSpec(a.shape, functools.partial(lambda n, i: (0,) * n, a.ndim))
        for a in (hidden, hn, go, router, mask, gain, *wo_list)
    ]
    for part in parts:
        if part.ndim == 3:
            specs.append(pl.BlockSpec((1,) + part.shape[1:], lambda i: (0, 0, 0)))
        else:
            specs.append(pl.BlockSpec(part.shape, lambda i: (0, 0)))
    cols = wo_list[0].shape[0]
    shapes = [
        jax.ShapeDtypeStruct((tok, width), jnp.float32),
        jax.ShapeDtypeStruct((tok, width), jnp.bfloat16),
    ]
    shapes += [jax.ShapeDtypeStruct((tok, cols), jnp.bfloat16)] * 4
    shapes += [jax.ShapeDtypeStruct((EXPERTS + 8, width), jnp.float32)]
    return pl.pallas_call(
        functools.partial(second_norm_back_kernel, low=low, tok=tok, parts=len(parts)),
        grid=(1,),
        in_specs=specs,
        out_specs=[pl.BlockSpec(s.shape, lambda i: (0, 0)) for s in shapes],
        out_shape=shapes,
        compiler_params=pltpu.CompilerParams(vmem_limit_bytes=48 * MIB),
        name="second_norm_back",
    )(hidden, hn, go, router, mask, gain, *wo_list, *parts)


def first_norm_back_kernel(x_ref, dh_ref, gain_ref, keep_ref, came_ref, far_ref, dx_ref, part_ref):
    x = x_ref[...].astype(jnp.float32)
    rinv = lax.rsqrt(jnp.mean(x * x, axis=1, keepdims=True) + EPSILON)
    unit = x * rinv
    dxn = keep_ref[0].astype(jnp.float32) + came_ref[0].astype(jnp.float32)
    dxn = dxn + far_ref[...].astype(jnp.float32)
    part_ref[...] = jnp.broadcast_to(jnp.sum(dxn * unit, axis=0, keepdims=True), part_ref.shape)
    scaled = dxn * gain_ref[...]
    dx_ref[...] = dh_ref[...] + rinv * (
        scaled - unit * jnp.mean(scaled * unit, axis=1, keepdims=True)
    )


def first_norm_back(x, dh, gain, keep, came, far):
    tok, width = x.shape
    flat = pl.BlockSpec((tok, width), lambda i: (0, 0))
    first = pl.BlockSpec((1, tok, width), lambda i: (0, 0, 0))
    return pl.pallas_call(
        first_norm_back_kernel,
        grid=(1,),
        in_specs=[flat, flat, pl.BlockSpec((1, width), lambda i: (0, 0)), first, first, flat],
        out_specs=[flat, pl.BlockSpec((8, width), lambda i: (0, 0))],
        out_shape=[
            jax.ShapeDtypeStruct((tok, width), jnp.float32),
            jax.ShapeDtypeStruct((8, width), jnp.float32),
        ],
        compiler_params=pltpu.CompilerParams(vmem_limit_bytes=32 * MIB),
        name="first_norm_back",
    )(x, dh, gain, keep, came, far)


def output_kernel(*refs, low):
    hidden_ref, out_ref = refs[0], refs[-1]
    out_ref[...] = (hidden_ref[...] + whole_sum(refs[1:-1], low)).astype(jnp.bfloat16)


def layer_output(hidden, parts, low):
    specs = [pl.BlockSpec(hidden.shape, lambda i: (0, 0))]
    for part in parts:
        if part.ndim == 3:
            specs.append(pl.BlockSpec((1,) + part.shape[1:], lambda i: (0, 0, 0)))
        else:
            specs.append(pl.BlockSpec(part.shape, lambda i: (0, 0)))
    return pl.pallas_call(
        functools.partial(output_kernel, low=low),
        grid=(1,),
        in_specs=specs,
        out_specs=pl.BlockSpec(hidden.shape, lambda i: (0, 0)),
        out_shape=jax.ShapeDtypeStruct(hidden.shape, jnp.bfloat16),
        compiler_params=pltpu.CompilerParams(vmem_limit_bytes=32 * MIB),
        name="layer_output",
    )(hidden, *parts)


def expert_kernel(me_ref, *refs, total, chunk, tok, rows, cols):
    hn_refs, go_refs = refs[:total], refs[total : 2 * total]
    pos_ref, gate_ref, wg_ref, wu_ref, wd_ref = refs[2 * total : 2 * total + 5]
    y_ref, dx_ref, dgate_ref, grad_ref = refs[2 * total + 5 : 2 * total + 9]
    x_all, go_rows, slot_gate, sums = refs[2 * total + 9 :]
    for begin in range(0, total, chunk):
        for s in range(chunk):
            at = slice((begin + s) * tok, (begin + s + 1) * tok)
            spot = lax.broadcasted_iota(jnp.int32, (CAP, tok), 0)
            hot = spot == pos_ref[0, :, at]
            hot_low = hot.astype(jnp.bfloat16)
            mine = slice(s * CAP, (s + 1) * CAP)
            x_all[mine, :] = nn_dot(hot_low, hn_refs[begin + s][...]).astype(jnp.bfloat16)
            go_rows[mine, :] = nn_dot(hot_low, go_refs[begin + s][...]).astype(jnp.bfloat16)
            slot_gate[mine, :] = jnp.sum(
                jnp.where(hot, gate_ref[0, :, at], 0.0), axis=1, keepdims=True
            )
        x = x_all[...]
        go = go_rows[...]
        gate = slot_gate[...]
        a = nn_dot(x, wg_ref[0])
        b = nn_dot(x, wu_ref[0])
        dz = nt_dot(go, wd_ref[0])
        sig = 1.0 / (1.0 + jnp.exp(-a))
        silu = a * sig
        z = silu * b
        z_low = z.astype(jnp.bfloat16)
        dgate = jnp.sum(z_low.astype(jnp.float32) * dz, axis=1, keepdims=True)
        dz = dz * gate
        da = (dz * b * sig * (1.0 + a * (1.0 - sig))).astype(jnp.bfloat16)
        db = (dz * silu).astype(jnp.bfloat16)
        gz = (z * gate).astype(jnp.bfloat16)
        y = (nn_dot(z_low, wd_ref[0]) * gate).astype(jnp.bfloat16)
        dx = (nt_dot(da, wg_ref[0]) + nt_dot(db, wu_ref[0])).astype(jnp.bfloat16)
        for s in range(chunk):
            at = slice((begin + s) * tok, (begin + s + 1) * tok)
            mine = slice(s * CAP, (s + 1) * CAP)
            y_ref[begin + s, 0] = y[mine]
            dx_ref[begin + s, 0] = dx[mine]
            spot = lax.broadcasted_iota(jnp.int32, (CAP, tok), 0)
            hot = spot == pos_ref[0, :, at]
            dgate_ref[0, :, at] = jnp.sum(
                jnp.where(hot, dgate[mine], 0.0), axis=0, keepdims=True
            )
        for i, (left, right) in enumerate(((x, da), (x, db), (go, gz))):
            term = tn_dot(left, right).reshape(sums.shape[1:])
            if begin:
                sums[i] += term
            else:
                sums[i] = term
    for s in range(cols):
        grad_ref[:, s, 0] = jnp.swapaxes(sums[:, :, me_ref[1] ^ s], 0, 1).astype(jnp.bfloat16)


def experts(me, hn_list, go_list, pos, gate, w_gate, w_up, w_down, rows, cols, first, count):
    total = len(hn_list)
    tok, width = hn_list[0].shape
    hidden = w_gate.shape[2]
    chunk = 8 if total % 8 == 0 else total
    part = width // (rows * cols)
    slots = chunk * CAP

    def weight(shape):
        return pl.BlockSpec((1,) + shape, lambda e, m: (m[0] + first + e, 0, 0))

    token = pl.BlockSpec((tok, width), lambda e, m: (0, 0), pipeline_mode=pl.Buffered(1))
    line = pl.BlockSpec((1, 1, total * tok), lambda e, m: (first + e, 0, 0))
    slot = pl.BlockSpec((total, 1, CAP, width), lambda e, m: (0, e, 0, 0))
    return pl.pallas_call(
        functools.partial(
            expert_kernel, total=total, chunk=chunk, tok=tok, rows=rows, cols=cols
        ),
        grid_spec=pltpu.PrefetchScalarGridSpec(
            num_scalar_prefetch=1,
            grid=(count,),
            in_specs=[token] * (2 * total)
            + [line, line, weight((width, hidden)), weight((width, hidden)), weight((hidden, width))],
            out_specs=[
                slot,
                slot,
                pl.BlockSpec((1, 1, total * tok), lambda e, m: (e, 0, 0)),
                pl.BlockSpec(
                    (rows, cols, 1, 3, part, hidden), lambda e, m: (0, 0, e, 0, 0, 0)
                ),
            ],
            scratch_shapes=[
                pltpu.VMEM((slots, width), jnp.bfloat16),
                pltpu.VMEM((slots, width), jnp.bfloat16),
                pltpu.VMEM((slots, 1), jnp.float32),
                pltpu.VMEM((3, rows, cols, part, hidden), jnp.float32),
            ],
        ),
        out_shape=[
            jax.ShapeDtypeStruct((total, count, CAP, width), jnp.bfloat16),
            jax.ShapeDtypeStruct((total, count, CAP, width), jnp.bfloat16),
            jax.ShapeDtypeStruct((count, 1, total * tok), jnp.float32),
            jax.ShapeDtypeStruct((rows, cols, count, 3, part, hidden), jnp.bfloat16),
        ],
        compiler_params=pltpu.CompilerParams(vmem_limit_bytes=62 * MIB),
        name="experts",
    )(me, *hn_list, *go_list, pos, gate, w_gate, w_up, w_down)


def combine_kernel(me_ref, pos_ref, *refs, calls, count, tok, half, extra):
    y_refs, dx_refs, dgate_refs = refs[:calls], refs[calls : 2 * calls], refs[2 * calls : 3 * calls]
    out_keep, out_away, dhn_keep, dhn_away = refs[3 * calls :]
    width = out_keep.shape[2]
    spot = lax.broadcasted_iota(jnp.int32, (CAP, tok), 0)
    hot = jnp.concatenate(
        [(spot == pos_ref[e]).astype(jnp.float32).astype(jnp.bfloat16) for e in range(count)],
        axis=0,
    )

    def rows_of(value_refs):
        return jnp.concatenate([r[0].reshape(-1, width) for r in value_refs], axis=0)

    out = tn_dot(hot, rows_of(y_refs)).astype(jnp.bfloat16)
    dhn = tn_dot(hot, rows_of(dx_refs)).astype(jnp.bfloat16)
    row = lax.broadcasted_iota(jnp.int32, (extra, width), 0)
    lane = lax.broadcasted_iota(jnp.int32, (extra, width), 1)
    per_row = width // tok
    spare = jnp.zeros((extra, width), jnp.float32)
    done = 0
    for dgate_ref in dgate_refs:
        for e in range(dgate_ref.shape[0]):
            expert = me_ref[2] + done
            here = (row == expert // per_row) & (lane // tok == expert % per_row)
            line = jnp.concatenate([dgate_ref[e]] * per_row, axis=1)
            spare = spare + jnp.where(here, line, 0.0)
            done += 1
    spare_high = spare.astype(jnp.bfloat16)
    spare_low = (spare - spare_high.astype(jnp.float32)).astype(jnp.bfloat16)

    def store(out_ref, dhn_ref):
        out_ref[0] = out
        dhn_ref[0, :tok] = dhn
        dhn_ref[0, tok:] = jnp.concatenate([spare_high, spare_low], axis=0)

    @pl.when(pl.program_id(0) < half)
    def _():
        store(out_keep, dhn_keep)

    @pl.when(pl.program_id(0) >= half)
    def _():
        store(out_away, dhn_away)


def combine(me, pos, y_list, dx_list, dgate_list, tok):
    total, _, _, width = y_list[0].shape
    count = pos.shape[0]
    half = total // 2
    extra = EXPERTS * tok // width
    rows = tok + 2 * extra
    slots = [
        pl.BlockSpec((1,) + y.shape[1:], lambda s, m: (s, 0, 0, 0)) for y in y_list + dx_list
    ]
    lines = [pl.BlockSpec((d.shape[0], 1, tok), lambda s, m: (0, 0, s)) for d in dgate_list]

    def keep(s, m):
        return (jnp.minimum(s, half - 1), 0, 0)

    def away(s, m):
        return (jnp.maximum(s - half, 0), 0, 0)

    return pl.pallas_call(
        functools.partial(
            combine_kernel, calls=len(y_list), count=count, tok=tok, half=half, extra=extra
        ),
        grid_spec=pltpu.PrefetchScalarGridSpec(
            num_scalar_prefetch=1,
            grid=(total,),
            in_specs=[pl.BlockSpec((count, 1, tok), lambda s, m: (0, 0, s))] + slots + lines,
            out_specs=[
                pl.BlockSpec((1, tok, width), keep),
                pl.BlockSpec((1, tok, width), away),
                pl.BlockSpec((1, rows, width), keep),
                pl.BlockSpec((1, rows, width), away),
            ],
        ),
        out_shape=[
            jax.ShapeDtypeStruct((half, tok, width), jnp.bfloat16),
            jax.ShapeDtypeStruct((half, tok, width), jnp.bfloat16),
            jax.ShapeDtypeStruct((half, rows, width), jnp.bfloat16),
            jax.ShapeDtypeStruct((half, rows, width), jnp.bfloat16),
        ],
        compiler_params=pltpu.CompilerParams(vmem_limit_bytes=32 * MIB),
        name="combine",
    )(me, pos, *y_list, *dx_list, *dgate_list)


def finish_kernel(me_ref, *refs, calls):
    gate_ref, up_ref, down_ref = refs[4 * calls :]
    for s in range(4):

        @pl.when(pl.program_id(0) == s)
        def _(s=s):
            done = 0
            for call in range(calls):
                ref = refs[4 * call + s]
                for e in range(ref.shape[0]):
                    gate_ref[done] = ref[e, 0].astype(jnp.float32)
                    up_ref[done] = ref[e, 1].astype(jnp.float32)
                    down_ref[done] = ref[e, 2].astype(jnp.float32).T
                    done += 1


def finish(me, lists):
    calls = len(lists)
    parts = [p for one in lists for p in one]
    mine = sum(one[0].shape[0] for one in lists)
    part, hidden = parts[0].shape[2:]
    whole = [pl.BlockSpec(p.shape, lambda s, m: (0, 0, 0, 0)) for p in parts]
    return pl.pallas_call(
        functools.partial(finish_kernel, calls=calls),
        grid_spec=pltpu.PrefetchScalarGridSpec(
            num_scalar_prefetch=1,
            grid=(4,),
            in_specs=whole,
            out_specs=[
                pl.BlockSpec((mine, part, hidden), lambda s, m: (m[1] ^ s, 0, 0)),
                pl.BlockSpec((mine, part, hidden), lambda s, m: (m[1] ^ s, 0, 0)),
                pl.BlockSpec((mine, hidden, part), lambda s, m: (m[1] ^ s, 0, 0)),
            ],
        ),
        out_shape=[
            jax.ShapeDtypeStruct((4 * mine, part, hidden), jnp.float32),
            jax.ShapeDtypeStruct((4 * mine, part, hidden), jnp.float32),
            jax.ShapeDtypeStruct((4 * mine, hidden, part), jnp.float32),
        ],
        compiler_params=pltpu.CompilerParams(vmem_limit_bytes=40 * MIB),
        name="finish",
    )(me, *parts)


def places(seq_lengths, first_row, total_rows):
    seq_ends = jnp.cumsum(seq_lengths)
    spots = first_row + jnp.arange(total_rows, dtype=jnp.int32)
    passed = (spots[:, None] >= seq_ends[None, :]).astype(jnp.int32)
    starts = jnp.sum(passed * seq_lengths[None, :], axis=1)
    return spots, starts


def route_mask(routes_t, ids):
    return jnp.any(routes_t[None, :, :] == ids[:, None, None], axis=1)


def on_device(
    inputs,
    lengths,
    routes,
    norm1_gain,
    w_query,
    key_weight,
    value_weight,
    w_output,
    norm2_gain,
    router,
    w_gate,
    w_up,
    w_down,
    d_output,
):
    row_count = lax.axis_size("row")
    col_count = lax.axis_size("col")
    dp_count = lax.axis_size("dp")
    my_row, my_col = lax.axis_index("row"), lax.axis_index("col")
    tok, width = inputs.shape
    plane = tok * col_count
    query_cols, key_cols = w_query.shape[1], key_weight.shape[1]
    assert col_count == 4 and plane >= MAX_LEN - 1
    assert query_cols == 2 * LANES and key_cols == LANES
    local_experts = w_gate.shape[0]
    split = local_experts % col_count == 0
    axes = ("dp", "col") if split else ("dp",)
    mine_experts = local_experts // col_count if split else local_experts
    first_local = my_col * mine_experts if split else jnp.int32(0)
    first_expert = lax.axis_index("dp") * local_experts + first_local
    sources = dp_count * (col_count if split else 1)
    ids = jnp.arange(EXPERTS, dtype=jnp.int32)
    me = jnp.stack([my_col, my_row]).astype(jnp.int32)
    me_first = jnp.stack([first_local, my_col, first_expert]).astype(jnp.int32)

    x_list = gather_col(inputs)
    w_list = gather_row(jnp.concatenate([w_query, key_weight, value_weight], axis=1))
    spots, starts = places(lengths[0], my_row * plane, plane)
    frequency = jnp.exp(
        -math.log(ROPE_BASE) * jnp.arange(HEAD_SIZE // 2, dtype=jnp.float32) / (HEAD_SIZE // 2)
    )
    frequency = jnp.tile(frequency, 4)
    sign = jnp.tile(jnp.repeat(jnp.array([-1.0, 1.0], jnp.float32), HEAD_SIZE // 2), 2)
    angles = (spots - starts).astype(jnp.float32)[:, None] * frequency[None, :]
    cos_table = jnp.cos(angles)
    sin_table = jnp.sin(angles) * sign[None, :]
    start = (starts - (my_row - 1) * plane)[None, :]
    xn1, q4, kv, w_joined = project(me, norm1_gain[None, :], cos_table, sin_table, x_list, w_list)
    kv_before = lax.ppermute(kv, "row", [(i, i + 1) for i in range(row_count - 1)])

    wo_mine, routes_mine, go_mine = lax.optimization_barrier((w_output, routes, d_output, kv))[:3]
    wo_rows = gather_row(wo_mine)
    wo_place = jnp.zeros((query_cols, width), jnp.bfloat16)
    for s in range(row_count):
        at = lax.rem(my_row - s + row_count, row_count) * (width // row_count)
        wo_place = lax.dynamic_update_slice_in_dim(wo_place, wo_rows[s], at, 1)
    wo_list = gather_col(wo_place)
    routes_list = gather_tokens(routes_mine.reshape(-1, LANES), axes)
    go_list = gather_tokens(after(go_mine, wo_list[3]), axes)

    *heads, lse = attend(me, q4, kv_before, kv, start, tok)
    hidden, hn = second_norm(inputs, norm2_gain[None, :], exchange_col(heads), wo_list)

    routes_t = jnp.concatenate([r.reshape(tok, TOPK).T for r in routes_list], axis=1)
    mask_all = route_mask(routes_t, ids)
    mask_mine = lax.dynamic_slice_in_dim(mask_all, first_expert, mine_experts, 0)
    before = jnp.triu(jnp.ones((tok, tok), jnp.bfloat16), 1)
    rank = jnp.dot(
        mask_mine.reshape(mine_experts * sources, tok).astype(jnp.bfloat16),
        before,
        preferred_element_type=jnp.float32,
    ).astype(jnp.int32)
    pos = jnp.where(mask_mine, rank.reshape(mine_experts, sources * tok), -1)
    pos = pos.reshape(mine_experts, 1, sources * tok)
    per_row = width // tok
    mixed_ids = ids.reshape(-1, per_row).T.reshape(-1)
    mask_own = route_mask(routes.T, mixed_ids).astype(jnp.int32)
    router_t = router.T
    router_mixed = router_t.reshape(-1, per_row, width).swapaxes(0, 1).reshape(EXPERTS, width)

    hn_list = gather_tokens(hn, axes)
    logits_t = jnp.concatenate([nt_dot(router_t, h) for h in hn_list], axis=1)
    gate_all = masked_softmax(logits_t, mask_all)
    gate_mine = lax.dynamic_slice_in_dim(gate_all, first_expert, mine_experts, 0)
    gate_mine = gate_mine.reshape(mine_experts, 1, sources * tok)
    calls = 2 if split and mine_experts % 2 == 0 else 1
    count = mine_experts // calls
    results = [
        experts(
            me_first,
            hn_list,
            go_list,
            pos,
            gate_mine,
            w_gate,
            w_up,
            w_down,
            row_count,
            col_count,
            call * count,
            count,
        )
        for call in range(calls)
    ]
    y_list, dx_list, dgate_list, grad_list = [list(r) for r in zip(*results)]
    out_keep, out_away, dhn_keep, dhn_away = combine(
        me_first, pos, y_list, dx_list, dgate_list, tok
    )
    low = tok // 2
    if two_way(axes):
        dhn_parts = scatter_tokens(dhn_keep, dhn_away, low)
    else:
        dhn_terms = jnp.concatenate([dhn_keep, dhn_away], axis=0)
        dhn_parts = [lax.psum_scatter(dhn_terms, axes, scatter_dimension=0, tiled=False)]
    dh, dattn, *do_mine, small = second_norm_back(
        hidden, hn, d_output, router_mixed, mask_own, norm2_gain[None, :], wo_list, dhn_parts, low
    )

    do_list = exchange_col(do_mine)
    dq, dbefore, dkv = attend_back(
        me, q4, kv_before, kv, start, lse, do_list, cos_table, sin_table, tok
    )
    dafter = lax.ppermute(dbefore, "row", [(i + 1, i) for i in range(row_count - 1)])
    dqkv, dx_keep, dx_away = project_back(me, dq, dkv, dafter, cos_table, sin_table, w_joined, tok)
    dx_came = swap(dx_away, "col", 1)
    dx_far = (dx_keep[1].astype(jnp.float32) + dx_came[1].astype(jnp.float32)).astype(jnp.bfloat16)
    dx_far = swap(dx_far, "col", 2)
    d_inputs, gain_one = first_norm_back(
        inputs, dh, norm1_gain[None, :], dx_keep, dx_came, dx_far
    )

    out_keep, out_away, dattn_late = lax.optimization_barrier(
        (out_keep, out_away, dattn, do_list[2])
    )[:3]
    if two_way(axes):
        output = layer_output(hidden, scatter_tokens(out_keep, out_away, low), low)
    else:
        out_terms = jnp.concatenate([out_keep, out_away], axis=0)
        out_sum = lax.psum_scatter(out_terms, axes, scatter_dimension=0, tiled=False)
        output = (hidden + out_sum.astype(jnp.float32)).astype(jnp.bfloat16)
    wo_parts = wo_grad(me, heads, gather_col(dattn_late), row_count)
    d_w_output = sum_over_low(scatter_row(wo_parts).astype(jnp.bfloat16), "dp")
    qkv_parts = qkv_grad(me, xn1, dqkv, row_count)
    d_w_qkv = sum_over_low(scatter_row(qkv_parts).astype(jnp.bfloat16), "dp")

    if split:
        lists = []
        for grads in grad_list:
            sums = lax.psum_scatter(grads, "row", scatter_dimension=0, tiled=False)
            lists.append(exchange_col([sums[s] for s in range(col_count)]))
        d_w_gate, d_w_up, d_w_down = finish(me_first, lists)
    else:
        order = jnp.stack([my_col ^ s for s in range(col_count)])
        back = jnp.take(grad_list[0], order, axis=1)
        sums = lax.psum_scatter(
            back.reshape((row_count * col_count,) + back.shape[2:]),
            ("row", "col"),
            scatter_dimension=0,
            tiled=False,
        )
        d_w_gate = sums[:, 0].astype(jnp.float32)
        d_w_up = sums[:, 1].astype(jnp.float32)
        d_w_down = jnp.swapaxes(sums[:, 2], 1, 2).astype(jnp.float32)

    small = jnp.concatenate([small[: EXPERTS + 1], gain_one[:1]], axis=0)
    for axis in ("col", "dp", "row"):
        small = sum_over(small, axis)
    d_router = small[:EXPERTS].reshape(per_row, -1, width).swapaxes(0, 1).reshape(EXPERTS, width).T
    return (
        output,
        d_inputs,
        small[EXPERTS + 1],
        d_w_qkv[:, :query_cols],
        d_w_qkv[:, query_cols : query_cols + key_cols],
        d_w_qkv[:, query_cols + key_cols :],
        d_w_output,
        small[EXPERTS],
        d_router,
        d_w_gate,
        d_w_up,
        d_w_down,
    )


def solution(mesh):
    return jax.shard_map(
        on_device,
        mesh=mesh,
        in_specs=(
            P(("dp", "row", "col"), None),
            P("dp", None),
            P(("dp", "row", "col"), None),
            P(),
            P("row", "col"),
            P("row", "col"),
            P("row", "col"),
            P("col", "row"),
            P(),
            P(),
            P("dp", None, None),
            P("dp", None, None),
            P("dp", None, None),
            P(("dp", "row", "col"), None),
        ),
        out_specs=(
            P(("dp", "row", "col"), None),
            P(("dp", "row", "col"), None),
            P(),
            P("row", "col"),
            P("row", "col"),
            P("row", "col"),
            P("col", "row"),
            P(),
            P(),
            P("dp", ("row", "col"), None),
            P("dp", ("row", "col"), None),
            P("dp", None, ("row", "col")),
        ),
        check_vma=False,
    )
```

```python
import functools
import math

import jax
import jax.numpy as jnp
from jax import lax
from jax.experimental import pallas as pl
from jax.experimental.pallas import tpu as pltpu
from jax.sharding import PartitionSpec as P

HEAD_SIZE = 64
EXPERTS = 32
TOPK = 8
MAX_LEN = 1024
CAP = 96

EPSILON = 1e-06
MASKED_SCORE = -1e30
ROPE_BASE = 10000.0
LANES = 128
MIB = 1024 * 1024


def nt_dot(left, right):
    return lax.dot_general(
        left, right, (((1,), (1,)), ((), ())), preferred_element_type=jnp.float32
    )


def tn_dot(left, right):
    return lax.dot_general(
        left, right, (((0,), (0,)), ((), ())), preferred_element_type=jnp.float32
    )


def nn_dot(left, right):
    return jnp.dot(left, right, preferred_element_type=jnp.float32)


def swap(value, axis, step):
    return lax.ppermute(value, axis, [(i, i ^ step) for i in range(lax.axis_size(axis))])


def after(value, *others):
    return lax.optimization_barrier((value,) + others)[0]


def gather_col(value):
    far = swap(value, "col", 2)
    near = swap(value, "col", 1)
    return [value, near, far, swap(far, "col", 1)]


def exchange_col(blocks):
    return [blocks[0]] + [swap(blocks[s], "col", s) for s in (1, 2, 3)]


def shift_row(value, step):
    size = lax.axis_size("row")
    return lax.ppermute(value, "row", [(i, (i + step) % size) for i in range(size)])


def gather_row(value):
    return [value] + [shift_row(value, s) for s in range(1, lax.axis_size("row"))]


def scatter_row(blocks):
    total = blocks[0].astype(jnp.float32)
    for step in range(1, len(blocks)):
        total = total + shift_row(blocks[step], step).astype(jnp.float32)
    return total


def sum_over(value, axis):
    size = lax.axis_size(axis)
    if size & (size - 1):
        return lax.psum(value, axis)
    step = 1
    while step < size:
        value = value + swap(value, axis, step)
        step *= 2
    return value


def sum_over_low(value, axis):
    if lax.axis_size(axis) == 2:
        return value.astype(jnp.float32) + swap(value, axis, 1).astype(jnp.float32)
    return lax.psum(value, axis).astype(jnp.float32)


def two_way(axes):
    return axes == ("dp", "col") and lax.axis_size("dp") == 2


def gather_tokens(value, axes):
    if not two_way(axes):
        every = lax.all_gather(value, axes)
        return [every[s] for s in range(every.shape[0])]
    half = value.shape[0] // 2
    along_x = swap(value, "dp", 1)
    along_y = swap(value, "col", 2)
    near = swap(value, "col", 1)
    cross_low = swap(along_x[:half], "col", 2)
    cross_high = swap(along_y[half:], "dp", 1)
    near_x = swap(along_x, "col", 1)
    near_y = swap(along_y, "col", 1)
    cross = jnp.concatenate([cross_low, cross_high], axis=0)
    near_cross = swap(cross, "col", 1)
    return [value, along_y, along_x, cross, near, near_y, near_x, near_cross]


def add_first_kernel(keep_ref, came_ref, x_ref, y_ref, *, low):
    def total(spot, rows):
        return (
            keep_ref[spot, rows].astype(jnp.float32) + came_ref[spot, rows].astype(jnp.float32)
        ).astype(jnp.bfloat16)

    x_ref[0], x_ref[1] = total(2, slice(0, low)), total(3, slice(0, low))
    y_ref[0], y_ref[1] = total(1, slice(low, None)), total(3, slice(low, None))


def add_second_kernel(keep_ref, came_ref, x_ref, y_ref, low_ref, high_ref, *, low):
    def total(spot, rows, extra):
        return (
            keep_ref[spot, rows].astype(jnp.float32)
            + came_ref[spot, rows].astype(jnp.float32)
            + extra.astype(jnp.float32)
        ).astype(jnp.bfloat16)

    low_ref[...] = total(1, slice(0, low), x_ref[1])
    high_ref[...] = total(2, slice(low, None), y_ref[1])


def scatter_tokens(keep, away, low):
    rows, width = keep.shape[1:]
    high = rows - low
    came = swap(away, "col", 1)
    params = pltpu.CompilerParams(vmem_limit_bytes=60 * MIB)
    send_x, send_y = pl.pallas_call(
        functools.partial(add_first_kernel, low=low),
        out_shape=[
            jax.ShapeDtypeStruct((2, low, width), jnp.bfloat16),
            jax.ShapeDtypeStruct((2, high, width), jnp.bfloat16),
        ],
        compiler_params=params,
        name="add_first",
    )(keep, came)
    by_x, by_y = swap(send_x, "dp", 1), swap(send_y, "col", 2)
    last_low, last_high = pl.pallas_call(
        functools.partial(add_second_kernel, low=low),
        out_shape=[
            jax.ShapeDtypeStruct((low, width), jnp.bfloat16),
            jax.ShapeDtypeStruct((high, width), jnp.bfloat16),
        ],
        compiler_params=params,
        name="add_second",
    )(keep, came, by_x, by_y)
    return [keep, came, by_x, by_y, swap(last_low, "col", 2), swap(last_high, "dp", 1)]


def whole_sum(parts, low):
    keep, came, by_x, by_y, last_low, last_high = [p[...].astype(jnp.float32) for p in parts]
    return jnp.concatenate(
        [
            keep[0, :low] + came[0, :low] + by_x[0] + last_low,
            keep[0, low:] + came[0, low:] + by_y[0] + last_high,
        ],
        axis=0,
    )


def swap_halves(value):
    lane = lax.broadcasted_iota(jnp.int32, value.shape, 1)
    first = (lane % HEAD_SIZE) < HEAD_SIZE // 2
    half = HEAD_SIZE // 2
    return jnp.where(first, pltpu.roll(value, LANES - half, 1), pltpu.roll(value, half, 1))


def turn(value, cos_part, sin_part):
    return value * cos_part + swap_halves(value) * sin_part


def spread_heads(pairs):
    lane = lax.broadcasted_iota(jnp.int32, pairs[0].shape, 1)
    low_lane = lane < HEAD_SIZE
    return [
        jnp.where(low_lane, pairs[0], 0.0),
        jnp.where(low_lane, pltpu.roll(pairs[0], HEAD_SIZE, 1), 0.0),
        jnp.where(low_lane, 0.0, pltpu.roll(pairs[1], HEAD_SIZE, 1)),
        jnp.where(low_lane, 0.0, pairs[1]),
    ]


def join_heads(heads):
    lane = lax.broadcasted_iota(jnp.int32, heads[0].shape, 1)
    low_lane = lane < HEAD_SIZE
    return [
        jnp.where(low_lane, heads[0], pltpu.roll(heads[1], HEAD_SIZE, 1)),
        jnp.where(low_lane, pltpu.roll(heads[2], HEAD_SIZE, 1), heads[3]),
    ]


SMEM_SPEC = pl.BlockSpec(memory_space=pltpu.SMEM)
VMEM_SPEC = pl.BlockSpec(memory_space=pltpu.VMEM)


def place_rows(index, block):
    return pl.ds(pl.multiple_of(index * block, block), block)


def project_kernel(*refs, rows, block):
    me_ref, gain_ref, cos_ref, sin_ref = refs[:4]
    x_refs, w_refs = refs[4:8], refs[8 : 8 + rows]
    xn_ref, q_ref, kv_ref, w_ref = refs[8 + rows :]
    my_col, my_row = me_ref[0], me_ref[1]
    part = w_refs[0].shape[0]
    for s in range(rows):
        w_ref[place_rows(lax.rem(my_row - s + rows, rows), part), :] = w_refs[s][...]
    w_joined = w_ref[...]
    scale = 1.0 / math.sqrt(HEAD_SIZE)
    for s in range(4):
        at = place_rows(my_col ^ s, block)
        x = x_refs[s][...].astype(jnp.float32)
        rinv = lax.rsqrt(jnp.mean(x * x, axis=1, keepdims=True) + EPSILON)
        xn = (x * rinv * gain_ref[...]).astype(jnp.bfloat16)
        xn_ref[at, :] = xn
        joined = nn_dot(xn, w_joined)
        cos_part, sin_part = cos_ref[at, :], sin_ref[at, :]
        pairs = [
            turn(joined[:, i * LANES : (i + 1) * LANES], cos_part, sin_part) * scale
            for i in range(2)
        ]
        for h, head in enumerate(spread_heads(pairs)):
            q_ref[h, at, :] = head.astype(jnp.bfloat16)
        kv_ref[at, :LANES] = turn(joined[:, 2 * LANES : 3 * LANES], cos_part, sin_part).astype(
            jnp.bfloat16
        )
        kv_ref[at, LANES:] = joined[:, 3 * LANES :].astype(jnp.bfloat16)


def project(me, gain, cos_table, sin_table, x_list, w_list):
    block, width = x_list[0].shape
    rows = len(w_list)
    plane = 4 * block
    return pl.pallas_call(
        functools.partial(project_kernel, rows=rows, block=block),
        in_specs=[SMEM_SPEC] + [VMEM_SPEC] * (7 + rows),
        out_specs=[VMEM_SPEC] * 4,
        out_shape=[
            jax.ShapeDtypeStruct((plane, width), jnp.bfloat16),
            jax.ShapeDtypeStruct((4, plane, LANES), jnp.bfloat16),
            jax.ShapeDtypeStruct((plane, 2 * LANES), jnp.bfloat16),
            jax.ShapeDtypeStruct((width, 4 * LANES), jnp.bfloat16),
        ],
        compiler_params=pltpu.CompilerParams(vmem_limit_bytes=60 * MIB),
        name="project",
    )(me, gain, cos_table, sin_table, *x_list, *w_list)


def project_back_kernel(
    me_ref, dq_ref, own_ref, came_ref, cos_ref, sin_ref, w_ref, dqkv_ref, keep_ref, away_ref, *, block
):
    my_col = me_ref[0]
    for s in (1, 3, 0, 2):
        at = place_rows(my_col ^ s, block)
        total = own_ref[at, :] + came_ref[at, :].astype(jnp.float32)
        dk = turn(total[:, :LANES], cos_ref[at, :], -sin_ref[at, :]).astype(jnp.bfloat16)
        dqkv = jnp.concatenate([dq_ref[at, :], dk, total[:, LANES:].astype(jnp.bfloat16)], axis=1)
        dqkv_ref[at, :] = dqkv
        target = away_ref if s % 2 else keep_ref
        target[s // 2] = nt_dot(dqkv, w_ref[...]).astype(jnp.bfloat16)


def project_back(me, dq, own, came, cos_table, sin_table, w_joined, block):
    width = w_joined.shape[0]
    return pl.pallas_call(
        functools.partial(project_back_kernel, block=block),
        in_specs=[SMEM_SPEC] + [VMEM_SPEC] * 6,
        out_specs=[VMEM_SPEC] * 3,
        out_shape=[
            jax.ShapeDtypeStruct((dq.shape[0], 4 * LANES), jnp.bfloat16),
            jax.ShapeDtypeStruct((2, block, width), jnp.bfloat16),
            jax.ShapeDtypeStruct((2, block, width), jnp.bfloat16),
        ],
        compiler_params=pltpu.CompilerParams(vmem_limit_bytes=60 * MIB),
        name="project_back",
    )(me, dq, own, came, cos_table, sin_table, w_joined)


def qkv_grad_kernel(me_ref, xn_ref, dqkv_ref, *refs, rows):
    scratch = refs[rows]
    scratch[...] = tn_dot(xn_ref[...], dqkv_ref[...])
    part = refs[0].shape[0]
    for s in range(rows):
        at = place_rows(lax.rem(me_ref[1] + s, rows), part)
        refs[s][...] = scratch[at, :].astype(jnp.bfloat16)


def qkv_grad(me, xn, dqkv, rows):
    width, cols = xn.shape[1], dqkv.shape[1]
    return pl.pallas_call(
        functools.partial(qkv_grad_kernel, rows=rows),
        in_specs=[SMEM_SPEC, VMEM_SPEC, VMEM_SPEC],
        out_specs=[VMEM_SPEC] * rows,
        out_shape=[jax.ShapeDtypeStruct((width // rows, cols), jnp.bfloat16)] * rows,
        scratch_shapes=[pltpu.VMEM((width, cols), jnp.float32)],
        compiler_params=pltpu.CompilerParams(vmem_limit_bytes=60 * MIB),
        name="qkv_grad",
    )(me, xn, dqkv)


def wo_grad_kernel(me_ref, *refs, rows):
    scratch = refs[8 + rows]
    total = None
    for s in range(4):
        term = tn_dot(refs[s][...], refs[4 + s][...])
        total = term if total is None else total + term
    scratch[...] = total
    part = refs[8].shape[1]
    for s in range(rows):
        at = place_rows(lax.rem(me_ref[1] + s, rows), part)
        refs[8 + s][...] = scratch[:, at].astype(jnp.bfloat16)


def wo_grad(me, heads, dattn, rows):
    cols, width = heads[0].shape[1], dattn[0].shape[1]
    return pl.pallas_call(
        functools.partial(wo_grad_kernel, rows=rows),
        in_specs=[SMEM_SPEC] + [VMEM_SPEC] * 8,
        out_specs=[VMEM_SPEC] * rows,
        out_shape=[jax.ShapeDtypeStruct((cols, width // rows), jnp.bfloat16)] * rows,
        scratch_shapes=[pltpu.VMEM((cols, width), jnp.float32)],
        compiler_params=pltpu.CompilerParams(vmem_limit_bytes=60 * MIB),
        name="wo_grad",
    )(me, *heads, *dattn)


def window_bias(start, first_key, window, block, plane):
    key_at = first_key + lax.broadcasted_iota(jnp.int32, (window, block), 0)
    query_at = first_key + plane + lax.broadcasted_iota(jnp.int32, (window, block), 1)
    allowed = (key_at >= start) & (key_at <= query_at)
    return jnp.where(allowed, 0.0, MASKED_SCORE)


def attend_kernel(
    me_ref, q_ref, before_ref, kv_ref, start_ref, o0, o1, o2, o3, lse_ref, kv_all, *, plane, block
):
    window = plane + block
    step = pl.program_id(0)

    @pl.when(step == 0)
    def _():
        kv_all[:plane] = before_ref[...]
        kv_all[plane:] = kv_ref[...]

    first_key = pl.multiple_of((me_ref[0] ^ step) * block, block)
    keys = kv_all[pl.ds(first_key, window), :LANES]
    values = kv_all[pl.ds(first_key, window), LANES:]
    values_t = values.astype(jnp.float32).T.astype(jnp.bfloat16)
    bias = window_bias(start_ref[...], first_key, window, block, plane)
    heads = []
    for h in range(4):
        scores = nt_dot(keys, q_ref[h]) + bias
        top = jnp.max(scores, axis=0, keepdims=True)
        weights = jnp.exp(scores - top)
        total = jnp.sum(weights, axis=0, keepdims=True)
        mixed = nn_dot(values_t, weights.astype(jnp.bfloat16)) / total
        lse_ref[h : h + 1, :] = top + jnp.log(total)
        heads.append(mixed.T)
    pairs = jnp.concatenate([p.astype(jnp.bfloat16) for p in join_heads(heads)], axis=1)
    for s, o_ref in enumerate((o0, o1, o2, o3)):

        @pl.when(step == s)
        def _(o_ref=o_ref):
            o_ref[...] = pairs


def attend(me, q4, before, kv, start, block):
    plane = q4.shape[1]
    whole = pl.BlockSpec((plane, 2 * LANES), lambda i, m: (0, 0))
    return pl.pallas_call(
        functools.partial(attend_kernel, plane=plane, block=block),
        grid_spec=pltpu.PrefetchScalarGridSpec(
            num_scalar_prefetch=1,
            grid=(4,),
            in_specs=[
                pl.BlockSpec((4, block, LANES), lambda i, m: (0, m[0] ^ i, 0)),
                whole,
                whole,
                pl.BlockSpec((1, block), lambda i, m: (0, m[0] ^ i)),
            ],
            out_specs=[pl.BlockSpec((block, 2 * LANES), lambda i, m: (0, 0))] * 4
            + [pl.BlockSpec((4, block), lambda i, m: (0, m[0] ^ i))],
            scratch_shapes=[pltpu.VMEM((2 * plane, 2 * LANES), jnp.bfloat16)],
        ),
        out_shape=[jax.ShapeDtypeStruct((block, 2 * LANES), jnp.bfloat16)] * 4
        + [jax.ShapeDtypeStruct((4, plane), jnp.float32)],
        compiler_params=pltpu.CompilerParams(vmem_limit_bytes=60 * MIB),
        name="attend",
    )(me, q4, before, kv, start)


def attend_back_kernel(
    me_ref,
    q_ref,
    before_ref,
    kv_ref,
    start_ref,
    lse_ref,
    do0,
    do1,
    do2,
    do3,
    cos_ref,
    sin_ref,
    dq_ref,
    dbefore_ref,
    dkv_ref,
    kv_all,
    sums,
    do_now,
    *,
    plane,
    block,
):
    window = plane + block
    step = pl.program_id(0)

    @pl.when(step == 0)
    def _():
        kv_all[:plane] = before_ref[...]
        kv_all[plane:] = kv_ref[...]
        sums[...] = jnp.zeros_like(sums)

    for s, do_ref in enumerate((do0, do1, do2, do3)):

        @pl.when(step == s)
        def _(do_ref=do_ref):
            do_now[...] = do_ref[...]

    first_key = pl.multiple_of((me_ref[0] ^ step) * block, block)
    keys = kv_all[pl.ds(first_key, window), :LANES]
    values = kv_all[pl.ds(first_key, window), LANES:]
    keys_t = keys.astype(jnp.float32).T.astype(jnp.bfloat16)
    bias = window_bias(start_ref[...], first_key, window, block, plane)
    grad = do_now[...].astype(jnp.float32)
    grads = [g.astype(jnp.bfloat16) for g in spread_heads([grad[:, :LANES], grad[:, LANES:]])]
    heads = []
    dk_total, dv_total = None, None
    for h in range(4):
        q = q_ref[h]
        weights = jnp.exp(nt_dot(keys, q) + bias - lse_ref[h : h + 1, :])
        dv = nn_dot(weights.astype(jnp.bfloat16), grads[h])
        product = weights * nt_dot(values, grads[h])
        centre = jnp.sum(product, axis=0, keepdims=True)
        ds = (product - weights * centre).astype(jnp.bfloat16)
        dk = nn_dot(ds, q)
        heads.append(nn_dot(keys_t, ds).T)
        dk_total = dk if dk_total is None else dk_total + dk
        dv_total = dv if dv_total is None else dv_total + dv
    sums[pl.ds(first_key, window), :LANES] += dk_total
    sums[pl.ds(first_key, window), LANES:] += dv_total
    scale = 1.0 / math.sqrt(HEAD_SIZE)
    for i, pair in enumerate(join_heads(heads)):
        dq_ref[:, i * LANES : (i + 1) * LANES] = turn(
            pair * scale, cos_ref[...], -sin_ref[...]
        ).astype(jnp.bfloat16)

    @pl.when(step == 3)
    def _():
        dbefore_ref[...] = sums[:plane].astype(jnp.bfloat16)
        dkv_ref[...] = sums[plane:]


def attend_back(me, q4, before, kv, start, lse, do_list, cos_table, sin_table, block):
    plane = q4.shape[1]
    whole = pl.BlockSpec((plane, 2 * LANES), lambda i, m: (0, 0))
    small = pl.BlockSpec((block, 2 * LANES), lambda i, m: (0, 0))
    table = pl.BlockSpec((block, LANES), lambda i, m: (m[0] ^ i, 0))
    return pl.pallas_call(
        functools.partial(attend_back_kernel, plane=plane, block=block),
        grid_spec=pltpu.PrefetchScalarGridSpec(
            num_scalar_prefetch=1,
            grid=(4,),
            in_specs=[
                pl.BlockSpec((4, block, LANES), lambda i, m: (0, m[0] ^ i, 0)),
                whole,
                whole,
                pl.BlockSpec((1, block), lambda i, m: (0, m[0] ^ i)),
                pl.BlockSpec((4, block), lambda i, m: (0, m[0] ^ i)),
            ]
            + [small] * 4
            + [table, table],
            out_specs=[
                pl.BlockSpec((block, 2 * LANES), lambda i, m: (m[0] ^ i, 0)),
                whole,
                whole,
            ],
            scratch_shapes=[
                pltpu.VMEM((2 * plane, 2 * LANES), jnp.bfloat16),
                pltpu.VMEM((2 * plane, 2 * LANES), jnp.float32),
                pltpu.VMEM((block, 2 * LANES), jnp.bfloat16),
            ],
        ),
        out_shape=[
            jax.ShapeDtypeStruct((plane, 2 * LANES), jnp.bfloat16),
            jax.ShapeDtypeStruct((plane, 2 * LANES), jnp.bfloat16),
            jax.ShapeDtypeStruct((plane, 2 * LANES), jnp.float32),
        ],
        compiler_params=pltpu.CompilerParams(vmem_limit_bytes=60 * MIB),
        name="attend_back",
    )(me, q4, before, kv, start, lse, *do_list, cos_table, sin_table)


def hidden_kernel(x_ref, gain_ref, o0, o1, o2, o3, w0, w1, w2, w3, hidden_ref, hn_ref):
    hidden = x_ref[...].astype(jnp.float32)
    for o_ref, w_ref in ((o0, w0), (o1, w1), (o2, w2), (o3, w3)):
        hidden = hidden + nn_dot(o_ref[...], w_ref[...])
    hidden_ref[...] = hidden
    rinv = lax.rsqrt(jnp.mean(hidden * hidden, axis=1, keepdims=True) + EPSILON)
    hn_ref[...] = (hidden * rinv * gain_ref[...]).astype(jnp.bfloat16)


def second_norm(x, gain, o_list, wo_list):
    return pl.pallas_call(
        hidden_kernel,
        out_shape=[
            jax.ShapeDtypeStruct(x.shape, jnp.float32),
            jax.ShapeDtypeStruct(x.shape, jnp.bfloat16),
        ],
        compiler_params=pltpu.CompilerParams(vmem_limit_bytes=60 * MIB),
        name="second_norm",
    )(x, gain, *o_list, *wo_list)


def masked_softmax(logits, mask):
    shown = jnp.where(mask, logits, MASKED_SCORE)
    top = jnp.max(shown, axis=0, keepdims=True)
    raised = jnp.where(mask, jnp.exp(shown - top), 0.0)
    return raised / jnp.sum(raised, axis=0, keepdims=True)


def second_norm_back_kernel(*refs, low, tok, parts):
    hidden_ref, hn_ref, go_ref, router_ref, mask_ref, gain_ref = refs[:6]
    wo_refs = refs[6:10]
    part_refs = refs[10 : 10 + parts]
    dh_ref, dattn_ref, do0, do1, do2, do3, small_ref = refs[10 + parts :]
    if parts == 1:
        total = part_refs[0][...].astype(jnp.float32)
    else:
        total = whole_sum(part_refs, low)
    width = hidden_ref.shape[1]
    group = EXPERTS * tok // width
    spare = total[tok : tok + group] + total[tok + group :]
    dgate = jnp.concatenate(
        [spare[:, b * tok : (b + 1) * tok] for b in range(width // tok)], axis=0
    )
    hn = hn_ref[...]
    router = router_ref[...]
    gate = masked_softmax(nt_dot(router, hn), mask_ref[...] > 0)
    dlogits = gate * (dgate - jnp.sum(gate * dgate, axis=0, keepdims=True))
    dlogits = dlogits.astype(jnp.bfloat16)
    dhn = total[:tok] + tn_dot(dlogits, router)
    small_ref[:EXPERTS, :] = nn_dot(dlogits, hn)
    hidden = hidden_ref[...]
    rinv = lax.rsqrt(jnp.mean(hidden * hidden, axis=1, keepdims=True) + EPSILON)
    unit = hidden * rinv
    small_ref[EXPERTS:, :] = jnp.broadcast_to(
        jnp.sum(dhn * unit, axis=0, keepdims=True), (8, width)
    )
    scaled = dhn * gain_ref[...]
    dh = go_ref[...].astype(jnp.float32) + rinv * (
        scaled - unit * jnp.mean(scaled * unit, axis=1, keepdims=True)
    )
    dh_ref[...] = dh
    dattn = dh.astype(jnp.bfloat16)
    dattn_ref[...] = dattn
    for w_ref, do_ref in zip(wo_refs, (do0, do1, do2, do3)):
        do_ref[...] = nt_dot(dattn, w_ref[...]).astype(jnp.bfloat16)


def second_norm_back(hidden, hn, go, router, mask, gain, wo_list, parts, low):
    tok, width = hidden.shape
    first = pl.BlockSpec((1,) + parts[0].shape[1:], lambda i: (0, 0, 0))
    specs = [
        pl.BlockSpec(a.shape, functools.partial(lambda n, i: (0,) * n, a.ndim))
        for a in (hidden, hn, go, router, mask, gain, *wo_list)
    ]
    for part in parts:
        if part.ndim == 3:
            specs.append(pl.BlockSpec((1,) + part.shape[1:], lambda i: (0, 0, 0)))
        else:
            specs.append(pl.BlockSpec(part.shape, lambda i: (0, 0)))
    cols = wo_list[0].shape[0]
    shapes = [
        jax.ShapeDtypeStruct((tok, width), jnp.float32),
        jax.ShapeDtypeStruct((tok, width), jnp.bfloat16),
    ]
    shapes += [jax.ShapeDtypeStruct((tok, cols), jnp.bfloat16)] * 4
    shapes += [jax.ShapeDtypeStruct((EXPERTS + 8, width), jnp.float32)]
    return pl.pallas_call(
        functools.partial(second_norm_back_kernel, low=low, tok=tok, parts=len(parts)),
        grid=(1,),
        in_specs=specs,
        out_specs=[pl.BlockSpec(s.shape, lambda i: (0, 0)) for s in shapes],
        out_shape=shapes,
        compiler_params=pltpu.CompilerParams(vmem_limit_bytes=60 * MIB),
        name="second_norm_back",
    )(hidden, hn, go, router, mask, gain, *wo_list, *parts)


def first_norm_back_kernel(x_ref, dh_ref, gain_ref, keep_ref, came_ref, far_ref, dx_ref, part_ref):
    x = x_ref[...].astype(jnp.float32)
    rinv = lax.rsqrt(jnp.mean(x * x, axis=1, keepdims=True) + EPSILON)
    unit = x * rinv
    dxn = keep_ref[0].astype(jnp.float32) + came_ref[0].astype(jnp.float32)
    dxn = dxn + far_ref[...].astype(jnp.float32)
    part_ref[...] = jnp.broadcast_to(jnp.sum(dxn * unit, axis=0, keepdims=True), part_ref.shape)
    scaled = dxn * gain_ref[...]
    dx_ref[...] = dh_ref[...] + rinv * (
        scaled - unit * jnp.mean(scaled * unit, axis=1, keepdims=True)
    )


def first_norm_back(x, dh, gain, keep, came, far):
    tok, width = x.shape
    flat = pl.BlockSpec((tok, width), lambda i: (0, 0))
    first = pl.BlockSpec((1, tok, width), lambda i: (0, 0, 0))
    return pl.pallas_call(
        first_norm_back_kernel,
        grid=(1,),
        in_specs=[flat, flat, pl.BlockSpec((1, width), lambda i: (0, 0)), first, first, flat],
        out_specs=[flat, pl.BlockSpec((8, width), lambda i: (0, 0))],
        out_shape=[
            jax.ShapeDtypeStruct((tok, width), jnp.float32),
            jax.ShapeDtypeStruct((8, width), jnp.float32),
        ],
        compiler_params=pltpu.CompilerParams(vmem_limit_bytes=60 * MIB),
        name="first_norm_back",
    )(x, dh, gain, keep, came, far)


def output_kernel(*refs, low):
    hidden_ref, out_ref = refs[0], refs[-1]
    out_ref[...] = (hidden_ref[...] + whole_sum(refs[1:-1], low)).astype(jnp.bfloat16)


def layer_output(hidden, parts, low):
    specs = [pl.BlockSpec(hidden.shape, lambda i: (0, 0))]
    for part in parts:
        if part.ndim == 3:
            specs.append(pl.BlockSpec((1,) + part.shape[1:], lambda i: (0, 0, 0)))
        else:
            specs.append(pl.BlockSpec(part.shape, lambda i: (0, 0)))
    return pl.pallas_call(
        functools.partial(output_kernel, low=low),
        grid=(1,),
        in_specs=specs,
        out_specs=pl.BlockSpec(hidden.shape, lambda i: (0, 0)),
        out_shape=jax.ShapeDtypeStruct(hidden.shape, jnp.bfloat16),
        compiler_params=pltpu.CompilerParams(vmem_limit_bytes=60 * MIB),
        name="layer_output",
    )(hidden, *parts)


def expert_kernel(me_ref, *refs, total, chunk, tok, rows, cols):
    hn_refs, go_refs = refs[:total], refs[total : 2 * total]
    pos_ref, gate_ref, wg_ref, wu_ref, wd_ref = refs[2 * total : 2 * total + 5]
    y_ref, dx_ref, dgate_ref, grad_ref = refs[2 * total + 5 : 2 * total + 9]
    x_all, go_rows, slot_gate, sums = refs[2 * total + 9 :]
    for begin in range(0, total, chunk):
        for s in range(chunk):
            at = slice((begin + s) * tok, (begin + s + 1) * tok)
            spot = lax.broadcasted_iota(jnp.int32, (CAP, tok), 0)
            hot = spot == pos_ref[0, :, at]
            hot_low = hot.astype(jnp.bfloat16)
            mine = slice(s * CAP, (s + 1) * CAP)
            x_all[mine, :] = nn_dot(hot_low, hn_refs[begin + s][...]).astype(jnp.bfloat16)
            go_rows[mine, :] = nn_dot(hot_low, go_refs[begin + s][...]).astype(jnp.bfloat16)
            slot_gate[mine, :] = jnp.sum(
                jnp.where(hot, gate_ref[0, :, at], 0.0), axis=1, keepdims=True
            )
        x = x_all[...]
        go = go_rows[...]
        gate = slot_gate[...]
        a = nn_dot(x, wg_ref[0])
        b = nn_dot(x, wu_ref[0])
        dz = nt_dot(go, wd_ref[0])
        sig = 1.0 / (1.0 + jnp.exp(-a))
        silu = a * sig
        z = silu * b
        z_low = z.astype(jnp.bfloat16)
        dgate = jnp.sum(z_low.astype(jnp.float32) * dz, axis=1, keepdims=True)
        dz = dz * gate
        da = (dz * b * sig * (1.0 + a * (1.0 - sig))).astype(jnp.bfloat16)
        db = (dz * silu).astype(jnp.bfloat16)
        gz = (z * gate).astype(jnp.bfloat16)
        y = (nn_dot(z_low, wd_ref[0]) * gate).astype(jnp.bfloat16)
        dx = (nt_dot(da, wg_ref[0]) + nt_dot(db, wu_ref[0])).astype(jnp.bfloat16)
        for s in range(chunk):
            at = slice((begin + s) * tok, (begin + s + 1) * tok)
            mine = slice(s * CAP, (s + 1) * CAP)
            y_ref[begin + s, 0] = y[mine]
            dx_ref[begin + s, 0] = dx[mine]
            spot = lax.broadcasted_iota(jnp.int32, (CAP, tok), 0)
            hot = spot == pos_ref[0, :, at]
            dgate_ref[0, :, at] = jnp.sum(
                jnp.where(hot, dgate[mine], 0.0), axis=0, keepdims=True
            )
        for i, (left, right) in enumerate(((x, da), (x, db), (go, gz))):
            term = tn_dot(left, right).reshape(sums.shape[1:])
            if begin:
                sums[i] += term
            else:
                sums[i] = term
    for s in range(cols):
        grad_ref[:, s, 0] = jnp.swapaxes(sums[:, :, me_ref[1] ^ s], 0, 1).astype(jnp.bfloat16)


def experts(me, hn_list, go_list, pos, gate, w_gate, w_up, w_down, rows, cols, first, count):
    total = len(hn_list)
    tok, width = hn_list[0].shape
    hidden = w_gate.shape[2]
    chunk = 8 if total % 8 == 0 else total
    part = width // (rows * cols)
    slots = chunk * CAP

    def weight(shape):
        return pl.BlockSpec((1,) + shape, lambda e, m: (m[0] + first + e, 0, 0))

    token = pl.BlockSpec((tok, width), lambda e, m: (0, 0), pipeline_mode=pl.Buffered(1))
    line = pl.BlockSpec((1, 1, total * tok), lambda e, m: (first + e, 0, 0))
    slot = pl.BlockSpec((total, 1, CAP, width), lambda e, m: (0, e, 0, 0))
    return pl.pallas_call(
        functools.partial(
            expert_kernel, total=total, chunk=chunk, tok=tok, rows=rows, cols=cols
        ),
        grid_spec=pltpu.PrefetchScalarGridSpec(
            num_scalar_prefetch=1,
            grid=(count,),
            in_specs=[token] * (2 * total)
            + [line, line, weight((width, hidden)), weight((width, hidden)), weight((hidden, width))],
            out_specs=[
                slot,
                slot,
                pl.BlockSpec((1, 1, total * tok), lambda e, m: (e, 0, 0)),
                pl.BlockSpec(
                    (rows, cols, 1, 3, part, hidden), lambda e, m: (0, 0, e, 0, 0, 0)
                ),
            ],
            scratch_shapes=[
                pltpu.VMEM((slots, width), jnp.bfloat16),
                pltpu.VMEM((slots, width), jnp.bfloat16),
                pltpu.VMEM((slots, 1), jnp.float32),
                pltpu.VMEM((3, rows, cols, part, hidden), jnp.float32),
            ],
        ),
        out_shape=[
            jax.ShapeDtypeStruct((total, count, CAP, width), jnp.bfloat16),
            jax.ShapeDtypeStruct((total, count, CAP, width), jnp.bfloat16),
            jax.ShapeDtypeStruct((count, 1, total * tok), jnp.float32),
            jax.ShapeDtypeStruct((rows, cols, count, 3, part, hidden), jnp.bfloat16),
        ],
        compiler_params=pltpu.CompilerParams(vmem_limit_bytes=60 * MIB),
        name="experts",
    )(me, *hn_list, *go_list, pos, gate, w_gate, w_up, w_down)


def combine_kernel(me_ref, pos_ref, *refs, calls, count, tok, half, extra):
    y_refs, dx_refs, dgate_refs = refs[:calls], refs[calls : 2 * calls], refs[2 * calls : 3 * calls]
    out_keep, out_away, dhn_keep, dhn_away = refs[3 * calls :]
    width = out_keep.shape[2]
    spot = lax.broadcasted_iota(jnp.int32, (CAP, tok), 0)
    hot = jnp.concatenate(
        [(spot == pos_ref[e]).astype(jnp.float32).astype(jnp.bfloat16) for e in range(count)],
        axis=0,
    )

    def rows_of(value_refs):
        return jnp.concatenate([r[0].reshape(-1, width) for r in value_refs], axis=0)

    out = tn_dot(hot, rows_of(y_refs)).astype(jnp.bfloat16)
    dhn = tn_dot(hot, rows_of(dx_refs)).astype(jnp.bfloat16)
    row = lax.broadcasted_iota(jnp.int32, (extra, width), 0)
    lane = lax.broadcasted_iota(jnp.int32, (extra, width), 1)
    per_row = width // tok
    spare = jnp.zeros((extra, width), jnp.float32)
    done = 0
    for dgate_ref in dgate_refs:
        for e in range(dgate_ref.shape[0]):
            expert = me_ref[2] + done
            here = (row == expert // per_row) & (lane // tok == expert % per_row)
            line = jnp.concatenate([dgate_ref[e]] * per_row, axis=1)
            spare = spare + jnp.where(here, line, 0.0)
            done += 1
    spare_high = spare.astype(jnp.bfloat16)
    spare_low = (spare - spare_high.astype(jnp.float32)).astype(jnp.bfloat16)

    def store(out_ref, dhn_ref):
        out_ref[0] = out
        dhn_ref[0, :tok] = dhn
        dhn_ref[0, tok:] = jnp.concatenate([spare_high, spare_low], axis=0)

    @pl.when(pl.program_id(0) < half)
    def _():
        store(out_keep, dhn_keep)

    @pl.when(pl.program_id(0) >= half)
    def _():
        store(out_away, dhn_away)


def combine(me, pos, y_list, dx_list, dgate_list, tok):
    total, _, _, width = y_list[0].shape
    count = pos.shape[0]
    half = total // 2
    extra = EXPERTS * tok // width
    rows = tok + 2 * extra
    slots = [
        pl.BlockSpec((1,) + y.shape[1:], lambda s, m: (s, 0, 0, 0)) for y in y_list + dx_list
    ]
    lines = [pl.BlockSpec((d.shape[0], 1, tok), lambda s, m: (0, 0, s)) for d in dgate_list]

    def keep(s, m):
        return (jnp.minimum(s, half - 1), 0, 0)

    def away(s, m):
        return (jnp.maximum(s - half, 0), 0, 0)

    return pl.pallas_call(
        functools.partial(
            combine_kernel, calls=len(y_list), count=count, tok=tok, half=half, extra=extra
        ),
        grid_spec=pltpu.PrefetchScalarGridSpec(
            num_scalar_prefetch=1,
            grid=(total,),
            in_specs=[pl.BlockSpec((count, 1, tok), lambda s, m: (0, 0, s))] + slots + lines,
            out_specs=[
                pl.BlockSpec((1, tok, width), keep),
                pl.BlockSpec((1, tok, width), away),
                pl.BlockSpec((1, rows, width), keep),
                pl.BlockSpec((1, rows, width), away),
            ],
        ),
        out_shape=[
            jax.ShapeDtypeStruct((half, tok, width), jnp.bfloat16),
            jax.ShapeDtypeStruct((half, tok, width), jnp.bfloat16),
            jax.ShapeDtypeStruct((half, rows, width), jnp.bfloat16),
            jax.ShapeDtypeStruct((half, rows, width), jnp.bfloat16),
        ],
        compiler_params=pltpu.CompilerParams(vmem_limit_bytes=60 * MIB),
        name="combine",
    )(me, pos, *y_list, *dx_list, *dgate_list)


def finish_kernel(me_ref, *refs, calls):
    gate_ref, up_ref, down_ref = refs[4 * calls :]
    for s in range(4):

        @pl.when(pl.program_id(0) == s)
        def _(s=s):
            done = 0
            for call in range(calls):
                ref = refs[4 * call + s]
                for e in range(ref.shape[0]):
                    gate_ref[done] = ref[e, 0].astype(jnp.float32)
                    up_ref[done] = ref[e, 1].astype(jnp.float32)
                    down_ref[done] = ref[e, 2].astype(jnp.float32)
                    done += 1


def finish(me, lists):
    calls = len(lists)
    parts = [p for one in lists for p in one]
    mine = sum(one[0].shape[0] for one in lists)
    part, hidden = parts[0].shape[2:]
    whole = [pl.BlockSpec(p.shape, lambda s, m: (0, 0, 0, 0)) for p in parts]
    return pl.pallas_call(
        functools.partial(finish_kernel, calls=calls),
        grid_spec=pltpu.PrefetchScalarGridSpec(
            num_scalar_prefetch=1,
            grid=(4,),
            in_specs=whole,
            out_specs=[
                pl.BlockSpec((mine, part, hidden), lambda s, m: (m[1] ^ s, 0, 0)),
                pl.BlockSpec((mine, part, hidden), lambda s, m: (m[1] ^ s, 0, 0)),
                pl.BlockSpec((mine, part, hidden), lambda s, m: (m[1] ^ s, 0, 0)),
            ],
        ),
        out_shape=[
            jax.ShapeDtypeStruct((4 * mine, part, hidden), jnp.float32),
            jax.ShapeDtypeStruct((4 * mine, part, hidden), jnp.float32),
            jax.ShapeDtypeStruct((4 * mine, part, hidden), jnp.float32),
        ],
        compiler_params=pltpu.CompilerParams(vmem_limit_bytes=60 * MIB),
        name="finish",
    )(me, *parts)


def places(seq_lengths, first_row, total_rows):
    seq_ends = jnp.cumsum(seq_lengths)
    spots = first_row + jnp.arange(total_rows, dtype=jnp.int32)
    passed = (spots[:, None] >= seq_ends[None, :]).astype(jnp.int32)
    starts = jnp.sum(passed * seq_lengths[None, :], axis=1)
    return spots, starts


def route_mask(routes_t, ids):
    return jnp.any(routes_t[None, :, :] == ids[:, None, None], axis=1)


def on_device(
    inputs,
    lengths,
    routes,
    norm1_gain,
    w_query,
    key_weight,
    value_weight,
    w_output,
    norm2_gain,
    router,
    w_gate,
    w_up,
    w_down,
    d_output,
):
    row_count = lax.axis_size("row")
    col_count = lax.axis_size("col")
    dp_count = lax.axis_size("dp")
    my_row, my_col = lax.axis_index("row"), lax.axis_index("col")
    tok, width = inputs.shape
    plane = tok * col_count
    query_cols, key_cols = w_query.shape[1], key_weight.shape[1]
    assert col_count == 4 and plane >= MAX_LEN - 1
    assert query_cols == 2 * LANES and key_cols == LANES
    local_experts = w_gate.shape[0]
    split = local_experts % col_count == 0
    axes = ("dp", "col") if split else ("dp",)
    mine_experts = local_experts // col_count if split else local_experts
    first_local = my_col * mine_experts if split else jnp.int32(0)
    first_expert = lax.axis_index("dp") * local_experts + first_local
    sources = dp_count * (col_count if split else 1)
    ids = jnp.arange(EXPERTS, dtype=jnp.int32)
    me = jnp.stack([my_col, my_row]).astype(jnp.int32)
    me_first = jnp.stack([first_local, my_col, first_expert]).astype(jnp.int32)

    x_list = gather_col(inputs)
    w_list = gather_row(jnp.concatenate([w_query, key_weight, value_weight], axis=1))
    wo_rows = gather_row(after(w_output, w_list[0]))
    spots, starts = places(lengths[0], my_row * plane, plane)
    frequency = jnp.exp(
        -math.log(ROPE_BASE) * jnp.arange(HEAD_SIZE // 2, dtype=jnp.float32) / (HEAD_SIZE // 2)
    )
    frequency = jnp.tile(frequency, 4)
    sign = jnp.tile(jnp.repeat(jnp.array([-1.0, 1.0], jnp.float32), HEAD_SIZE // 2), 2)
    angles = (spots - starts).astype(jnp.float32)[:, None] * frequency[None, :]
    cos_table = jnp.cos(angles)
    sin_table = jnp.sin(angles) * sign[None, :]
    start = (starts - (my_row - 1) * plane)[None, :]
    xn1, q4, kv, w_joined = project(me, norm1_gain[None, :], cos_table, sin_table, x_list, w_list)
    kv_before = lax.ppermute(kv, "row", [(i, i + 1) for i in range(row_count - 1)])

    wo_rows, routes_mine, go_mine = lax.optimization_barrier((wo_rows, routes, d_output, kv))[:3]
    wo_place = jnp.zeros((query_cols, width), jnp.bfloat16)
    for s in range(row_count):
        at = lax.rem(my_row - s + row_count, row_count) * (width // row_count)
        wo_place = lax.dynamic_update_slice_in_dim(wo_place, wo_rows[s], at, 1)
    wo_list = gather_col(wo_place)
    routes_list = gather_tokens(routes_mine.reshape(-1, LANES), axes)
    go_list = gather_tokens(go_mine, axes)

    *heads, lse = attend(me, q4, kv_before, kv, start, tok)
    o_list = exchange_col(heads)
    o_list, go_list = lax.optimization_barrier((o_list, go_list))
    hidden, hn = second_norm(inputs, norm2_gain[None, :], o_list, wo_list)

    routes_t = jnp.concatenate([r.reshape(tok, TOPK).T for r in routes_list], axis=1)
    mask_all = route_mask(routes_t, ids)
    mask_mine = lax.dynamic_slice_in_dim(mask_all, first_expert, mine_experts, 0)
    before = jnp.triu(jnp.ones((tok, tok), jnp.bfloat16), 1)
    rank = jnp.dot(
        mask_mine.reshape(mine_experts * sources, tok).astype(jnp.bfloat16),
        before,
        preferred_element_type=jnp.float32,
    ).astype(jnp.int32)
    pos = jnp.where(mask_mine, rank.reshape(mine_experts, sources * tok), -1)
    pos = pos.reshape(mine_experts, 1, sources * tok)
    per_row = width // tok
    mixed_ids = ids.reshape(-1, per_row).T.reshape(-1)
    mask_own = route_mask(routes.T, mixed_ids).astype(jnp.int32)
    router_t = router.T
    router_mixed = router_t.reshape(-1, per_row, width).swapaxes(0, 1).reshape(EXPERTS, width)

    hn_list = gather_tokens(hn, axes)
    logits_t = jnp.concatenate([nt_dot(router_t, h) for h in hn_list], axis=1)
    gate_all = masked_softmax(logits_t, mask_all)
    gate_mine = lax.dynamic_slice_in_dim(gate_all, first_expert, mine_experts, 0)
    gate_mine = gate_mine.reshape(mine_experts, 1, sources * tok)
    calls = mine_experts if split else 1
    count = mine_experts // calls
    results = [
        experts(
            me_first,
            hn_list,
            go_list,
            pos,
            gate_mine,
            w_gate,
            w_up,
            w_down,
            row_count,
            col_count,
            call * count,
            count,
        )
        for call in range(calls)
    ]
    y_list, dx_list, dgate_list, grad_list = [list(r) for r in zip(*results)]
    out_keep, out_away, dhn_keep, dhn_away = combine(
        me_first, pos, y_list, dx_list, dgate_list, tok
    )
    low = tok // 2
    if two_way(axes):
        dhn_parts = scatter_tokens(dhn_keep, dhn_away, low)
    else:
        dhn_terms = jnp.concatenate([dhn_keep, dhn_away], axis=0)
        dhn_parts = [lax.psum_scatter(dhn_terms, axes, scatter_dimension=0, tiled=False)]
    dh, dattn, *do_mine, small = second_norm_back(
        hidden, hn, d_output, router_mixed, mask_own, norm2_gain[None, :], wo_list, dhn_parts, low
    )

    do_list = exchange_col(do_mine)
    dq, dbefore, dkv = attend_back(
        me, q4, kv_before, kv, start, lse, do_list, cos_table, sin_table, tok
    )
    dafter = lax.ppermute(dbefore, "row", [(i + 1, i) for i in range(row_count - 1)])
    dqkv, dx_keep, dx_away = project_back(me, dq, dkv, dafter, cos_table, sin_table, w_joined, tok)
    dx_came = swap(dx_away, "col", 1)
    dx_far = (dx_keep[1].astype(jnp.float32) + dx_came[1].astype(jnp.float32)).astype(jnp.bfloat16)
    dx_far = swap(dx_far, "col", 2)
    lists = []
    if split:
        for grads in grad_list:
            sums = lax.psum_scatter(grads, "row", scatter_dimension=0, tiled=False)
            lists.append(exchange_col([sums[s] for s in range(col_count)]))
        early = len(lists) // 2
        dx_far, lists[:early] = lax.optimization_barrier((dx_far, lists[:early]))
    d_inputs, gain_one = first_norm_back(
        inputs, dh, norm1_gain[None, :], dx_keep, dx_came, dx_far
    )

    out_keep, out_away, dattn_late = lax.optimization_barrier(
        (out_keep, out_away, dattn, do_list[2])
    )[:3]
    if two_way(axes):
        output = layer_output(hidden, scatter_tokens(out_keep, out_away, low), low)
    else:
        out_terms = jnp.concatenate([out_keep, out_away], axis=0)
        out_sum = lax.psum_scatter(out_terms, axes, scatter_dimension=0, tiled=False)
        output = (hidden + out_sum.astype(jnp.float32)).astype(jnp.bfloat16)
    wo_parts = wo_grad(me, heads, gather_col(dattn_late), row_count)
    d_w_output = sum_over_low(scatter_row(wo_parts).astype(jnp.bfloat16), "dp")
    qkv_parts = qkv_grad(me, xn1, dqkv, row_count)
    d_w_qkv = sum_over_low(scatter_row(qkv_parts).astype(jnp.bfloat16), "dp")

    if split:
        d_w_gate, d_w_up, d_w_down = finish(me_first, lists)
        d_w_down = jnp.swapaxes(d_w_down, 1, 2)
    else:
        order = jnp.stack([my_col ^ s for s in range(col_count)])
        back = jnp.take(grad_list[0], order, axis=1)
        sums = lax.psum_scatter(
            back.reshape((row_count * col_count,) + back.shape[2:]),
            ("row", "col"),
            scatter_dimension=0,
            tiled=False,
        )
        d_w_gate = sums[:, 0].astype(jnp.float32)
        d_w_up = sums[:, 1].astype(jnp.float32)
        d_w_down = jnp.swapaxes(sums[:, 2], 1, 2).astype(jnp.float32)

    small = jnp.concatenate([small[: EXPERTS + 1], gain_one[:1]], axis=0)
    for axis in ("col", "dp", "row"):
        small = sum_over(small, axis)
    d_router = small[:EXPERTS].reshape(per_row, -1, width).swapaxes(0, 1).reshape(EXPERTS, width).T
    return (
        output,
        d_inputs,
        small[EXPERTS + 1],
        d_w_qkv[:, :query_cols],
        d_w_qkv[:, query_cols : query_cols + key_cols],
        d_w_qkv[:, query_cols + key_cols :],
        d_w_output,
        small[EXPERTS],
        d_router,
        d_w_gate,
        d_w_up,
        d_w_down,
    )


def solution(mesh):
    return jax.shard_map(
        on_device,
        mesh=mesh,
        in_specs=(
            P(("dp", "row", "col"), None),
            P("dp", None),
            P(("dp", "row", "col"), None),
            P(),
            P("row", "col"),
            P("row", "col"),
            P("row", "col"),
            P("col", "row"),
            P(),
            P(),
            P("dp", None, None),
            P("dp", None, None),
            P("dp", None, None),
            P(("dp", "row", "col"), None),
        ),
        out_specs=(
            P(("dp", "row", "col"), None),
            P(("dp", "row", "col"), None),
            P(),
            P("row", "col"),
            P("row", "col"),
            P("row", "col"),
            P("col", "row"),
            P(),
            P(),
            P("dp", ("row", "col"), None),
            P("dp", ("row", "col"), None),
            P("dp", None, ("row", "col")),
        ),
        check_vma=False,
    )
```

```python
import functools
import math

import jax
import jax.numpy as jnp
from jax import lax
from jax.experimental import pallas as pl
from jax.experimental.pallas import tpu as pltpu
from jax.sharding import PartitionSpec as P

HEAD_SIZE = 64
EXPERTS = 32
TOPK = 8
MAX_LEN = 1024
CAP = 96

EPSILON = 1e-06
MASKED_SCORE = -1e30
ROPE_BASE = 10000.0
LANES = 128
MIB = 1024 * 1024


def nt_dot(left, right):
    return lax.dot_general(
        left, right, (((1,), (1,)), ((), ())), preferred_element_type=jnp.float32
    )


def tn_dot(left, right):
    return lax.dot_general(
        left, right, (((0,), (0,)), ((), ())), preferred_element_type=jnp.float32
    )


def nn_dot(left, right):
    return jnp.dot(left, right, preferred_element_type=jnp.float32)


SMALL = pltpu.CompilerParams(vmem_limit_bytes=32 * MIB)


def swap(value, axis, step):
    return lax.ppermute(value, axis, [(i, i ^ step) for i in range(lax.axis_size(axis))])


def after(value, *others):
    return lax.optimization_barrier((value,) + others)[0]


def gather_col(value):
    far = swap(value, "col", 2)
    near = swap(value, "col", 1)
    return [value, near, far, swap(far, "col", 1)]


def exchange_col(blocks):
    return [blocks[0]] + [swap(blocks[s], "col", s) for s in (1, 2, 3)]


def shift_row(value, step):
    size = lax.axis_size("row")
    return lax.ppermute(value, "row", [(i, (i + step) % size) for i in range(size)])


def gather_row(value):
    return [value] + [shift_row(value, s) for s in range(1, lax.axis_size("row"))]


def scatter_row(blocks):
    total = blocks[0].astype(jnp.float32)
    for step in range(1, len(blocks)):
        total = total + shift_row(blocks[step], step).astype(jnp.float32)
    return total


def sum_over(value, axis):
    size = lax.axis_size(axis)
    if size & (size - 1):
        return lax.psum(value, axis)
    if size == 4:
        near, far, cross = [swap(value, axis, step) for step in (1, 2, 3)]
        return (value + near) + (far + cross)
    step = 1
    while step < size:
        value = value + swap(value, axis, step)
        step *= 2
    return value


def sum_over_low(value, axis):
    if lax.axis_size(axis) == 2:
        return value.astype(jnp.float32) + swap(value, axis, 1).astype(jnp.float32)
    return lax.psum(value, axis).astype(jnp.float32)


def two_way(axes):
    return axes == ("dp", "col") and lax.axis_size("dp") == 2


def gather_tokens(value, axes):
    if not two_way(axes):
        every = lax.all_gather(value, axes)
        return [every[s] for s in range(every.shape[0])]
    half = value.shape[0] // 2
    along_x = swap(value, "dp", 1)
    along_y = swap(value, "col", 2)
    near = swap(value, "col", 1)
    cross_low = swap(along_x[:half], "col", 2)
    cross_high = swap(along_y[half:], "dp", 1)
    near_x = swap(along_x, "col", 1)
    near_y = swap(along_y, "col", 1)
    cross = jnp.concatenate([cross_low, cross_high], axis=0)
    near_cross = swap(cross, "col", 1)
    return [value, along_y, along_x, cross, near, near_y, near_x, near_cross]


def gather_pair(value, axes):
    if not two_way(axes):
        return gather_tokens(value, axes)
    other = swap(value, "row", 1)
    return gather_tokens(value, axes) + gather_tokens(other, axes)


def add_first_kernel(keep_ref, came_ref, x_ref, y_ref, *, low):
    def total(spot, rows):
        return (
            keep_ref[spot, rows].astype(jnp.float32) + came_ref[spot, rows].astype(jnp.float32)
        ).astype(jnp.bfloat16)

    x_ref[0], x_ref[1] = total(2, slice(0, low)), total(3, slice(0, low))
    y_ref[0], y_ref[1] = total(1, slice(low, None)), total(3, slice(low, None))


def add_second_kernel(keep_ref, came_ref, x_ref, y_ref, low_ref, high_ref, *, low):
    def total(spot, rows, extra):
        return (
            keep_ref[spot, rows].astype(jnp.float32)
            + came_ref[spot, rows].astype(jnp.float32)
            + extra.astype(jnp.float32)
        ).astype(jnp.bfloat16)

    low_ref[...] = total(1, slice(0, low), x_ref[1])
    high_ref[...] = total(2, slice(low, None), y_ref[1])


def scatter_first(keep, away, low):
    rows, width = keep.shape[1:]
    came = swap(away, "col", 1)
    send_x, send_y = pl.pallas_call(
        functools.partial(add_first_kernel, low=low),
        out_shape=[
            jax.ShapeDtypeStruct((2, low, width), jnp.bfloat16),
            jax.ShapeDtypeStruct((2, rows - low, width), jnp.bfloat16),
        ],
        compiler_params=SMALL,
        name="add_first",
    )(keep, came)
    return keep, came, send_x, send_y


def scatter_second(keep, came, send_x, send_y, low):
    rows, width = keep.shape[1:]
    by_x, by_y = swap(send_x, "dp", 1), swap(send_y, "col", 2)
    last_low, last_high = pl.pallas_call(
        functools.partial(add_second_kernel, low=low),
        out_shape=[
            jax.ShapeDtypeStruct((low, width), jnp.bfloat16),
            jax.ShapeDtypeStruct((rows - low, width), jnp.bfloat16),
        ],
        compiler_params=SMALL,
        name="add_second",
    )(keep, came, by_x, by_y)
    return keep, came, by_x, by_y, last_low, last_high


def scatter_third(keep, came, by_x, by_y, last_low, last_high):
    return [keep, came, by_x, by_y, swap(last_low, "col", 2), swap(last_high, "dp", 1)]


def whole_sum(parts, low):
    keep, came, by_x, by_y, last_low, last_high = [
        p[...].astype(jnp.float32) for p in parts[:6]
    ]
    total = jnp.concatenate(
        [
            keep[0, :low] + came[0, :low] + by_x[0] + last_low,
            keep[0, low:] + came[0, low:] + by_y[0] + last_high,
        ],
        axis=0,
    )
    for part in parts[6:]:
        total = total + part[...].astype(jnp.float32)
    return total


def part_specs(parts):
    specs = []
    for part in parts:
        if part.ndim == 3:
            specs.append(pl.BlockSpec((1,) + part.shape[1:], lambda i: (0, 0, 0)))
        else:
            specs.append(pl.BlockSpec(part.shape, lambda i: (0, 0)))
    return specs


def part_sum_kernel(*refs, low):
    refs[-1][...] = whole_sum(refs[:-1], low).astype(jnp.bfloat16)


def part_sum(parts, low):
    shape = parts[0].shape[1:]
    return pl.pallas_call(
        functools.partial(part_sum_kernel, low=low),
        grid=(1,),
        in_specs=part_specs(parts),
        out_specs=pl.BlockSpec(shape, lambda i: (0, 0)),
        out_shape=jax.ShapeDtypeStruct(shape, jnp.bfloat16),
        compiler_params=SMALL,
        name="part_sum",
    )(*parts)


def swap_halves(value):
    lane = lax.broadcasted_iota(jnp.int32, value.shape, 1)
    first = (lane % HEAD_SIZE) < HEAD_SIZE // 2
    half = HEAD_SIZE // 2
    return jnp.where(first, pltpu.roll(value, LANES - half, 1), pltpu.roll(value, half, 1))


def turn(value, cos_part, sin_part):
    return value * cos_part + swap_halves(value) * sin_part


def spread_heads(pairs):
    lane = lax.broadcasted_iota(jnp.int32, pairs[0].shape, 1)
    low_lane = lane < HEAD_SIZE
    return [
        jnp.where(low_lane, pairs[0], 0.0),
        jnp.where(low_lane, pltpu.roll(pairs[0], HEAD_SIZE, 1), 0.0),
        jnp.where(low_lane, 0.0, pltpu.roll(pairs[1], HEAD_SIZE, 1)),
        jnp.where(low_lane, 0.0, pairs[1]),
    ]


def join_heads(heads):
    lane = lax.broadcasted_iota(jnp.int32, heads[0].shape, 1)
    low_lane = lane < HEAD_SIZE
    return [
        jnp.where(low_lane, heads[0], pltpu.roll(heads[1], HEAD_SIZE, 1)),
        jnp.where(low_lane, pltpu.roll(heads[2], HEAD_SIZE, 1), heads[3]),
    ]


SMEM_SPEC = pl.BlockSpec(memory_space=pltpu.SMEM)
VMEM_SPEC = pl.BlockSpec(memory_space=pltpu.VMEM)


def place_rows(index, block):
    return pl.ds(pl.multiple_of(index * block, block), block)


def project_kernel(*refs, rows, block):
    me_ref, gain_ref, cos_ref, sin_ref = refs[:4]
    x_refs, w_refs = refs[4:8], refs[8 : 8 + rows]
    xn_ref, q_ref, kv_ref, w_ref = refs[8 + rows :]
    my_col, my_row = me_ref[0], me_ref[1]
    part = w_refs[0].shape[0]
    for s in range(rows):
        w_ref[place_rows(lax.rem(my_row - s + rows, rows), part), :] = w_refs[s][...]
    w_joined = w_ref[...]
    scale = 1.0 / math.sqrt(HEAD_SIZE)
    for s in range(4):
        at = place_rows(my_col ^ s, block)
        x = x_refs[s][...].astype(jnp.float32)
        rinv = lax.rsqrt(jnp.mean(x * x, axis=1, keepdims=True) + EPSILON)
        xn = (x * rinv * gain_ref[...]).astype(jnp.bfloat16)
        xn_ref[at, :] = xn
        joined = nn_dot(xn, w_joined)
        cos_part, sin_part = cos_ref[at, :], sin_ref[at, :]
        pairs = [
            turn(joined[:, i * LANES : (i + 1) * LANES], cos_part, sin_part) * scale
            for i in range(2)
        ]
        for h, head in enumerate(spread_heads(pairs)):
            q_ref[h, at, :] = head.astype(jnp.bfloat16)
        kv_ref[at, :LANES] = turn(joined[:, 2 * LANES : 3 * LANES], cos_part, sin_part).astype(
            jnp.bfloat16
        )
        kv_ref[at, LANES:] = joined[:, 3 * LANES :].astype(jnp.bfloat16)


def project(me, gain, cos_table, sin_table, x_list, w_list):
    block, width = x_list[0].shape
    rows = len(w_list)
    plane = 4 * block
    return pl.pallas_call(
        functools.partial(project_kernel, rows=rows, block=block),
        in_specs=[SMEM_SPEC] + [VMEM_SPEC] * (7 + rows),
        out_specs=[VMEM_SPEC] * 4,
        out_shape=[
            jax.ShapeDtypeStruct((plane, width), jnp.bfloat16),
            jax.ShapeDtypeStruct((4, plane, LANES), jnp.bfloat16),
            jax.ShapeDtypeStruct((plane, 2 * LANES), jnp.bfloat16),
            jax.ShapeDtypeStruct((width, 4 * LANES), jnp.bfloat16),
        ],
        compiler_params=SMALL,
        name="project",
    )(me, gain, cos_table, sin_table, *x_list, *w_list)


def project_back_kernel(
    me_ref, dq_ref, own_ref, came_ref, cos_ref, sin_ref, w_ref, dqkv_ref, keep_ref, away_ref, *, block
):
    my_col = me_ref[0]
    for s in (1, 3, 0, 2):
        at = place_rows(my_col ^ s, block)
        total = own_ref[at, :] + came_ref[at, :].astype(jnp.float32)
        dk = turn(total[:, :LANES], cos_ref[at, :], -sin_ref[at, :]).astype(jnp.bfloat16)
        dqkv = jnp.concatenate([dq_ref[at, :], dk, total[:, LANES:].astype(jnp.bfloat16)], axis=1)
        dqkv_ref[at, :] = dqkv
        target = away_ref if s % 2 else keep_ref
        target[s // 2] = nt_dot(dqkv, w_ref[...]).astype(jnp.bfloat16)


def project_back(me, dq, own, came, cos_table, sin_table, w_joined, block):
    width = w_joined.shape[0]
    return pl.pallas_call(
        functools.partial(project_back_kernel, block=block),
        in_specs=[SMEM_SPEC] + [VMEM_SPEC] * 6,
        out_specs=[VMEM_SPEC] * 3,
        out_shape=[
            jax.ShapeDtypeStruct((dq.shape[0], 4 * LANES), jnp.bfloat16),
            jax.ShapeDtypeStruct((2, block, width), jnp.bfloat16),
            jax.ShapeDtypeStruct((2, block, width), jnp.bfloat16),
        ],
        compiler_params=SMALL,
        name="project_back",
    )(me, dq, own, came, cos_table, sin_table, w_joined)


def qkv_grad_kernel(me_ref, xn_ref, dqkv_ref, *refs, rows):
    scratch = refs[rows]
    scratch[...] = tn_dot(xn_ref[...], dqkv_ref[...])
    part = refs[0].shape[0]
    for s in range(rows):
        at = place_rows(lax.rem(me_ref[1] + s, rows), part)
        refs[s][...] = scratch[at, :].astype(jnp.bfloat16)


def qkv_grad(me, xn, dqkv, rows):
    width, cols = xn.shape[1], dqkv.shape[1]
    return pl.pallas_call(
        functools.partial(qkv_grad_kernel, rows=rows),
        in_specs=[SMEM_SPEC, VMEM_SPEC, VMEM_SPEC],
        out_specs=[VMEM_SPEC] * rows,
        out_shape=[jax.ShapeDtypeStruct((width // rows, cols), jnp.bfloat16)] * rows,
        scratch_shapes=[pltpu.VMEM((width, cols), jnp.float32)],
        compiler_params=SMALL,
        name="qkv_grad",
    )(me, xn, dqkv)


def wo_grad_kernel(me_ref, *refs, rows):
    scratch = refs[8 + rows]
    total = None
    for s in range(4):
        term = tn_dot(refs[s][...], refs[4 + s][...])
        total = term if total is None else total + term
    scratch[...] = total
    part = refs[8].shape[1]
    for s in range(rows):
        at = place_rows(lax.rem(me_ref[1] + s, rows), part)
        refs[8 + s][...] = scratch[:, at].astype(jnp.bfloat16)


def wo_grad(me, heads, dattn, rows):
    cols, width = heads[0].shape[1], dattn[0].shape[1]
    return pl.pallas_call(
        functools.partial(wo_grad_kernel, rows=rows),
        in_specs=[SMEM_SPEC] + [VMEM_SPEC] * 8,
        out_specs=[VMEM_SPEC] * rows,
        out_shape=[jax.ShapeDtypeStruct((cols, width // rows), jnp.bfloat16)] * rows,
        scratch_shapes=[pltpu.VMEM((cols, width), jnp.float32)],
        compiler_params=SMALL,
        name="wo_grad",
    )(me, *heads, *dattn)


def window_bias(start, first_key, window, block, plane):
    key_at = first_key + lax.broadcasted_iota(jnp.int32, (window, block), 0)
    query_at = first_key + plane + lax.broadcasted_iota(jnp.int32, (window, block), 1)
    allowed = (key_at >= start) & (key_at <= query_at)
    return jnp.where(allowed, 0.0, MASKED_SCORE)


def attend_kernel(
    me_ref, q_ref, before_ref, kv_ref, start_ref, o0, o1, o2, o3, lse_ref, kv_all, *, plane, block
):
    window = plane + block
    step = pl.program_id(0)

    @pl.when(step == 0)
    def _():
        kv_all[:plane] = before_ref[...]
        kv_all[plane:] = kv_ref[...]

    first_key = pl.multiple_of((me_ref[0] ^ step) * block, block)
    keys = kv_all[pl.ds(first_key, window), :LANES]
    values = kv_all[pl.ds(first_key, window), LANES:]
    values_t = values.astype(jnp.float32).T.astype(jnp.bfloat16)
    bias = window_bias(start_ref[...], first_key, window, block, plane)
    heads = []
    for h in range(4):
        scores = nt_dot(keys, q_ref[h]) + bias
        top = jnp.max(scores, axis=0, keepdims=True)
        weights = jnp.exp(scores - top)
        total = jnp.sum(weights, axis=0, keepdims=True)
        mixed = nn_dot(values_t, weights.astype(jnp.bfloat16)) / total
        lse_ref[h : h + 1, :] = top + jnp.log(total)
        heads.append(mixed.T)
    pairs = jnp.concatenate([p.astype(jnp.bfloat16) for p in join_heads(heads)], axis=1)
    for s, o_ref in enumerate((o0, o1, o2, o3)):

        @pl.when(step == s)
        def _(o_ref=o_ref):
            o_ref[...] = pairs


def attend(me, q4, before, kv, start, block):
    plane = q4.shape[1]
    whole = pl.BlockSpec((plane, 2 * LANES), lambda i, m: (0, 0))
    return pl.pallas_call(
        functools.partial(attend_kernel, plane=plane, block=block),
        grid_spec=pltpu.PrefetchScalarGridSpec(
            num_scalar_prefetch=1,
            grid=(4,),
            in_specs=[
                pl.BlockSpec((4, block, LANES), lambda i, m: (0, m[0] ^ i, 0)),
                whole,
                whole,
                pl.BlockSpec((1, block), lambda i, m: (0, m[0] ^ i)),
            ],
            out_specs=[pl.BlockSpec((block, 2 * LANES), lambda i, m: (0, 0))] * 4
            + [pl.BlockSpec((4, block), lambda i, m: (0, m[0] ^ i))],
            scratch_shapes=[pltpu.VMEM((2 * plane, 2 * LANES), jnp.bfloat16)],
        ),
        out_shape=[jax.ShapeDtypeStruct((block, 2 * LANES), jnp.bfloat16)] * 4
        + [jax.ShapeDtypeStruct((4, plane), jnp.float32)],
        compiler_params=SMALL,
        name="attend",
    )(me, q4, before, kv, start)


def attend_back_kernel(
    me_ref,
    q_ref,
    before_ref,
    kv_ref,
    start_ref,
    lse_ref,
    do0,
    do1,
    do2,
    do3,
    cos_ref,
    sin_ref,
    dq_ref,
    dbefore_ref,
    dkv_ref,
    kv_all,
    sums,
    do_now,
    *,
    plane,
    block,
):
    window = plane + block
    step = pl.program_id(0)

    @pl.when(step == 0)
    def _():
        kv_all[:plane] = before_ref[...]
        kv_all[plane:] = kv_ref[...]
        sums[...] = jnp.zeros_like(sums)

    for s, do_ref in enumerate((do0, do1, do2, do3)):

        @pl.when(step == s)
        def _(do_ref=do_ref):
            do_now[...] = do_ref[...]

    first_key = pl.multiple_of((me_ref[0] ^ step) * block, block)
    keys = kv_all[pl.ds(first_key, window), :LANES]
    values = kv_all[pl.ds(first_key, window), LANES:]
    keys_t = keys.astype(jnp.float32).T.astype(jnp.bfloat16)
    bias = window_bias(start_ref[...], first_key, window, block, plane)
    grad = do_now[...].astype(jnp.float32)
    grads = [g.astype(jnp.bfloat16) for g in spread_heads([grad[:, :LANES], grad[:, LANES:]])]
    heads = []
    dk_total, dv_total = None, None
    for h in range(4):
        q = q_ref[h]
        weights = jnp.exp(nt_dot(keys, q) + bias - lse_ref[h : h + 1, :])
        dv = nn_dot(weights.astype(jnp.bfloat16), grads[h])
        product = weights * nt_dot(values, grads[h])
        centre = jnp.sum(product, axis=0, keepdims=True)
        ds = (product - weights * centre).astype(jnp.bfloat16)
        dk = nn_dot(ds, q)
        heads.append(nn_dot(keys_t, ds).T)
        dk_total = dk if dk_total is None else dk_total + dk
        dv_total = dv if dv_total is None else dv_total + dv
    sums[pl.ds(first_key, window), :LANES] += dk_total
    sums[pl.ds(first_key, window), LANES:] += dv_total
    scale = 1.0 / math.sqrt(HEAD_SIZE)
    for i, pair in enumerate(join_heads(heads)):
        dq_ref[:, i * LANES : (i + 1) * LANES] = turn(
            pair * scale, cos_ref[...], -sin_ref[...]
        ).astype(jnp.bfloat16)

    @pl.when(step == 3)
    def _():
        dbefore_ref[...] = sums[:plane].astype(jnp.bfloat16)
        dkv_ref[...] = sums[plane:]


def attend_back(me, q4, before, kv, start, lse, do_list, cos_table, sin_table, block):
    plane = q4.shape[1]
    whole = pl.BlockSpec((plane, 2 * LANES), lambda i, m: (0, 0))
    small = pl.BlockSpec((block, 2 * LANES), lambda i, m: (0, 0))
    table = pl.BlockSpec((block, LANES), lambda i, m: (m[0] ^ i, 0))
    return pl.pallas_call(
        functools.partial(attend_back_kernel, plane=plane, block=block),
        grid_spec=pltpu.PrefetchScalarGridSpec(
            num_scalar_prefetch=1,
            grid=(4,),
            in_specs=[
                pl.BlockSpec((4, block, LANES), lambda i, m: (0, m[0] ^ i, 0)),
                whole,
                whole,
                pl.BlockSpec((1, block), lambda i, m: (0, m[0] ^ i)),
                pl.BlockSpec((4, block), lambda i, m: (0, m[0] ^ i)),
            ]
            + [small] * 4
            + [table, table],
            out_specs=[
                pl.BlockSpec((block, 2 * LANES), lambda i, m: (m[0] ^ i, 0)),
                whole,
                whole,
            ],
            scratch_shapes=[
                pltpu.VMEM((2 * plane, 2 * LANES), jnp.bfloat16),
                pltpu.VMEM((2 * plane, 2 * LANES), jnp.float32),
                pltpu.VMEM((block, 2 * LANES), jnp.bfloat16),
            ],
        ),
        out_shape=[
            jax.ShapeDtypeStruct((plane, 2 * LANES), jnp.bfloat16),
            jax.ShapeDtypeStruct((plane, 2 * LANES), jnp.bfloat16),
            jax.ShapeDtypeStruct((plane, 2 * LANES), jnp.float32),
        ],
        compiler_params=SMALL,
        name="attend_back",
    )(me, q4, before, kv, start, lse, *do_list, cos_table, sin_table)


def hidden_kernel(x_ref, gain_ref, o0, o1, o2, o3, w0, w1, w2, w3, hidden_ref, hn_ref):
    hidden = x_ref[...].astype(jnp.float32)
    for o_ref, w_ref in ((o0, w0), (o1, w1), (o2, w2), (o3, w3)):
        hidden = hidden + nn_dot(o_ref[...], w_ref[...])
    hidden_ref[...] = hidden
    rinv = lax.rsqrt(jnp.mean(hidden * hidden, axis=1, keepdims=True) + EPSILON)
    hn_ref[...] = (hidden * rinv * gain_ref[...]).astype(jnp.bfloat16)


def second_norm(x, gain, o_list, wo_list):
    return pl.pallas_call(
        hidden_kernel,
        out_shape=[
            jax.ShapeDtypeStruct(x.shape, jnp.float32),
            jax.ShapeDtypeStruct(x.shape, jnp.bfloat16),
        ],
        compiler_params=SMALL,
        name="second_norm",
    )(x, gain, *o_list, *wo_list)


def masked_softmax(logits, mask):
    shown = jnp.where(mask, logits, MASKED_SCORE)
    top = jnp.max(shown, axis=0, keepdims=True)
    raised = jnp.where(mask, jnp.exp(shown - top), 0.0)
    return raised / jnp.sum(raised, axis=0, keepdims=True)


def second_norm_back_kernel(*refs, low, tok, parts):
    hidden_ref, hn_ref, go_ref, router_ref, mask_ref, gain_ref = refs[:6]
    wo_refs = refs[6:10]
    part_refs = refs[10 : 10 + parts]
    dh_ref, dattn_ref, do0, do1, do2, do3, small_ref = refs[10 + parts :]
    if parts == 1:
        total = part_refs[0][...].astype(jnp.float32)
    else:
        total = whole_sum(part_refs, low)
    width = hidden_ref.shape[1]
    group = EXPERTS * tok // width
    spare = total[tok : tok + group] + total[tok + group :]
    dgate = jnp.concatenate(
        [spare[:, b * tok : (b + 1) * tok] for b in range(width // tok)], axis=0
    )
    hn = hn_ref[...]
    router = router_ref[...]
    gate = masked_softmax(nt_dot(router, hn), mask_ref[...] > 0)
    dlogits = gate * (dgate - jnp.sum(gate * dgate, axis=0, keepdims=True))
    dlogits = dlogits.astype(jnp.bfloat16)
    dhn = total[:tok] + tn_dot(dlogits, router)
    small_ref[:EXPERTS, :] = nn_dot(dlogits, hn)
    hidden = hidden_ref[...]
    rinv = lax.rsqrt(jnp.mean(hidden * hidden, axis=1, keepdims=True) + EPSILON)
    unit = hidden * rinv
    small_ref[EXPERTS:, :] = jnp.broadcast_to(
        jnp.sum(dhn * unit, axis=0, keepdims=True), (8, width)
    )
    scaled = dhn * gain_ref[...]
    dh = go_ref[...].astype(jnp.float32) + rinv * (
        scaled - unit * jnp.mean(scaled * unit, axis=1, keepdims=True)
    )
    dh_ref[...] = dh
    dattn = dh.astype(jnp.bfloat16)
    dattn_ref[...] = dattn
    for w_ref, do_ref in zip(wo_refs, (do0, do1, do2, do3)):
        do_ref[...] = nt_dot(dattn, w_ref[...]).astype(jnp.bfloat16)


def second_norm_back(hidden, hn, go, router, mask, gain, wo_list, parts, low):
    tok, width = hidden.shape
    specs = [
        pl.BlockSpec(a.shape, functools.partial(lambda n, i: (0,) * n, a.ndim))
        for a in (hidden, hn, go, router, mask, gain, *wo_list)
    ]
    specs += part_specs(parts)
    cols = wo_list[0].shape[0]
    shapes = [
        jax.ShapeDtypeStruct((tok, width), jnp.float32),
        jax.ShapeDtypeStruct((tok, width), jnp.bfloat16),
    ]
    shapes += [jax.ShapeDtypeStruct((tok, cols), jnp.bfloat16)] * 4
    shapes += [jax.ShapeDtypeStruct((EXPERTS + 8, width), jnp.float32)]
    return pl.pallas_call(
        functools.partial(second_norm_back_kernel, low=low, tok=tok, parts=len(parts)),
        grid=(1,),
        in_specs=specs,
        out_specs=[pl.BlockSpec(s.shape, lambda i: (0, 0)) for s in shapes],
        out_shape=shapes,
        compiler_params=SMALL,
        name="second_norm_back",
    )(hidden, hn, go, router, mask, gain, *wo_list, *parts)


def first_norm_back_kernel(x_ref, dh_ref, gain_ref, keep_ref, came_ref, far_ref, dx_ref, part_ref):
    x = x_ref[...].astype(jnp.float32)
    rinv = lax.rsqrt(jnp.mean(x * x, axis=1, keepdims=True) + EPSILON)
    unit = x * rinv
    dxn = keep_ref[0].astype(jnp.float32) + came_ref[0].astype(jnp.float32)
    dxn = dxn + far_ref[...].astype(jnp.float32)
    part_ref[...] = jnp.broadcast_to(jnp.sum(dxn * unit, axis=0, keepdims=True), part_ref.shape)
    scaled = dxn * gain_ref[...]
    dx_ref[...] = dh_ref[...] + rinv * (
        scaled - unit * jnp.mean(scaled * unit, axis=1, keepdims=True)
    )


def first_norm_back(x, dh, gain, keep, came, far):
    tok, width = x.shape
    flat = pl.BlockSpec((tok, width), lambda i: (0, 0))
    first = pl.BlockSpec((1, tok, width), lambda i: (0, 0, 0))
    return pl.pallas_call(
        first_norm_back_kernel,
        grid=(1,),
        in_specs=[flat, flat, pl.BlockSpec((1, width), lambda i: (0, 0)), first, first, flat],
        out_specs=[flat, pl.BlockSpec((8, width), lambda i: (0, 0))],
        out_shape=[
            jax.ShapeDtypeStruct((tok, width), jnp.float32),
            jax.ShapeDtypeStruct((8, width), jnp.float32),
        ],
        compiler_params=SMALL,
        name="first_norm_back",
    )(x, dh, gain, keep, came, far)


def output_kernel(*refs, low):
    hidden_ref, out_ref = refs[0], refs[-1]
    out_ref[...] = (hidden_ref[...] + whole_sum(refs[1:-1], low)).astype(jnp.bfloat16)


def layer_output(hidden, parts, low):
    specs = [pl.BlockSpec(hidden.shape, lambda i: (0, 0))] + part_specs(parts)
    return pl.pallas_call(
        functools.partial(output_kernel, low=low),
        grid=(1,),
        in_specs=specs,
        out_specs=pl.BlockSpec(hidden.shape, lambda i: (0, 0)),
        out_shape=jax.ShapeDtypeStruct(hidden.shape, jnp.bfloat16),
        compiler_params=SMALL,
        name="layer_output",
    )(hidden, *parts)


def expert_kernel(me_ref, *refs, later, chunk, tok, count):
    hn_refs, go_refs = refs[:8], refs[8:16]
    pos_ref, gate_ref, wg_ref, wu_ref, wd_ref = refs[16:21]
    begin_refs = refs[21:23] if later else ()
    outs = refs[23 if later else 21 :]
    out_refs, dhn_refs, grad_refs = outs[:2], outs[2:4], outs[4:6]
    x_all, go_rows, slot_gate, sums, y_all, dx_all, lines = outs[6:]
    e = pl.program_id(0)
    width = x_all.shape[1]
    spot = lax.broadcasted_iota(jnp.int32, (CAP, tok), 0)
    for begin in range(0, 8, chunk):
        for s in range(chunk):
            at = slice((begin + s) * tok, (begin + s + 1) * tok)
            hot = spot == pos_ref[e, :, at]
            hot_low = hot.astype(jnp.float32).astype(jnp.bfloat16)
            mine = slice(s * CAP, (s + 1) * CAP)
            x_all[mine, :] = nn_dot(hot_low, hn_refs[begin + s][...]).astype(jnp.bfloat16)
            go_rows[mine, :] = nn_dot(hot_low, go_refs[begin + s][...]).astype(jnp.bfloat16)
            slot_gate[mine, :] = jnp.sum(
                jnp.where(hot, gate_ref[e, :, at], 0.0), axis=1, keepdims=True
            )
        x = x_all[...]
        go = go_rows[...]
        gate = slot_gate[...]
        a = nn_dot(x, wg_ref[0])
        b = nn_dot(x, wu_ref[0])
        dz = nt_dot(go, wd_ref[0])
        sig = 1.0 / (1.0 + jnp.exp(-a))
        silu = a * sig
        z = silu * b
        z_low = z.astype(jnp.bfloat16)
        dgate = jnp.sum(z_low.astype(jnp.float32) * dz, axis=1, keepdims=True)
        dz = dz * gate
        da = (dz * b * sig * (1.0 + a * (1.0 - sig))).astype(jnp.bfloat16)
        db = (dz * silu).astype(jnp.bfloat16)
        gz = (z * gate).astype(jnp.bfloat16)
        y = (nn_dot(z_low, wd_ref[0]) * gate).astype(jnp.bfloat16)
        dx = (nt_dot(da, wg_ref[0]) + nt_dot(db, wu_ref[0])).astype(jnp.bfloat16)
        place = pl.ds(pl.multiple_of(e * CAP, CAP), CAP)
        for s in range(chunk):
            at = slice((begin + s) * tok, (begin + s + 1) * tok)
            mine = slice(s * CAP, (s + 1) * CAP)
            y_all[begin + s, place, :] = y[mine]
            dx_all[begin + s, place, :] = dx[mine]
            hot = spot == pos_ref[e, :, at]
            lines[e, :, at] = jnp.sum(jnp.where(hot, dgate[mine], 0.0), axis=0, keepdims=True)
        for i, (left, right) in enumerate(((x, da), (x, db), (go, gz))):
            term = tn_dot(left, right).reshape(sums.shape[1:])
            if begin:
                sums[i] += term
            else:
                sums[i] = term
    for q in range(4):
        for s in range(4):
            term = sums[:, me_ref[3] ^ q, me_ref[1] ^ s]
            if later:
                term = term + begin_refs[q // 2][0, q % 2, s].astype(jnp.float32)
            grad_refs[q // 2][0, q % 2, s] = term.astype(jnp.bfloat16)

    @pl.when(e == count - 1)
    def _():
        extra = EXPERTS * tok // width
        per_row = width // tok
        row = lax.broadcasted_iota(jnp.int32, (extra, width), 0)
        lane = lax.broadcasted_iota(jnp.int32, (extra, width), 1)
        for s in range(8):
            at = slice(s * tok, (s + 1) * tok)
            hot = jnp.concatenate(
                [
                    (spot == pos_ref[j, :, at]).astype(jnp.float32).astype(jnp.bfloat16)
                    for j in range(count)
                ],
                axis=0,
            )
            out_refs[s // 4][s % 4] = tn_dot(hot, y_all[s]).astype(jnp.bfloat16)
            dhn_refs[s // 4][s % 4, :tok] = tn_dot(hot, dx_all[s]).astype(jnp.bfloat16)
            spare = jnp.zeros((extra, width), jnp.float32)
            for j in range(count):
                expert = me_ref[2] + j
                here = (row == expert // per_row) & (lane // tok == expert % per_row)
                line = jnp.concatenate([lines[j, :, at]] * per_row, axis=1)
                spare = spare + jnp.where(here, line, 0.0)
            spare_high = spare.astype(jnp.bfloat16)
            spare_low = (spare - spare_high.astype(jnp.float32)).astype(jnp.bfloat16)
            dhn_refs[s // 4][s % 4, tok:] = jnp.concatenate([spare_high, spare_low], axis=0)


def experts(me, hn_list, go_list, pos, gate, w_gate, w_up, w_down, earlier=()):
    tok, width = hn_list[0].shape
    hidden = w_gate.shape[2]
    count = pos.shape[0]
    chunk = 4
    part = width // 16
    slots = chunk * CAP
    extra = EXPERTS * tok // width

    def weight(shape):
        return pl.BlockSpec((1,) + shape, lambda e, m: (m[0] + e, 0, 0))

    once = pl.Buffered(1)
    token = pl.BlockSpec((tok, width), lambda e, m: (0, 0), pipeline_mode=once)
    line = pl.BlockSpec((count, 1, 8 * tok), lambda e, m: (0, 0, 0))
    out = pl.BlockSpec((4, tok, width), lambda e, m: (0, 0, 0), pipeline_mode=once)
    dhn = pl.BlockSpec(
        (4, tok + 2 * extra, width), lambda e, m: (0, 0, 0), pipeline_mode=once
    )
    grad = pl.BlockSpec((1, 2, 4, 3, part, hidden), lambda e, m: (e, 0, 0, 0, 0, 0))
    return pl.pallas_call(
        functools.partial(
            expert_kernel, later=len(earlier) > 0, chunk=chunk, tok=tok, count=count
        ),
        grid_spec=pltpu.PrefetchScalarGridSpec(
            num_scalar_prefetch=1,
            grid=(count,),
            in_specs=[token] * 16
            + [line, line, weight((width, hidden)), weight((width, hidden)), weight((hidden, width))]
            + [grad] * len(earlier),
            out_specs=[out, out, dhn, dhn, grad, grad],
            scratch_shapes=[
                pltpu.VMEM((slots, width), jnp.bfloat16),
                pltpu.VMEM((slots, width), jnp.bfloat16),
                pltpu.VMEM((slots, 1), jnp.float32),
                pltpu.VMEM((3, 4, 4, part, hidden), jnp.float32),
                pltpu.VMEM((8, count * CAP, width), jnp.bfloat16),
                pltpu.VMEM((8, count * CAP, width), jnp.bfloat16),
                pltpu.VMEM((count, 1, 8 * tok), jnp.float32),
            ],
        ),
        out_shape=[jax.ShapeDtypeStruct((4, tok, width), jnp.bfloat16)] * 2
        + [jax.ShapeDtypeStruct((4, tok + 2 * extra, width), jnp.bfloat16)] * 2
        + [jax.ShapeDtypeStruct((count, 2, 4, 3, part, hidden), jnp.bfloat16)] * 2,
        compiler_params=pltpu.CompilerParams(vmem_limit_bytes=62 * MIB),
        name="experts",
    )(me, *hn_list, *go_list, pos, gate, w_gate, w_up, w_down, *earlier)


def finish_kernel(me_ref, *refs, calls):
    gate_ref, up_ref, down_ref = refs[4 * calls :]
    for s in range(4):
        for p in range(2):

            @pl.when((pl.program_id(0) == s) & (pl.program_id(1) == p))
            def _(s=s, p=p):
                for call in range(calls):
                    ref = refs[4 * call + s]
                    gate_ref[call] = ref[p, 0].astype(jnp.float32)
                    up_ref[call] = ref[p, 1].astype(jnp.float32)
                    down_ref[call] = ref[p, 2].astype(jnp.float32)


def finish(me, lists):
    calls = len(lists)
    parts = [p for one in lists for p in one]
    part, hidden = parts[0].shape[2:]
    whole = [pl.BlockSpec(p.shape, lambda s, p, m: (0, 0, 0, 0)) for p in parts]

    def spot(s, p, m):
        return ((m[1] ^ s) * 2 + ((m[3] % 2) ^ p), 0, 0)

    return pl.pallas_call(
        functools.partial(finish_kernel, calls=calls),
        grid_spec=pltpu.PrefetchScalarGridSpec(
            num_scalar_prefetch=1,
            grid=(4, 2),
            in_specs=whole,
            out_specs=[pl.BlockSpec((calls, part, hidden), spot)] * 3,
        ),
        out_shape=[jax.ShapeDtypeStruct((8 * calls, part, hidden), jnp.float32)] * 3,
        compiler_params=SMALL,
        name="finish",
    )(me, *parts)


def places(seq_lengths, first_row, total_rows):
    seq_ends = jnp.cumsum(seq_lengths)
    spots = first_row + jnp.arange(total_rows, dtype=jnp.int32)
    passed = (spots[:, None] >= seq_ends[None, :]).astype(jnp.int32)
    starts = jnp.sum(passed * seq_lengths[None, :], axis=1)
    return spots, starts


def route_mask(routes_t, ids):
    return jnp.any(routes_t[None, :, :] == ids[:, None, None], axis=1)


def on_device(
    inputs,
    lengths,
    routes,
    norm1_gain,
    w_query,
    key_weight,
    value_weight,
    w_output,
    norm2_gain,
    router,
    w_gate,
    w_up,
    w_down,
    d_output,
):
    row_count = lax.axis_size("row")
    col_count = lax.axis_size("col")
    dp_count = lax.axis_size("dp")
    my_row, my_col = lax.axis_index("row"), lax.axis_index("col")
    tok, width = inputs.shape
    plane = tok * col_count
    query_cols, key_cols = w_query.shape[1], key_weight.shape[1]
    assert col_count == 4 and plane >= MAX_LEN - 1
    assert query_cols == 2 * LANES and key_cols == LANES
    local_experts = w_gate.shape[0]
    split = dp_count == 2
    axes = ("dp", "col") if split else ("dp",)
    mine_experts = local_experts // (2 * col_count) if split else local_experts
    first_local = (my_col * 2 + my_row % 2) * mine_experts if split else jnp.int32(0)
    first_expert = lax.axis_index("dp") * local_experts + first_local
    sources = dp_count * (2 * col_count if split else 1)
    assert sources == 16 and mine_experts == 2 and row_count == 4
    ids = jnp.arange(EXPERTS, dtype=jnp.int32)
    me = jnp.stack([my_col, my_row]).astype(jnp.int32)
    me_first = jnp.stack([first_local, my_col, first_expert, my_row]).astype(jnp.int32)

    x_list = gather_col(inputs)
    w_list = gather_row(jnp.concatenate([w_query, key_weight, value_weight], axis=1))
    wo_rows = gather_row(after(w_output, w_list[0]))
    spots, starts = places(lengths[0], my_row * plane, plane)
    frequency = jnp.exp(
        -math.log(ROPE_BASE) * jnp.arange(HEAD_SIZE // 2, dtype=jnp.float32) / (HEAD_SIZE // 2)
    )
    frequency = jnp.tile(frequency, 4)
    sign = jnp.tile(jnp.repeat(jnp.array([-1.0, 1.0], jnp.float32), HEAD_SIZE // 2), 2)
    angles = (spots - starts).astype(jnp.float32)[:, None] * frequency[None, :]
    cos_table = jnp.cos(angles)
    sin_table = jnp.sin(angles) * sign[None, :]
    start = (starts - (my_row - 1) * plane)[None, :]
    xn1, q4, kv, w_joined = project(me, norm1_gain[None, :], cos_table, sin_table, x_list, w_list)
    kv_before = lax.ppermute(kv, "row", [(i, i + 1) for i in range(row_count - 1)])

    wo_rows, routes_mine, go_mine = lax.optimization_barrier((wo_rows, routes, d_output, kv))[:3]
    wo_place = jnp.zeros((query_cols, width), jnp.bfloat16)
    for s in range(row_count):
        at = lax.rem(my_row - s + row_count, row_count) * (width // row_count)
        wo_place = lax.dynamic_update_slice_in_dim(wo_place, wo_rows[s], at, 1)
    wo_list = gather_col(wo_place)
    routes_flat = routes_mine.reshape(-1, LANES)
    if split:
        both = jnp.concatenate([routes_flat, swap(routes_flat, "row", 1)], axis=0)
        both = gather_tokens(both, axes)
        part = routes_flat.shape[0]
        routes_list = [r[:part] for r in both] + [r[part:] for r in both]
    else:
        routes_list = gather_tokens(routes_flat, axes)
    go_list = gather_pair(go_mine, axes)

    *heads, lse = attend(me, q4, kv_before, kv, start, tok)
    o_list = exchange_col(heads)
    o_list, go_list[:8] = lax.optimization_barrier((o_list, go_list[:8]))
    hidden, hn = second_norm(inputs, norm2_gain[None, :], o_list, wo_list)

    routes_t = jnp.concatenate([r.reshape(tok, TOPK).T for r in routes_list], axis=1)
    mask_all = route_mask(routes_t, ids)
    mask_mine = lax.dynamic_slice_in_dim(mask_all, first_expert, mine_experts, 0)
    before = jnp.triu(jnp.ones((tok, tok), jnp.bfloat16), 1)
    rank = jnp.dot(
        mask_mine.reshape(mine_experts * sources, tok).astype(jnp.bfloat16),
        before,
        preferred_element_type=jnp.float32,
    ).astype(jnp.int32)
    pos = jnp.where(mask_mine, rank.reshape(mine_experts, sources * tok), -1)
    pos = pos.reshape(mine_experts, 1, sources * tok)
    per_row = width // tok
    mixed_ids = ids.reshape(-1, per_row).T.reshape(-1)
    mask_own = route_mask(routes.T, mixed_ids).astype(jnp.int32)
    router_t = router.T
    router_mixed = router_t.reshape(-1, per_row, width).swapaxes(0, 1).reshape(EXPERTS, width)

    hn_list = gather_pair(hn, axes)
    halves = []
    for half in (0, 1):
        at = slice(half * 8 * tok, (half + 1) * 8 * tok)
        logits_t = jnp.concatenate(
            [nt_dot(router_t, h) for h in hn_list[half * 8 : half * 8 + 8]], axis=1
        )
        gate = masked_softmax(logits_t, mask_all[:, at])
        gate = lax.dynamic_slice_in_dim(gate, first_expert, mine_experts, 0)
        halves.append((pos[:, :, at], gate[:, None, :]))
    weights = (w_gate, w_up, w_down)
    out_one, away_one, dhn_one, dhn_away_one, *grads_one = experts(
        me_first, hn_list[:8], go_list[:8], *halves[0], *weights
    )
    low = tok // 2
    pos_two = halves[1][0]
    if split:
        first_one = scatter_first(dhn_one, dhn_away_one, low)
        pos_two, *first_one = lax.optimization_barrier((pos_two, *first_one))
    out_two, away_two, dhn_two, dhn_away_two, *grads_two = experts(
        me_first, hn_list[8:], go_list[8:], pos_two, halves[1][1], *weights, earlier=grads_one
    )
    if split:
        second_one = scatter_second(*first_one, low)
        first_two = scatter_first(dhn_two, dhn_away_two, low)
        dhn_parts = scatter_third(*second_one)
        dhn_other = part_sum(scatter_third(*scatter_second(*first_two, low)), low)
        dhn_parts = dhn_parts + [swap(dhn_other, "row", 1)]
    else:
        dhn_terms = jnp.concatenate([dhn_one, dhn_away_one, dhn_two, dhn_away_two], axis=0)
        dhn_parts = [lax.psum_scatter(dhn_terms, axes, scatter_dimension=0, tiled=False)]
    dh, dattn, *do_mine, small = second_norm_back(
        hidden, hn, d_output, router_mixed, mask_own, norm2_gain[None, :], wo_list, dhn_parts, low
    )

    do_list = exchange_col(do_mine)
    if split:
        out_firsts = [scatter_first(out_one, away_one, low), scatter_first(out_two, away_two, low)]
        do_list, out_firsts = lax.optimization_barrier((do_list, out_firsts))
    dattn_list = gather_col(after(dattn, do_list[2]))
    dq, dbefore, dkv = attend_back(
        me, q4, kv_before, kv, start, lse, do_list, cos_table, sin_table, tok
    )
    dafter = lax.ppermute(dbefore, "row", [(i + 1, i) for i in range(row_count - 1)])
    wo_parts = wo_grad(me, heads, dattn_list, row_count)
    dq, wo_parts = lax.optimization_barrier((dq, wo_parts))
    if split:
        out_seconds = [scatter_second(*f, low) for f in out_firsts]
        dq, out_seconds = lax.optimization_barrier((dq, out_seconds))
        out_other = part_sum(scatter_third(*out_seconds[1]), low)
        out_parts = scatter_third(*out_seconds[0]) + [swap(out_other, "row", 1)]
    dqkv, dx_keep, dx_away = project_back(me, dq, dkv, dafter, cos_table, sin_table, w_joined, tok)
    dx_came = swap(dx_away, "col", 1)
    qkv_parts = qkv_grad(me, xn1, dqkv, row_count)
    dx_far = (dx_keep[1].astype(jnp.float32) + dx_came[1].astype(jnp.float32)).astype(jnp.bfloat16)
    dx_far = swap(dx_far, "col", 2)
    d_inputs, gain_one = first_norm_back(
        inputs, dh, norm1_gain[None, :], dx_keep, dx_came, dx_far
    )
    if split:
        output = layer_output(hidden, out_parts, low)
    else:
        out_terms = jnp.concatenate([out_one, away_one, out_two, away_two], axis=0)
        out_sum = lax.psum_scatter(out_terms, axes, scatter_dimension=0, tiled=False)
        output = (hidden + out_sum.astype(jnp.float32)).astype(jnp.bfloat16)
    d_w_output = sum_over_low(scatter_row(wo_parts).astype(jnp.bfloat16), "dp")
    d_w_qkv = sum_over_low(scatter_row(qkv_parts).astype(jnp.bfloat16), "dp")

    keep, send = grads_two
    if split:
        lists = []
        for e in range(mine_experts):
            came = swap(send[e], "row", 2)
            sums = (keep[e].astype(jnp.float32) + came.astype(jnp.float32)).astype(jnp.bfloat16)
            other = swap(sums[1], "row", 1)
            lists.append(
                exchange_col([jnp.stack([sums[0, s], other[s]]) for s in range(col_count)])
            )
        d_w_gate, d_w_up, d_w_down = finish(me_first, lists)
        d_w_down = jnp.swapaxes(d_w_down, 1, 2)
    else:
        order = jnp.arange(4, dtype=jnp.int32)
        back = jnp.concatenate([keep, send], axis=1)
        back = jnp.take(jnp.take(back, order ^ my_row, axis=1), order ^ my_col, axis=2)
        back = jnp.moveaxis(back, 0, 2)
        sums = lax.psum_scatter(
            back.reshape((row_count * col_count,) + back.shape[2:]),
            ("row", "col"),
            scatter_dimension=0,
            tiled=False,
        )
        d_w_gate = sums[:, 0].astype(jnp.float32)
        d_w_up = sums[:, 1].astype(jnp.float32)
        d_w_down = jnp.swapaxes(sums[:, 2], 1, 2).astype(jnp.float32)

    small = small[: EXPERTS + 1]
    gain_one = gain_one[0].reshape(-1, LANES)
    small = after(small, dqkv)
    for axis in ("col", "dp", "row"):
        small = sum_over(small, axis)
        gain_one = sum_over(gain_one, axis)
    d_router = small[:EXPERTS].reshape(per_row, -1, width).swapaxes(0, 1).reshape(EXPERTS, width).T
    return (
        output,
        d_inputs,
        gain_one.reshape(-1),
        d_w_qkv[:, :query_cols],
        d_w_qkv[:, query_cols : query_cols + key_cols],
        d_w_qkv[:, query_cols + key_cols :],
        d_w_output,
        small[EXPERTS],
        d_router,
        d_w_gate,
        d_w_up,
        d_w_down,
    )


def solution(mesh):
    return jax.shard_map(
        on_device,
        mesh=mesh,
        in_specs=(
            P(("dp", "row", "col"), None),
            P("dp", None),
            P(("dp", "row", "col"), None),
            P(),
            P("row", "col"),
            P("row", "col"),
            P("row", "col"),
            P("col", "row"),
            P(),
            P(),
            P("dp", None, None),
            P("dp", None, None),
            P("dp", None, None),
            P(("dp", "row", "col"), None),
        ),
        out_specs=(
            P(("dp", "row", "col"), None),
            P(("dp", "row", "col"), None),
            P(),
            P("row", "col"),
            P("row", "col"),
            P("row", "col"),
            P("col", "row"),
            P(),
            P(),
            P("dp", ("row", "col"), None),
            P("dp", ("row", "col"), None),
            P("dp", None, ("row", "col")),
        ),
        check_vma=False,
    )
```

```python
import functools
import math

import jax
import jax.numpy as jnp
from jax import lax
from jax.experimental import pallas as pl
from jax.experimental.pallas import tpu as pltpu
from jax.sharding import PartitionSpec as P

HEAD_SIZE = 64
EXPERTS = 32
TOPK = 8
MAX_LEN = 1024
CAP = 96

EPSILON = 1e-06
MASKED_SCORE = -1e30
ROPE_BASE = 10000.0
LANES = 128
MIB = 1024 * 1024


def nt_dot(left, right):
    return lax.dot_general(
        left, right, (((1,), (1,)), ((), ())), preferred_element_type=jnp.float32
    )


def tn_dot(left, right):
    return lax.dot_general(
        left, right, (((0,), (0,)), ((), ())), preferred_element_type=jnp.float32
    )


def nn_dot(left, right):
    return jnp.dot(left, right, preferred_element_type=jnp.float32)


def swap(value, axis, step):
    return lax.ppermute(value, axis, [(i, i ^ step) for i in range(lax.axis_size(axis))])


def after(value, *others):
    return lax.optimization_barrier((value,) + others)[0]


def gather_col(value):
    far = swap(value, "col", 2)
    near = swap(value, "col", 1)
    return [value, near, far, swap(far, "col", 1)]


def exchange_col(blocks):
    return [blocks[0]] + [swap(blocks[s], "col", s) for s in (1, 2, 3)]


def shift_row(value, step):
    size = lax.axis_size("row")
    return lax.ppermute(value, "row", [(i, (i + step) % size) for i in range(size)])


def gather_row(value):
    return [value] + [shift_row(value, s) for s in range(1, lax.axis_size("row"))]


def scatter_row(blocks, late):
    total = after(blocks[0], late).astype(jnp.float32)
    for step in range(1, len(blocks)):
        total = total + shift_row(blocks[step], step).astype(jnp.float32)
    return total


def sum_over(value, axis):
    size = lax.axis_size(axis)
    if size & (size - 1):
        return lax.psum(value, axis)
    if size == 4:
        near, far, cross = [swap(value, axis, step) for step in (1, 2, 3)]
        return (value + near) + (far + cross)
    step = 1
    while step < size:
        value = value + swap(value, axis, step)
        step *= 2
    return value


def sum_over_low(value, axis):
    if lax.axis_size(axis) == 2:
        return value.astype(jnp.float32) + swap(value, axis, 1).astype(jnp.float32)
    return lax.psum(value, axis).astype(jnp.float32)


def two_way(axes):
    return axes == ("dp", "col") and lax.axis_size("dp") == 2


def gather_tokens(value, axes):
    if not two_way(axes):
        every = lax.all_gather(value, axes)
        return [every[s] for s in range(every.shape[0])]
    half = value.shape[0] // 32 * 16
    along_x = swap(value, "dp", 1)
    along_y = swap(value, "col", 2)
    near = swap(value, "col", 1)
    cross_low = swap(along_x[:half], "col", 2)
    cross_high = swap(along_y[half:], "dp", 1)
    near_x = swap(along_x, "col", 1)
    near_y = swap(along_y, "col", 1)
    cross = jnp.concatenate([cross_low, cross_high], axis=0)
    near_cross = swap(cross, "col", 1)
    return [value, along_y, along_x, cross, near, near_y, near_x, near_cross]


def add_first_kernel(keep_ref, came_ref, x_ref, y_ref, *, low):
    def total(spot, rows):
        return (
            keep_ref[spot, rows].astype(jnp.float32) + came_ref[spot, rows].astype(jnp.float32)
        ).astype(jnp.bfloat16)

    x_ref[0], x_ref[1] = total(2, slice(0, low)), total(3, slice(0, low))
    y_ref[0], y_ref[1] = total(1, slice(low, None)), total(3, slice(low, None))


def add_second_kernel(keep_ref, came_ref, x_ref, y_ref, low_ref, high_ref, *, low):
    def total(spot, rows, extra):
        return (
            keep_ref[spot, rows].astype(jnp.float32)
            + came_ref[spot, rows].astype(jnp.float32)
            + extra.astype(jnp.float32)
        ).astype(jnp.bfloat16)

    low_ref[...] = total(1, slice(0, low), x_ref[1])
    high_ref[...] = total(2, slice(low, None), y_ref[1])


def scatter_tokens(keep, away, low):
    rows, width = keep.shape[1:]
    high = rows - low
    came = swap(away, "col", 1)
    params = pltpu.CompilerParams(vmem_limit_bytes=60 * MIB)
    send_x, send_y = pl.pallas_call(
        functools.partial(add_first_kernel, low=low),
        out_shape=[
            jax.ShapeDtypeStruct((2, low, width), jnp.bfloat16),
            jax.ShapeDtypeStruct((2, high, width), jnp.bfloat16),
        ],
        compiler_params=params,
        name="add_first",
    )(keep, came)
    by_x, by_y = swap(send_x, "dp", 1), swap(send_y, "col", 2)
    last_low, last_high = pl.pallas_call(
        functools.partial(add_second_kernel, low=low),
        out_shape=[
            jax.ShapeDtypeStruct((low, width), jnp.bfloat16),
            jax.ShapeDtypeStruct((high, width), jnp.bfloat16),
        ],
        compiler_params=params,
        name="add_second",
    )(keep, came, by_x, by_y)
    return [keep, came, by_x, by_y, swap(last_low, "col", 2), swap(last_high, "dp", 1)]


def part_specs(parts):
    specs = []
    for part in parts:
        if part.ndim == 3:
            specs.append(pl.BlockSpec((1,) + part.shape[1:], lambda i: (0, 0, 0)))
        else:
            specs.append(pl.BlockSpec(part.shape, lambda i: (0, 0)))
    return specs


def swap_halves(value):
    lane = lax.broadcasted_iota(jnp.int32, value.shape, 1)
    first = (lane % HEAD_SIZE) < HEAD_SIZE // 2
    half = HEAD_SIZE // 2
    return jnp.where(first, pltpu.roll(value, LANES - half, 1), pltpu.roll(value, half, 1))


def turn(value, cos_part, sin_part):
    return value * cos_part + swap_halves(value) * sin_part


def spread_heads(pairs):
    lane = lax.broadcasted_iota(jnp.int32, pairs[0].shape, 1)
    low_lane = lane < HEAD_SIZE
    return [
        jnp.where(low_lane, pairs[0], 0.0),
        jnp.where(low_lane, pltpu.roll(pairs[0], HEAD_SIZE, 1), 0.0),
        jnp.where(low_lane, 0.0, pltpu.roll(pairs[1], HEAD_SIZE, 1)),
        jnp.where(low_lane, 0.0, pairs[1]),
    ]


def join_heads(heads):
    lane = lax.broadcasted_iota(jnp.int32, heads[0].shape, 1)
    low_lane = lane < HEAD_SIZE
    return [
        jnp.where(low_lane, heads[0], pltpu.roll(heads[1], HEAD_SIZE, 1)),
        jnp.where(low_lane, pltpu.roll(heads[2], HEAD_SIZE, 1), heads[3]),
    ]


SMEM_SPEC = pl.BlockSpec(memory_space=pltpu.SMEM)
VMEM_SPEC = pl.BlockSpec(memory_space=pltpu.VMEM)


def place_rows(index, block):
    return pl.ds(pl.multiple_of(index * block, block), block)


def project_kernel(*refs, rows, block):
    me_ref, gain_ref, cos_ref, sin_ref = refs[:4]
    x_refs, w_refs = refs[4:8], refs[8 : 8 + rows]
    xn_ref, q_ref, kv_ref, w_ref = refs[8 + rows :]
    my_col, my_row = me_ref[0], me_ref[1]
    part = w_refs[0].shape[0]
    for s in range(rows):
        w_ref[place_rows(lax.rem(my_row - s + rows, rows), part), :] = w_refs[s][...]
    w_joined = w_ref[...]
    scale = 1.0 / math.sqrt(HEAD_SIZE)
    for s in range(4):
        at = place_rows(my_col ^ s, block)
        x = x_refs[s][...].astype(jnp.float32)
        rinv = lax.rsqrt(jnp.mean(x * x, axis=1, keepdims=True) + EPSILON)
        xn = (x * rinv * gain_ref[...]).astype(jnp.bfloat16)
        xn_ref[at, :] = xn
        joined = nn_dot(xn, w_joined)
        cos_part, sin_part = cos_ref[at, :], sin_ref[at, :]
        pairs = [
            turn(joined[:, i * LANES : (i + 1) * LANES], cos_part, sin_part) * scale
            for i in range(2)
        ]
        for h, head in enumerate(spread_heads(pairs)):
            q_ref[h, at, :] = head.astype(jnp.bfloat16)
        kv_ref[at, :LANES] = turn(joined[:, 2 * LANES : 3 * LANES], cos_part, sin_part).astype(
            jnp.bfloat16
        )
        kv_ref[at, LANES:] = joined[:, 3 * LANES :].astype(jnp.bfloat16)


def project(me, gain, cos_table, sin_table, x_list, w_list):
    block, width = x_list[0].shape
    rows = len(w_list)
    plane = 4 * block
    return pl.pallas_call(
        functools.partial(project_kernel, rows=rows, block=block),
        in_specs=[SMEM_SPEC] + [VMEM_SPEC] * (7 + rows),
        out_specs=[VMEM_SPEC] * 4,
        out_shape=[
            jax.ShapeDtypeStruct((plane, width), jnp.bfloat16),
            jax.ShapeDtypeStruct((4, plane, LANES), jnp.bfloat16),
            jax.ShapeDtypeStruct((plane, 2 * LANES), jnp.bfloat16),
            jax.ShapeDtypeStruct((width, 4 * LANES), jnp.bfloat16),
        ],
        compiler_params=pltpu.CompilerParams(vmem_limit_bytes=60 * MIB),
        name="project",
    )(me, gain, cos_table, sin_table, *x_list, *w_list)


def project_back_kernel(
    me_ref, dq_ref, own_ref, came_ref, cos_ref, sin_ref, w_ref, dqkv_ref, keep_ref, away_ref, *, block
):
    my_col = me_ref[0]
    for s in (1, 3, 0, 2):
        at = place_rows(my_col ^ s, block)
        total = own_ref[at, :] + came_ref[at, :].astype(jnp.float32)
        dk = turn(total[:, :LANES], cos_ref[at, :], -sin_ref[at, :]).astype(jnp.bfloat16)
        dqkv = jnp.concatenate([dq_ref[at, :], dk, total[:, LANES:].astype(jnp.bfloat16)], axis=1)
        dqkv_ref[at, :] = dqkv
        target = away_ref if s % 2 else keep_ref
        target[s // 2] = nt_dot(dqkv, w_ref[...]).astype(jnp.bfloat16)


def project_back(me, dq, own, came, cos_table, sin_table, w_joined, block):
    width = w_joined.shape[0]
    return pl.pallas_call(
        functools.partial(project_back_kernel, block=block),
        in_specs=[SMEM_SPEC] + [VMEM_SPEC] * 6,
        out_specs=[VMEM_SPEC] * 3,
        out_shape=[
            jax.ShapeDtypeStruct((dq.shape[0], 4 * LANES), jnp.bfloat16),
            jax.ShapeDtypeStruct((2, block, width), jnp.bfloat16),
            jax.ShapeDtypeStruct((2, block, width), jnp.bfloat16),
        ],
        compiler_params=pltpu.CompilerParams(vmem_limit_bytes=60 * MIB),
        name="project_back",
    )(me, dq, own, came, cos_table, sin_table, w_joined)


def weight_grad_kernel(me_ref, xn_ref, dqkv_ref, *refs, rows, dps):
    heads, dattn = refs[:4], refs[4:8]
    send_ref, keep_ref, scratch, scratch_out = refs[8:]
    scratch[...] = tn_dot(xn_ref[...], dqkv_ref[...])
    total = None
    for s in range(4):
        term = tn_dot(heads[s][...], dattn[s][...])
        total = term if total is None else total + term
    scratch_out[...] = total
    part = keep_ref.shape[2]
    tall, half = scratch.shape[0] // rows, scratch_out.shape[0] // dps
    for s in range(rows):
        row = lax.rem(me_ref[1] + s, rows)
        for d, ref in enumerate((keep_ref, send_ref)[:dps]):
            mine = me_ref[2] ^ d
            ref[s, :tall] = scratch[place_rows(row, tall), place_rows(mine, part)].astype(
                jnp.bfloat16
            )
            ref[s, tall:] = scratch_out[place_rows(mine, half), place_rows(row, part)].astype(
                jnp.bfloat16
            )


def weight_grad(me, xn, dqkv, heads, dattn, rows):
    width, cols = xn.shape[1], dqkv.shape[1]
    out_rows = heads[0].shape[1]
    shape = (rows, width // rows + out_rows // 2, cols // 2)
    return pl.pallas_call(
        functools.partial(weight_grad_kernel, rows=rows, dps=2),
        in_specs=[SMEM_SPEC] + [VMEM_SPEC] * 10,
        out_specs=[VMEM_SPEC] * 2,
        out_shape=[jax.ShapeDtypeStruct(shape, jnp.bfloat16)] * 2,
        scratch_shapes=[
            pltpu.VMEM((width, cols), jnp.float32),
            pltpu.VMEM((out_rows, width), jnp.float32),
        ],
        compiler_params=pltpu.CompilerParams(vmem_limit_bytes=60 * MIB),
        name="weight_grad",
    )(me, xn, dqkv, *heads, *dattn)


def window_bias(start, first_key, window, block, plane):
    key_at = first_key + lax.broadcasted_iota(jnp.int32, (window, block), 0)
    query_at = first_key + plane + lax.broadcasted_iota(jnp.int32, (window, block), 1)
    allowed = (key_at >= start) & (key_at <= query_at)
    return jnp.where(allowed, 0.0, MASKED_SCORE)


def attend_kernel(
    me_ref, q_ref, before_ref, kv_ref, start_ref, o0, o1, o2, o3, lse_ref, kv_all, *, plane, block
):
    window = plane + block
    step = pl.program_id(0)

    @pl.when(step == 0)
    def _():
        kv_all[:plane] = before_ref[...]
        kv_all[plane:] = kv_ref[...]

    first_key = pl.multiple_of((me_ref[0] ^ step) * block, block)
    keys = kv_all[pl.ds(first_key, window), :LANES]
    values = kv_all[pl.ds(first_key, window), LANES:]
    values_t = values.astype(jnp.float32).T.astype(jnp.bfloat16)
    bias = window_bias(start_ref[...], first_key, window, block, plane)
    heads = []
    for h in range(4):
        scores = nt_dot(keys, q_ref[h]) + bias
        top = jnp.max(scores, axis=0, keepdims=True)
        weights = jnp.exp(scores - top)
        total = jnp.sum(weights, axis=0, keepdims=True)
        mixed = nn_dot(values_t, weights.astype(jnp.bfloat16)) / total
        lse_ref[h : h + 1, :] = top + jnp.log(total)
        heads.append(mixed.T)
    pairs = jnp.concatenate([p.astype(jnp.bfloat16) for p in join_heads(heads)], axis=1)
    for s, o_ref in enumerate((o0, o1, o2, o3)):

        @pl.when(step == s)
        def _(o_ref=o_ref):
            o_ref[...] = pairs


def attend(me, q4, before, kv, start, block):
    plane = q4.shape[1]
    whole = pl.BlockSpec((plane, 2 * LANES), lambda i, m: (0, 0))
    return pl.pallas_call(
        functools.partial(attend_kernel, plane=plane, block=block),
        grid_spec=pltpu.PrefetchScalarGridSpec(
            num_scalar_prefetch=1,
            grid=(4,),
            in_specs=[
                pl.BlockSpec((4, block, LANES), lambda i, m: (0, m[0] ^ i, 0)),
                whole,
                whole,
                pl.BlockSpec((1, block), lambda i, m: (0, m[0] ^ i)),
            ],
            out_specs=[pl.BlockSpec((block, 2 * LANES), lambda i, m: (0, 0))] * 4
            + [pl.BlockSpec((4, block), lambda i, m: (0, m[0] ^ i))],
            scratch_shapes=[pltpu.VMEM((2 * plane, 2 * LANES), jnp.bfloat16)],
        ),
        out_shape=[jax.ShapeDtypeStruct((block, 2 * LANES), jnp.bfloat16)] * 4
        + [jax.ShapeDtypeStruct((4, plane), jnp.float32)],
        compiler_params=pltpu.CompilerParams(vmem_limit_bytes=60 * MIB),
        name="attend",
    )(me, q4, before, kv, start)


def attend_back_kernel(
    me_ref,
    q_ref,
    before_ref,
    kv_ref,
    start_ref,
    lse_ref,
    do0,
    do1,
    do2,
    do3,
    cos_ref,
    sin_ref,
    dq_ref,
    dbefore_ref,
    dkv_ref,
    kv_all,
    sums,
    do_now,
    *,
    plane,
    block,
):
    window = plane + block
    step = pl.program_id(0)

    @pl.when(step == 0)
    def _():
        kv_all[:plane] = before_ref[...]
        kv_all[plane:] = kv_ref[...]
        sums[...] = jnp.zeros_like(sums)

    for s, do_ref in enumerate((do0, do1, do2, do3)):

        @pl.when(step == s)
        def _(do_ref=do_ref):
            do_now[...] = do_ref[...]

    first_key = pl.multiple_of((me_ref[0] ^ step) * block, block)
    keys = kv_all[pl.ds(first_key, window), :LANES]
    values = kv_all[pl.ds(first_key, window), LANES:]
    keys_t = keys.astype(jnp.float32).T.astype(jnp.bfloat16)
    bias = window_bias(start_ref[...], first_key, window, block, plane)
    grad = do_now[...].astype(jnp.float32)
    grads = [g.astype(jnp.bfloat16) for g in spread_heads([grad[:, :LANES], grad[:, LANES:]])]
    heads = []
    dk_total, dv_total = None, None
    for h in range(4):
        q = q_ref[h]
        weights = jnp.exp(nt_dot(keys, q) + bias - lse_ref[h : h + 1, :])
        dv = nn_dot(weights.astype(jnp.bfloat16), grads[h])
        product = weights * nt_dot(values, grads[h])
        centre = jnp.sum(product, axis=0, keepdims=True)
        ds = (product - weights * centre).astype(jnp.bfloat16)
        dk = nn_dot(ds, q)
        heads.append(nn_dot(keys_t, ds).T)
        dk_total = dk if dk_total is None else dk_total + dk
        dv_total = dv if dv_total is None else dv_total + dv
    sums[pl.ds(first_key, window), :LANES] += dk_total
    sums[pl.ds(first_key, window), LANES:] += dv_total
    scale = 1.0 / math.sqrt(HEAD_SIZE)
    for i, pair in enumerate(join_heads(heads)):
        dq_ref[:, i * LANES : (i + 1) * LANES] = turn(
            pair * scale, cos_ref[...], -sin_ref[...]
        ).astype(jnp.bfloat16)

    @pl.when(step == 3)
    def _():
        dbefore_ref[...] = sums[:plane].astype(jnp.bfloat16)
        dkv_ref[...] = sums[plane:]


def attend_back(me, q4, before, kv, start, lse, do_list, cos_table, sin_table, block):
    plane = q4.shape[1]
    whole = pl.BlockSpec((plane, 2 * LANES), lambda i, m: (0, 0))
    small = pl.BlockSpec((block, 2 * LANES), lambda i, m: (0, 0))
    table = pl.BlockSpec((block, LANES), lambda i, m: (m[0] ^ i, 0))
    return pl.pallas_call(
        functools.partial(attend_back_kernel, plane=plane, block=block),
        grid_spec=pltpu.PrefetchScalarGridSpec(
            num_scalar_prefetch=1,
            grid=(4,),
            in_specs=[
                pl.BlockSpec((4, block, LANES), lambda i, m: (0, m[0] ^ i, 0)),
                whole,
                whole,
                pl.BlockSpec((1, block), lambda i, m: (0, m[0] ^ i)),
                pl.BlockSpec((4, block), lambda i, m: (0, m[0] ^ i)),
            ]
            + [small] * 4
            + [table, table],
            out_specs=[
                pl.BlockSpec((block, 2 * LANES), lambda i, m: (m[0] ^ i, 0)),
                whole,
                whole,
            ],
            scratch_shapes=[
                pltpu.VMEM((2 * plane, 2 * LANES), jnp.bfloat16),
                pltpu.VMEM((2 * plane, 2 * LANES), jnp.float32),
                pltpu.VMEM((block, 2 * LANES), jnp.bfloat16),
            ],
        ),
        out_shape=[
            jax.ShapeDtypeStruct((plane, 2 * LANES), jnp.bfloat16),
            jax.ShapeDtypeStruct((plane, 2 * LANES), jnp.bfloat16),
            jax.ShapeDtypeStruct((plane, 2 * LANES), jnp.float32),
        ],
        compiler_params=pltpu.CompilerParams(vmem_limit_bytes=60 * MIB),
        name="attend_back",
    )(me, q4, before, kv, start, lse, *do_list, cos_table, sin_table)


def hidden_kernel(x_ref, gain_ref, o0, o1, o2, o3, w0, w1, w2, w3, hidden_ref, hn_ref):
    hidden = x_ref[...].astype(jnp.float32)
    for o_ref, w_ref in ((o0, w0), (o1, w1), (o2, w2), (o3, w3)):
        hidden = hidden + nn_dot(o_ref[...], w_ref[...])
    hidden_ref[...] = hidden
    rinv = lax.rsqrt(jnp.mean(hidden * hidden, axis=1, keepdims=True) + EPSILON)
    hn_ref[...] = (hidden * rinv * gain_ref[...]).astype(jnp.bfloat16)


def second_norm(x, gain, o_list, wo_list):
    return pl.pallas_call(
        hidden_kernel,
        out_shape=[
            jax.ShapeDtypeStruct(x.shape, jnp.float32),
            jax.ShapeDtypeStruct(x.shape, jnp.bfloat16),
        ],
        compiler_params=pltpu.CompilerParams(vmem_limit_bytes=60 * MIB),
        name="second_norm",
    )(x, gain, *o_list, *wo_list)


def masked_softmax(logits, mask):
    shown = jnp.where(mask, logits, MASKED_SCORE)
    top = jnp.max(shown, axis=0, keepdims=True)
    raised = jnp.where(mask, jnp.exp(shown - top), 0.0)
    return raised / jnp.sum(raised, axis=0, keepdims=True)


def second_norm_back_kernel(*refs, low, tok, parts):
    hidden_ref, hn_ref, go_ref, router_ref, mask_ref, gain_ref = refs[:6]
    wo_refs = refs[6:10]
    part_refs = refs[10 : 10 + parts]
    dh_ref, dattn_ref, do0, do1, do2, do3, small_ref = refs[10 + parts :]
    total = part_refs[0][:low, :] if parts == 1 else part_refs[0][0, :low]
    total = total.astype(jnp.float32)
    if parts > 1:
        total = total + part_refs[1][0, :low].astype(jnp.float32)
        total = total + part_refs[2][0].astype(jnp.float32)
        total = total + part_refs[3][...].astype(jnp.float32)
    width = hidden_ref.shape[1]
    group = EXPERTS * tok // width
    spare = total[tok : tok + group] + total[tok + group :]
    dgate = jnp.concatenate(
        [spare[:, b * tok : (b + 1) * tok] for b in range(width // tok)], axis=0
    )
    hn = hn_ref[...]
    router = router_ref[...]
    gate = masked_softmax(nt_dot(router, hn), mask_ref[...] > 0)
    dlogits = gate * (dgate - jnp.sum(gate * dgate, axis=0, keepdims=True))
    dlogits = dlogits.astype(jnp.bfloat16)
    dhn = total[:tok] + tn_dot(dlogits, router)
    small_ref[:EXPERTS, :] = nn_dot(dlogits, hn)
    hidden = hidden_ref[...]
    rinv = lax.rsqrt(jnp.mean(hidden * hidden, axis=1, keepdims=True) + EPSILON)
    unit = hidden * rinv
    small_ref[EXPERTS:, :] = jnp.broadcast_to(
        jnp.sum(dhn * unit, axis=0, keepdims=True), (8, width)
    )
    scaled = dhn * gain_ref[...]
    dh = go_ref[...].astype(jnp.float32) + rinv * (
        scaled - unit * jnp.mean(scaled * unit, axis=1, keepdims=True)
    )
    dh_ref[...] = dh
    dattn = dh.astype(jnp.bfloat16)
    dattn_ref[...] = dattn
    for w_ref, do_ref in zip(wo_refs, (do0, do1, do2, do3)):
        do_ref[...] = nt_dot(dattn, w_ref[...]).astype(jnp.bfloat16)


def second_norm_back(hidden, hn, go, router, mask, gain, wo_list, parts, low):
    tok, width = hidden.shape
    specs = [
        pl.BlockSpec(a.shape, functools.partial(lambda n, i: (0,) * n, a.ndim))
        for a in (hidden, hn, go, router, mask, gain, *wo_list)
    ]
    specs += part_specs(parts)
    cols = wo_list[0].shape[0]
    shapes = [
        jax.ShapeDtypeStruct((tok, width), jnp.float32),
        jax.ShapeDtypeStruct((tok, width), jnp.bfloat16),
    ]
    shapes += [jax.ShapeDtypeStruct((tok, cols), jnp.bfloat16)] * 4
    shapes += [jax.ShapeDtypeStruct((EXPERTS + 8, width), jnp.float32)]
    return pl.pallas_call(
        functools.partial(second_norm_back_kernel, low=low, tok=tok, parts=len(parts)),
        grid=(1,),
        in_specs=specs,
        out_specs=[pl.BlockSpec(s.shape, lambda i: (0, 0)) for s in shapes],
        out_shape=shapes,
        compiler_params=pltpu.CompilerParams(vmem_limit_bytes=60 * MIB),
        name="second_norm_back",
    )(hidden, hn, go, router, mask, gain, *wo_list, *parts)


def first_norm_back_kernel(x_ref, dh_ref, gain_ref, keep_ref, came_ref, far_ref, dx_ref, part_ref):
    x = x_ref[...].astype(jnp.float32)
    rinv = lax.rsqrt(jnp.mean(x * x, axis=1, keepdims=True) + EPSILON)
    unit = x * rinv
    dxn = keep_ref[0].astype(jnp.float32) + came_ref[0].astype(jnp.float32)
    dxn = dxn + far_ref[...].astype(jnp.float32)
    part_ref[...] = jnp.broadcast_to(jnp.sum(dxn * unit, axis=0, keepdims=True), part_ref.shape)
    scaled = dxn * gain_ref[...]
    dx_ref[...] = dh_ref[...] + rinv * (
        scaled - unit * jnp.mean(scaled * unit, axis=1, keepdims=True)
    )


def first_norm_back(x, dh, gain, keep, came, far):
    tok, width = x.shape
    flat = pl.BlockSpec((tok, width), lambda i: (0, 0))
    first = pl.BlockSpec((1, tok, width), lambda i: (0, 0, 0))
    return pl.pallas_call(
        first_norm_back_kernel,
        grid=(1,),
        in_specs=[flat, flat, pl.BlockSpec((1, width), lambda i: (0, 0)), first, first, flat],
        out_specs=[flat, pl.BlockSpec((8, width), lambda i: (0, 0))],
        out_shape=[
            jax.ShapeDtypeStruct((tok, width), jnp.float32),
            jax.ShapeDtypeStruct((8, width), jnp.float32),
        ],
        compiler_params=pltpu.CompilerParams(vmem_limit_bytes=60 * MIB),
        name="first_norm_back",
    )(x, dh, gain, keep, came, far)


def output_kernel(hidden_ref, keep_ref, came_ref, by_ref, last_ref, out_ref, *, low):
    total = hidden_ref[...] + keep_ref[0, low:].astype(jnp.float32)
    total = total + came_ref[0, low:].astype(jnp.float32)
    total = total + by_ref[0].astype(jnp.float32) + last_ref[...].astype(jnp.float32)
    out_ref[...] = total.astype(jnp.bfloat16)


def layer_output(hidden, parts, low):
    whole = pl.BlockSpec(hidden.shape, lambda i: (0, 0))
    return pl.pallas_call(
        functools.partial(output_kernel, low=low),
        grid=(1,),
        in_specs=[whole] + part_specs(parts),
        out_specs=whole,
        out_shape=jax.ShapeDtypeStruct(hidden.shape, jnp.bfloat16),
        compiler_params=pltpu.CompilerParams(vmem_limit_bytes=60 * MIB),
        name="layer_output",
    )(hidden, *parts)


def expert_kernel(me_ref, *refs, total, chunk, tok, rows, cols):
    hn_refs, go_refs = refs[:total], refs[total : 2 * total]
    pos_ref, gate_ref, wg_ref, wu_ref, wd_ref = refs[2 * total : 2 * total + 5]
    y_ref, dx_ref, dgate_ref, grad_ref = refs[2 * total + 5 : 2 * total + 9]
    x_all, go_rows, slot_gate, sums = refs[2 * total + 9 :]
    for begin in range(0, total, chunk):
        for s in range(chunk):
            at = slice((begin + s) * tok, (begin + s + 1) * tok)
            spot = lax.broadcasted_iota(jnp.int32, (CAP, tok), 0)
            hot = spot == pos_ref[0, :, at]
            hot_low = hot.astype(jnp.bfloat16)
            mine = slice(s * CAP, (s + 1) * CAP)
            x_all[mine, :] = nn_dot(hot_low, hn_refs[begin + s][...]).astype(jnp.bfloat16)
            go_rows[mine, :] = nn_dot(hot_low, go_refs[begin + s][:tok, :]).astype(jnp.bfloat16)
            slot_gate[mine, :] = jnp.sum(
                jnp.where(hot, gate_ref[0, :, at], 0.0), axis=1, keepdims=True
            )
        x = x_all[...]
        go = go_rows[...]
        gate = slot_gate[...]
        a = nn_dot(x, wg_ref[0])
        b = nn_dot(x, wu_ref[0])
        dz = nt_dot(go, wd_ref[0])
        sig = 1.0 / (1.0 + jnp.exp(-a))
        silu = a * sig
        z = silu * b
        z_low = z.astype(jnp.bfloat16)
        dgate = jnp.sum(z_low.astype(jnp.float32) * dz, axis=1, keepdims=True)
        dz = dz * gate
        da = (dz * b * sig * (1.0 + a * (1.0 - sig))).astype(jnp.bfloat16)
        db = (dz * silu).astype(jnp.bfloat16)
        gz = (z * gate).astype(jnp.bfloat16)
        y = (nn_dot(z_low, wd_ref[0]) * gate).astype(jnp.bfloat16)
        dx = (nt_dot(da, wg_ref[0]) + nt_dot(db, wu_ref[0])).astype(jnp.bfloat16)
        for s in range(chunk):
            at = slice((begin + s) * tok, (begin + s + 1) * tok)
            mine = slice(s * CAP, (s + 1) * CAP)
            y_ref[begin + s, 0] = y[mine]
            dx_ref[begin + s, 0] = dx[mine]
            spot = lax.broadcasted_iota(jnp.int32, (CAP, tok), 0)
            hot = spot == pos_ref[0, :, at]
            dgate_ref[0, :, at] = jnp.sum(
                jnp.where(hot, dgate[mine], 0.0), axis=0, keepdims=True
            )
        for i, (left, right) in enumerate(((x, da), (x, db), (go, gz))):
            term = tn_dot(left, right).reshape(sums.shape[1:])
            if begin:
                sums[i] += term
            else:
                sums[i] = term
    for s in range(cols):
        grad_ref[:, s, 0] = jnp.swapaxes(sums[:, :, me_ref[1] ^ s], 0, 1).astype(jnp.bfloat16)


def experts(me, hn_list, go_list, pos, gate, w_gate, w_up, w_down, rows, cols, first, count):
    total = len(hn_list)
    tok, width = hn_list[0].shape
    hidden = w_gate.shape[2]
    chunk = 8 if total % 8 == 0 else total
    part = width // (rows * cols)
    slots = chunk * CAP

    def weight(shape):
        return pl.BlockSpec((1,) + shape, lambda e, m: (m[0] + first + e, 0, 0))

    token = pl.BlockSpec((tok, width), lambda e, m: (0, 0), pipeline_mode=pl.Buffered(1))
    grad_token = pl.BlockSpec(go_list[0].shape, lambda e, m: (0, 0), pipeline_mode=pl.Buffered(1))
    line = pl.BlockSpec((1, 1, total * tok), lambda e, m: (first + e, 0, 0))
    slot = pl.BlockSpec((total, 1, CAP, width), lambda e, m: (0, e, 0, 0))
    return pl.pallas_call(
        functools.partial(
            expert_kernel, total=total, chunk=chunk, tok=tok, rows=rows, cols=cols
        ),
        grid_spec=pltpu.PrefetchScalarGridSpec(
            num_scalar_prefetch=1,
            grid=(count,),
            in_specs=[token] * total
            + [grad_token] * total
            + [line, line, weight((width, hidden)), weight((width, hidden)), weight((hidden, width))],
            out_specs=[
                slot,
                slot,
                pl.BlockSpec((1, 1, total * tok), lambda e, m: (e, 0, 0)),
                pl.BlockSpec(
                    (rows, cols, 1, 3, part, hidden), lambda e, m: (0, 0, e, 0, 0, 0)
                ),
            ],
            scratch_shapes=[
                pltpu.VMEM((slots, width), jnp.bfloat16),
                pltpu.VMEM((slots, width), jnp.bfloat16),
                pltpu.VMEM((slots, 1), jnp.float32),
                pltpu.VMEM((3, rows, cols, part, hidden), jnp.float32),
            ],
        ),
        out_shape=[
            jax.ShapeDtypeStruct((total, count, CAP, width), jnp.bfloat16),
            jax.ShapeDtypeStruct((total, count, CAP, width), jnp.bfloat16),
            jax.ShapeDtypeStruct((count, 1, total * tok), jnp.float32),
            jax.ShapeDtypeStruct((rows, cols, count, 3, part, hidden), jnp.bfloat16),
        ],
        compiler_params=pltpu.CompilerParams(vmem_limit_bytes=62 * MIB),
        name="experts",
    )(me, *hn_list, *go_list, pos, gate, w_gate, w_up, w_down)


def combine_kernel(me_ref, pos_ref, *refs, calls, count, tok, half, extra):
    y_refs, dx_refs, dgate_refs = refs[:calls], refs[calls : 2 * calls], refs[2 * calls : 3 * calls]
    keep_ref, away_ref = refs[3 * calls :]
    width = keep_ref.shape[2]
    low = tok + 2 * extra
    spot = lax.broadcasted_iota(jnp.int32, (CAP, tok), 0)
    hot = jnp.concatenate(
        [(spot == pos_ref[e]).astype(jnp.float32).astype(jnp.bfloat16) for e in range(count)],
        axis=0,
    )

    def rows_of(value_refs):
        return jnp.concatenate([r[0].reshape(-1, width) for r in value_refs], axis=0)

    out = tn_dot(hot, rows_of(y_refs)).astype(jnp.bfloat16)
    dhn = tn_dot(hot, rows_of(dx_refs)).astype(jnp.bfloat16)
    row = lax.broadcasted_iota(jnp.int32, (extra, width), 0)
    lane = lax.broadcasted_iota(jnp.int32, (extra, width), 1)
    per_row = width // tok
    spare = jnp.zeros((extra, width), jnp.float32)
    done = 0
    for dgate_ref in dgate_refs:
        for e in range(dgate_ref.shape[0]):
            expert = me_ref[2] + done
            here = (row == expert // per_row) & (lane // tok == expert % per_row)
            line = jnp.concatenate([dgate_ref[e]] * per_row, axis=1)
            spare = spare + jnp.where(here, line, 0.0)
            done += 1
    spare_high = spare.astype(jnp.bfloat16)
    spare_low = (spare - spare_high.astype(jnp.float32)).astype(jnp.bfloat16)

    def store(ref):
        ref[0, :tok] = dhn
        ref[0, tok:low] = jnp.concatenate([spare_high, spare_low], axis=0)
        ref[0, low:] = out

    @pl.when(pl.program_id(0) < half)
    def _():
        store(keep_ref)

    @pl.when(pl.program_id(0) >= half)
    def _():
        store(away_ref)


def combine(me, pos, y_list, dx_list, dgate_list, tok):
    total, _, _, width = y_list[0].shape
    count = pos.shape[0]
    half = total // 2
    extra = EXPERTS * tok // width
    rows = 2 * tok + 2 * extra
    slots = [
        pl.BlockSpec((1,) + y.shape[1:], lambda s, m: (s, 0, 0, 0)) for y in y_list + dx_list
    ]
    lines = [pl.BlockSpec((d.shape[0], 1, tok), lambda s, m: (0, 0, s)) for d in dgate_list]

    def keep(s, m):
        return (jnp.minimum(s, half - 1), 0, 0)

    def away(s, m):
        return (jnp.maximum(s - half, 0), 0, 0)

    return pl.pallas_call(
        functools.partial(
            combine_kernel, calls=len(y_list), count=count, tok=tok, half=half, extra=extra
        ),
        grid_spec=pltpu.PrefetchScalarGridSpec(
            num_scalar_prefetch=1,
            grid=(total,),
            in_specs=[pl.BlockSpec((count, 1, tok), lambda s, m: (0, 0, s))] + slots + lines,
            out_specs=[
                pl.BlockSpec((1, rows, width), keep),
                pl.BlockSpec((1, rows, width), away),
            ],
        ),
        out_shape=[
            jax.ShapeDtypeStruct((half, rows, width), jnp.bfloat16),
            jax.ShapeDtypeStruct((half, rows, width), jnp.bfloat16),
        ],
        compiler_params=pltpu.CompilerParams(vmem_limit_bytes=60 * MIB),
        name="combine",
    )(me, pos, *y_list, *dx_list, *dgate_list)


def finish_kernel(me_ref, *refs, calls):
    gate_ref, up_ref, down_ref = refs[4 * calls :]
    for s in range(4):

        @pl.when(pl.program_id(0) == s)
        def _(s=s):
            done = 0
            for call in range(calls):
                ref = refs[4 * call + s]
                for e in range(ref.shape[0]):
                    gate_ref[done] = ref[e, 0].astype(jnp.float32)
                    up_ref[done] = ref[e, 1].astype(jnp.float32)
                    down_ref[done] = ref[e, 2].astype(jnp.float32)
                    done += 1


def finish(me, lists):
    calls = len(lists)
    parts = [p for one in lists for p in one]
    mine = sum(one[0].shape[0] for one in lists)
    part, hidden = parts[0].shape[2:]
    whole = [pl.BlockSpec(p.shape, lambda s, m: (0, 0, 0, 0)) for p in parts]
    return pl.pallas_call(
        functools.partial(finish_kernel, calls=calls),
        grid_spec=pltpu.PrefetchScalarGridSpec(
            num_scalar_prefetch=1,
            grid=(4,),
            in_specs=whole,
            out_specs=[
                pl.BlockSpec((mine, part, hidden), lambda s, m: (m[1] ^ s, 0, 0)),
                pl.BlockSpec((mine, part, hidden), lambda s, m: (m[1] ^ s, 0, 0)),
                pl.BlockSpec((mine, part, hidden), lambda s, m: (m[1] ^ s, 0, 0)),
            ],
        ),
        out_shape=[
            jax.ShapeDtypeStruct((4 * mine, part, hidden), jnp.float32),
            jax.ShapeDtypeStruct((4 * mine, part, hidden), jnp.float32),
            jax.ShapeDtypeStruct((4 * mine, part, hidden), jnp.float32),
        ],
        compiler_params=pltpu.CompilerParams(vmem_limit_bytes=60 * MIB),
        name="finish",
    )(me, *parts)


def places(seq_lengths, first_row, total_rows):
    seq_ends = jnp.cumsum(seq_lengths)
    spots = first_row + jnp.arange(total_rows, dtype=jnp.int32)
    passed = (spots[:, None] >= seq_ends[None, :]).astype(jnp.int32)
    starts = jnp.sum(passed * seq_lengths[None, :], axis=1)
    return spots, starts


def route_mask(routes_t, ids):
    return jnp.any(routes_t[None, :, :] == ids[:, None, None], axis=1)


def on_device(
    inputs,
    lengths,
    routes,
    norm1_gain,
    w_query,
    key_weight,
    value_weight,
    w_output,
    norm2_gain,
    router,
    w_gate,
    w_up,
    w_down,
    d_output,
):
    row_count = lax.axis_size("row")
    col_count = lax.axis_size("col")
    dp_count = lax.axis_size("dp")
    my_row, my_col = lax.axis_index("row"), lax.axis_index("col")
    tok, width = inputs.shape
    plane = tok * col_count
    query_cols, key_cols = w_query.shape[1], key_weight.shape[1]
    assert col_count == 4 and plane >= MAX_LEN - 1
    assert query_cols == 2 * LANES and key_cols == LANES
    local_experts = w_gate.shape[0]
    split = local_experts % col_count == 0
    axes = ("dp", "col") if split else ("dp",)
    mine_experts = local_experts // col_count if split else local_experts
    first_local = my_col * mine_experts if split else jnp.int32(0)
    first_expert = lax.axis_index("dp") * local_experts + first_local
    sources = dp_count * (col_count if split else 1)
    ids = jnp.arange(EXPERTS, dtype=jnp.int32)
    my_half = lax.axis_index("dp") % 2
    me = jnp.stack([my_col, my_row, my_half]).astype(jnp.int32)
    me_first = jnp.stack([first_local, my_col, first_expert]).astype(jnp.int32)

    x_list = gather_col(inputs)
    w_list = gather_row(jnp.concatenate([w_query, key_weight, value_weight], axis=1))
    wo_rows = gather_row(after(w_output, w_list[0]))
    spots, starts = places(lengths[0], my_row * plane, plane)
    frequency = jnp.exp(
        -math.log(ROPE_BASE) * jnp.arange(HEAD_SIZE // 2, dtype=jnp.float32) / (HEAD_SIZE // 2)
    )
    frequency = jnp.tile(frequency, 4)
    sign = jnp.tile(jnp.repeat(jnp.array([-1.0, 1.0], jnp.float32), HEAD_SIZE // 2), 2)
    angles = (spots - starts).astype(jnp.float32)[:, None] * frequency[None, :]
    cos_table = jnp.cos(angles)
    sin_table = jnp.sin(angles) * sign[None, :]
    start = (starts - (my_row - 1) * plane)[None, :]
    route_rows = routes.astype(jnp.bfloat16).reshape(-1, width)
    extra = route_rows.shape[0]
    blank = jnp.zeros((16 - extra, width), jnp.bfloat16)
    go = jnp.concatenate([d_output, route_rows, blank], axis=0)
    xn1, q4, kv, w_joined = project(me, norm1_gain[None, :], cos_table, sin_table, x_list, w_list)
    kv_before = lax.ppermute(kv, "row", [(i, i + 1) for i in range(row_count - 1)])

    wo_rows, go_mine = lax.optimization_barrier((wo_rows, go, kv))[:2]
    wo_place = jnp.zeros((query_cols, width), jnp.bfloat16)
    for s in range(row_count):
        at = lax.rem(my_row - s + row_count, row_count) * (width // row_count)
        wo_place = lax.dynamic_update_slice_in_dim(wo_place, wo_rows[s], at, 1)
    wo_list = gather_col(wo_place)
    go_list = gather_tokens(go_mine, axes)

    *heads, lse = attend(me, q4, kv_before, kv, start, tok)
    o_list = exchange_col(heads)
    o_list, go_list = lax.optimization_barrier((o_list, go_list))
    hidden, hn = second_norm(inputs, norm2_gain[None, :], o_list, wo_list)

    routes_all = jnp.concatenate([g[tok : tok + extra] for g in go_list], axis=0)
    routes_t = routes_all.reshape(sources * tok, TOPK).astype(jnp.int32).T
    mask_all = route_mask(routes_t, ids)
    mask_mine = lax.dynamic_slice_in_dim(mask_all, first_expert, mine_experts, 0)
    before = jnp.triu(jnp.ones((tok, tok), jnp.bfloat16), 1)
    rank = jnp.dot(
        mask_mine.reshape(mine_experts * sources, tok).astype(jnp.bfloat16),
        before,
        preferred_element_type=jnp.float32,
    ).astype(jnp.int32)
    pos = jnp.where(mask_mine, rank.reshape(mine_experts, sources * tok), -1)
    pos = pos.reshape(mine_experts, 1, sources * tok)
    per_row = width // tok
    mixed_ids = ids.reshape(-1, per_row).T.reshape(-1)
    mask_own = route_mask(routes.T, mixed_ids).astype(jnp.int32)
    router_t = router.T
    router_mixed = router_t.reshape(-1, per_row, width).swapaxes(0, 1).reshape(EXPERTS, width)

    hn_list = gather_tokens(hn, axes)
    logits_t = jnp.concatenate([nt_dot(router_t, h) for h in hn_list], axis=1)
    gate_all = masked_softmax(logits_t, mask_all)
    gate_mine = lax.dynamic_slice_in_dim(gate_all, first_expert, mine_experts, 0)
    gate_mine = gate_mine.reshape(mine_experts, 1, sources * tok)
    calls = mine_experts if split else 1
    count = mine_experts // calls
    results = [
        experts(
            me_first,
            hn_list,
            go_list,
            pos,
            gate_mine,
            w_gate,
            w_up,
            w_down,
            row_count,
            col_count,
            call * count,
            count,
        )
        for call in range(calls)
    ]
    y_list, dx_list, dgate_list, grad_list = [list(r) for r in zip(*results)]
    keep, away = combine(me_first, pos, y_list, dx_list, dgate_list, tok)
    low = tok + 2 * EXPERTS * tok // width
    if two_way(axes):
        keep, came, by_x, by_y, last_low, last_high = scatter_tokens(keep, away, low)
        dhn_parts, out_parts = [keep, came, by_x, last_low], [keep, came, by_y, last_high]
    else:
        terms = jnp.concatenate([keep, away], axis=0)
        dhn_parts = [lax.psum_scatter(terms, axes, scatter_dimension=0, tiled=False)]
    dh, dattn, *do_mine, small = second_norm_back(
        hidden, hn, d_output, router_mixed, mask_own, norm2_gain[None, :], wo_list, dhn_parts, low
    )

    do_list = exchange_col(do_mine)
    dattn_late = after(dattn, do_list[2])
    dattn_list = [dattn_late] + [swap(dattn_late, "col", s) for s in (1, 2, 3)]
    dq, dbefore, dkv = attend_back(
        me, q4, kv_before, kv, start, lse, do_list, cos_table, sin_table, tok
    )
    lists, sums_list = [], []
    if split:
        sums_list = [
            lax.psum_scatter(grads, "row", scatter_dimension=0, tiled=False) for grads in grad_list
        ]

    def spread(sums):
        return exchange_col([sums[s] for s in range(col_count)])

    if split:
        lists = [spread(after(sums, do_list[2])) for sums in sums_list[: calls // 2]]
    dafter = lax.ppermute(dbefore, "row", [(i + 1, i) for i in range(row_count - 1)])
    dq, dattn_list = lax.optimization_barrier((dq, dattn_list))
    if two_way(axes):
        output = layer_output(after(hidden, dq), out_parts, low)
        dq, output, lists = lax.optimization_barrier((dq, output, lists))
    else:
        output = (hidden + dhn_parts[0][low:].astype(jnp.float32)).astype(jnp.bfloat16)
    dqkv, dx_keep, dx_away = project_back(me, dq, dkv, dafter, cos_table, sin_table, w_joined, tok)
    dx_came = swap(dx_away, "col", 1)
    grad_send, grad_keep = weight_grad(me, xn1, dqkv, heads, dattn_list, row_count)
    dx_came, grad_send = lax.optimization_barrier((dx_came, grad_send))
    grad_came = swap(grad_send, "dp", 1)
    dx_far = (dx_keep[1].astype(jnp.float32) + dx_came[1].astype(jnp.float32)).astype(jnp.bfloat16)
    dx_gone = swap(dx_far, "col", 2)

    if split:
        lists += [spread(after(sums, dx_far)) for sums in sums_list[calls // 2 : calls - 1]]
    dx_gone, lists, grad_came = lax.optimization_barrier((dx_gone, lists, grad_came))
    d_inputs, gain_one = first_norm_back(
        inputs, dh, norm1_gain[None, :], dx_keep, dx_came, dx_gone
    )
    small = jnp.concatenate([small[: EXPERTS + 1], gain_one[:1]], axis=0)
    small = sum_over(sum_over(small, "col"), "dp")

    grad_keep = after(grad_keep, small)
    pair = (grad_keep.astype(jnp.float32) + grad_came.astype(jnp.float32)).astype(jnp.bfloat16)
    mine = scatter_row([pair[s] for s in range(row_count)], small)
    step = 2
    while step < dp_count:
        mine = mine + swap(mine.astype(jnp.bfloat16), "dp", step).astype(jnp.float32)
        step *= 2
    mine = mine.astype(jnp.bfloat16)
    other = swap(mine, "dp", 1)
    first, second = jnp.where(my_half == 0, mine, other), jnp.where(my_half == 0, other, mine)
    tall = width // row_count
    d_w_qkv = jnp.concatenate([first[:tall], second[:tall]], axis=1).astype(jnp.float32)
    d_w_output = jnp.concatenate([first[tall:], second[tall:]], axis=0).astype(jnp.float32)

    if split:
        lists.append(spread(after(sums_list[-1], small)))
    small = sum_over(small, "row")
    if split:
        lists[-1] = lax.optimization_barrier((lists[-1], small, d_w_qkv))[0]
        d_w_gate, d_w_up, d_w_down = finish(me_first, lists)
        d_w_down = jnp.swapaxes(d_w_down, 1, 2)
    else:
        order = jnp.stack([my_col ^ s for s in range(col_count)])
        back = jnp.take(grad_list[0], order, axis=1)
        sums = lax.psum_scatter(
            back.reshape((row_count * col_count,) + back.shape[2:]),
            ("row", "col"),
            scatter_dimension=0,
            tiled=False,
        )
        d_w_gate = sums[:, 0].astype(jnp.float32)
        d_w_up = sums[:, 1].astype(jnp.float32)
        d_w_down = jnp.swapaxes(sums[:, 2], 1, 2).astype(jnp.float32)

    d_router = small[:EXPERTS].reshape(per_row, -1, width).swapaxes(0, 1).reshape(EXPERTS, width).T
    return (
        output,
        d_inputs,
        small[EXPERTS + 1],
        d_w_qkv[:, :query_cols],
        d_w_qkv[:, query_cols : query_cols + key_cols],
        d_w_qkv[:, query_cols + key_cols :],
        d_w_output,
        small[EXPERTS],
        d_router,
        d_w_gate,
        d_w_up,
        d_w_down,
    )


def solution(mesh):
    return jax.shard_map(
        on_device,
        mesh=mesh,
        in_specs=(
            P(("dp", "row", "col"), None),
            P("dp", None),
            P(("dp", "row", "col"), None),
            P(),
            P("row", "col"),
            P("row", "col"),
            P("row", "col"),
            P("col", "row"),
            P(),
            P(),
            P("dp", None, None),
            P("dp", None, None),
            P("dp", None, None),
            P(("dp", "row", "col"), None),
        ),
        out_specs=(
            P(("dp", "row", "col"), None),
            P(("dp", "row", "col"), None),
            P(),
            P("row", "col"),
            P("row", "col"),
            P("row", "col"),
            P("col", "row"),
            P(),
            P(),
            P("dp", ("row", "col"), None),
            P("dp", ("row", "col"), None),
            P("dp", None, ("row", "col")),
        ),
        check_vma=False,
    )
```

```python
import functools
import math

import jax
import jax.numpy as jnp
from jax import lax
from jax.experimental import pallas as pl
from jax.experimental.pallas import tpu as pltpu
from jax.sharding import PartitionSpec as P

HEAD_SIZE = 64
EXPERTS = 32
TOPK = 8
MAX_LEN = 1024
CAP = 96

EPSILON = 1e-06
MASKED_SCORE = -1e30
ROPE_BASE = 10000.0
LANES = 128
MIB = 1024 * 1024


def nt_dot(left, right):
    return lax.dot_general(
        left, right, (((1,), (1,)), ((), ())), preferred_element_type=jnp.float32
    )


def tn_dot(left, right):
    return lax.dot_general(
        left, right, (((0,), (0,)), ((), ())), preferred_element_type=jnp.float32
    )


def nn_dot(left, right):
    return jnp.dot(left, right, preferred_element_type=jnp.float32)


def swap(value, axis, step):
    return lax.ppermute(value, axis, [(i, i ^ step) for i in range(lax.axis_size(axis))])


def after(value, *others):
    return lax.optimization_barrier((value,) + others)[0]


def gather_col(value):
    far = swap(value, "col", 2)
    near = swap(value, "col", 1)
    return [value, near, far, swap(far, "col", 1)]


def exchange_col(blocks):
    return [blocks[0]] + [swap(blocks[s], "col", s) for s in (1, 2, 3)]


def shift_row(value, step):
    size = lax.axis_size("row")
    return lax.ppermute(value, "row", [(i, (i + step) % size) for i in range(size)])


def gather_row(value):
    return [value] + [shift_row(value, s) for s in range(1, lax.axis_size("row"))]


def scatter_row(blocks, late):
    total = after(blocks[0], late).astype(jnp.float32)
    for step in range(1, len(blocks)):
        total = total + shift_row(blocks[step], step).astype(jnp.float32)
    return total


def sum_over(value, axis):
    size = lax.axis_size(axis)
    if size & (size - 1):
        return lax.psum(value, axis)
    if size == 4:
        near, far, cross = [swap(value, axis, step) for step in (1, 2, 3)]
        return (value + near) + (far + cross)
    step = 1
    while step < size:
        value = value + swap(value, axis, step)
        step *= 2
    return value


def sum_over_low(value, axis):
    if lax.axis_size(axis) == 2:
        return value.astype(jnp.float32) + swap(value, axis, 1).astype(jnp.float32)
    return lax.psum(value, axis).astype(jnp.float32)


def two_way(axes):
    return axes == ("dp", "col") and lax.axis_size("dp") == 2


def gather_tokens(value, axes):
    if not two_way(axes):
        every = lax.all_gather(value, axes)
        return [every[s] for s in range(every.shape[0])]
    half = value.shape[0] // 32 * 16
    along_x = swap(value, "dp", 1)
    along_y = swap(value, "col", 2)
    near = swap(value, "col", 1)
    cross_low = swap(along_x[:half], "col", 2)
    cross_high = swap(along_y[half:], "dp", 1)
    near_x = swap(along_x, "col", 1)
    near_y = swap(along_y, "col", 1)
    cross = jnp.concatenate([cross_low, cross_high], axis=0)
    near_cross = swap(cross, "col", 1)
    return [value, along_y, along_x, cross, near, near_y, near_x, near_cross]


def add_first_kernel(keep_ref, came_ref, x_ref, y_ref, *, low):
    def total(spot, rows):
        return (
            keep_ref[spot, rows].astype(jnp.float32) + came_ref[spot, rows].astype(jnp.float32)
        ).astype(jnp.bfloat16)

    x_ref[0], x_ref[1] = total(2, slice(0, low)), total(3, slice(0, low))
    y_ref[0], y_ref[1] = total(1, slice(low, None)), total(3, slice(low, None))


def add_second_kernel(keep_ref, came_ref, x_ref, y_ref, low_ref, high_ref, *, low):
    def total(spot, rows, extra):
        return (
            keep_ref[spot, rows].astype(jnp.float32)
            + came_ref[spot, rows].astype(jnp.float32)
            + extra.astype(jnp.float32)
        ).astype(jnp.bfloat16)

    low_ref[...] = total(1, slice(0, low), x_ref[1])
    high_ref[...] = total(2, slice(low, None), y_ref[1])


def scatter_tokens(keep, away, low):
    rows, width = keep.shape[1:]
    high = rows - low
    came = swap(away, "col", 1)
    params = pltpu.CompilerParams(vmem_limit_bytes=60 * MIB)
    send_x, send_y = pl.pallas_call(
        functools.partial(add_first_kernel, low=low),
        out_shape=[
            jax.ShapeDtypeStruct((2, low, width), jnp.bfloat16),
            jax.ShapeDtypeStruct((2, high, width), jnp.bfloat16),
        ],
        compiler_params=params,
        name="add_first",
    )(keep, came)
    by_x, by_y = swap(send_x, "dp", 1), swap(send_y, "col", 2)
    last_low, last_high = pl.pallas_call(
        functools.partial(add_second_kernel, low=low),
        out_shape=[
            jax.ShapeDtypeStruct((low, width), jnp.bfloat16),
            jax.ShapeDtypeStruct((high, width), jnp.bfloat16),
        ],
        compiler_params=params,
        name="add_second",
    )(keep, came, by_x, by_y)
    return [keep, came, by_x, by_y, swap(last_low, "col", 2), swap(last_high, "dp", 1)]


def part_specs(parts):
    specs = []
    for part in parts:
        if part.ndim == 3:
            specs.append(pl.BlockSpec((1,) + part.shape[1:], lambda i: (0, 0, 0)))
        else:
            specs.append(pl.BlockSpec(part.shape, lambda i: (0, 0)))
    return specs


def swap_halves(value):
    lane = lax.broadcasted_iota(jnp.int32, value.shape, 1)
    first = (lane % HEAD_SIZE) < HEAD_SIZE // 2
    half = HEAD_SIZE // 2
    return jnp.where(first, pltpu.roll(value, LANES - half, 1), pltpu.roll(value, half, 1))


def turn(value, cos_part, sin_part):
    return value * cos_part + swap_halves(value) * sin_part


def spread_heads(pairs):
    lane = lax.broadcasted_iota(jnp.int32, pairs[0].shape, 1)
    low_lane = lane < HEAD_SIZE
    return [
        jnp.where(low_lane, pairs[0], 0.0),
        jnp.where(low_lane, pltpu.roll(pairs[0], HEAD_SIZE, 1), 0.0),
        jnp.where(low_lane, 0.0, pltpu.roll(pairs[1], HEAD_SIZE, 1)),
        jnp.where(low_lane, 0.0, pairs[1]),
    ]


def join_heads(heads):
    lane = lax.broadcasted_iota(jnp.int32, heads[0].shape, 1)
    low_lane = lane < HEAD_SIZE
    return [
        jnp.where(low_lane, heads[0], pltpu.roll(heads[1], HEAD_SIZE, 1)),
        jnp.where(low_lane, pltpu.roll(heads[2], HEAD_SIZE, 1), heads[3]),
    ]


SMEM_SPEC = pl.BlockSpec(memory_space=pltpu.SMEM)
VMEM_SPEC = pl.BlockSpec(memory_space=pltpu.VMEM)


def place_rows(index, block):
    return pl.ds(pl.multiple_of(index * block, block), block)


def project_kernel(*refs, rows, block):
    me_ref, gain_ref, cos_ref, sin_ref = refs[:4]
    x_refs, w_refs = refs[4:8], refs[8 : 8 + rows]
    xn_ref, q_ref, kv_ref, w_ref = refs[8 + rows :]
    my_col, my_row = me_ref[0], me_ref[1]
    part = w_refs[0].shape[0]
    for s in range(rows):
        w_ref[place_rows(lax.rem(my_row - s + rows, rows), part), :] = w_refs[s][...]
    w_joined = w_ref[...]
    scale = 1.0 / math.sqrt(HEAD_SIZE)
    for s in range(4):
        at = place_rows(my_col ^ s, block)
        x = x_refs[s][...].astype(jnp.float32)
        rinv = lax.rsqrt(jnp.mean(x * x, axis=1, keepdims=True) + EPSILON)
        xn = (x * rinv * gain_ref[...]).astype(jnp.bfloat16)
        xn_ref[at, :] = xn
        joined = nn_dot(xn, w_joined)
        cos_part, sin_part = cos_ref[at, :], sin_ref[at, :]
        pairs = [
            turn(joined[:, i * LANES : (i + 1) * LANES], cos_part, sin_part) * scale
            for i in range(2)
        ]
        for h, head in enumerate(spread_heads(pairs)):
            q_ref[h, at, :] = head.astype(jnp.bfloat16)
        kv_ref[at, :LANES] = turn(joined[:, 2 * LANES : 3 * LANES], cos_part, sin_part).astype(
            jnp.bfloat16
        )
        kv_ref[at, LANES:] = joined[:, 3 * LANES :].astype(jnp.bfloat16)


def project(me, gain, cos_table, sin_table, x_list, w_list):
    block, width = x_list[0].shape
    rows = len(w_list)
    plane = 4 * block
    return pl.pallas_call(
        functools.partial(project_kernel, rows=rows, block=block),
        in_specs=[SMEM_SPEC] + [VMEM_SPEC] * (7 + rows),
        out_specs=[VMEM_SPEC] * 4,
        out_shape=[
            jax.ShapeDtypeStruct((plane, width), jnp.bfloat16),
            jax.ShapeDtypeStruct((4, plane, LANES), jnp.bfloat16),
            jax.ShapeDtypeStruct((plane, 2 * LANES), jnp.bfloat16),
            jax.ShapeDtypeStruct((width, 4 * LANES), jnp.bfloat16),
        ],
        compiler_params=pltpu.CompilerParams(vmem_limit_bytes=60 * MIB),
        name="project",
    )(me, gain, cos_table, sin_table, *x_list, *w_list)


def project_back_kernel(
    me_ref, dq_ref, own_ref, came_ref, cos_ref, sin_ref, w_ref, dqkv_ref, keep_ref, away_ref, *, block
):
    my_col = me_ref[0]
    for s in (1, 3, 0, 2):
        at = place_rows(my_col ^ s, block)
        total = own_ref[at, :] + came_ref[at, :].astype(jnp.float32)
        dk = turn(total[:, :LANES], cos_ref[at, :], -sin_ref[at, :]).astype(jnp.bfloat16)
        dqkv = jnp.concatenate([dq_ref[at, :], dk, total[:, LANES:].astype(jnp.bfloat16)], axis=1)
        dqkv_ref[at, :] = dqkv
        target = away_ref if s % 2 else keep_ref
        target[s // 2] = nt_dot(dqkv, w_ref[...]).astype(jnp.bfloat16)


def project_back(me, dq, own, came, cos_table, sin_table, w_joined, block):
    width = w_joined.shape[0]
    return pl.pallas_call(
        functools.partial(project_back_kernel, block=block),
        in_specs=[SMEM_SPEC] + [VMEM_SPEC] * 6,
        out_specs=[VMEM_SPEC] * 3,
        out_shape=[
            jax.ShapeDtypeStruct((dq.shape[0], 4 * LANES), jnp.bfloat16),
            jax.ShapeDtypeStruct((2, block, width), jnp.bfloat16),
            jax.ShapeDtypeStruct((2, block, width), jnp.bfloat16),
        ],
        compiler_params=pltpu.CompilerParams(vmem_limit_bytes=32 * MIB),
        name="project_back",
    )(me, dq, own, came, cos_table, sin_table, w_joined)


def weight_grad_kernel(me_ref, xn_ref, dqkv_ref, *refs, rows, dps):
    heads, dattn = refs[:4], refs[4:8]
    send_ref, keep_ref, scratch, scratch_out = refs[8:]
    scratch[...] = tn_dot(xn_ref[...], dqkv_ref[...])
    total = None
    for s in range(4):
        term = tn_dot(heads[s][...], dattn[s][...])
        total = term if total is None else total + term
    scratch_out[...] = total
    part = keep_ref.shape[2]
    tall, half = scratch.shape[0] // rows, scratch_out.shape[0] // dps
    for s in range(rows):
        row = lax.rem(me_ref[1] + s, rows)
        for d, ref in enumerate((keep_ref, send_ref)[:dps]):
            mine = me_ref[2] ^ d
            ref[s, :tall] = scratch[place_rows(row, tall), place_rows(mine, part)].astype(
                jnp.bfloat16
            )
            ref[s, tall:] = scratch_out[place_rows(mine, half), place_rows(row, part)].astype(
                jnp.bfloat16
            )


def weight_grad(me, xn, dqkv, heads, dattn, rows):
    width, cols = xn.shape[1], dqkv.shape[1]
    out_rows = heads[0].shape[1]
    shape = (rows, width // rows + out_rows // 2, cols // 2)
    return pl.pallas_call(
        functools.partial(weight_grad_kernel, rows=rows, dps=2),
        in_specs=[SMEM_SPEC] + [VMEM_SPEC] * 10,
        out_specs=[VMEM_SPEC] * 2,
        out_shape=[jax.ShapeDtypeStruct(shape, jnp.bfloat16)] * 2,
        scratch_shapes=[
            pltpu.VMEM((width, cols), jnp.float32),
            pltpu.VMEM((out_rows, width), jnp.float32),
        ],
        compiler_params=pltpu.CompilerParams(vmem_limit_bytes=32 * MIB),
        name="weight_grad",
    )(me, xn, dqkv, *heads, *dattn)


def window_bias(start, first_key, window, block, plane):
    key_at = first_key + lax.broadcasted_iota(jnp.int32, (window, block), 0)
    query_at = first_key + plane + lax.broadcasted_iota(jnp.int32, (window, block), 1)
    allowed = (key_at >= start) & (key_at <= query_at)
    return jnp.where(allowed, 0.0, MASKED_SCORE)


def attend_kernel(
    me_ref, q_ref, before_ref, kv_ref, start_ref, o0, o1, o2, o3, lse_ref, kv_all, *, plane, block
):
    window = plane + block
    step = pl.program_id(0)

    @pl.when(step == 0)
    def _():
        kv_all[:plane] = before_ref[...]
        kv_all[plane:] = kv_ref[...]

    first_key = pl.multiple_of((me_ref[0] ^ step) * block, block)
    keys = kv_all[pl.ds(first_key, window), :LANES]
    values = kv_all[pl.ds(first_key, window), LANES:]
    values_t = values.astype(jnp.float32).T.astype(jnp.bfloat16)
    bias = window_bias(start_ref[...], first_key, window, block, plane)
    heads = []
    for h in range(4):
        scores = nt_dot(keys, q_ref[h]) + bias
        top = jnp.max(scores, axis=0, keepdims=True)
        weights = jnp.exp(scores - top)
        total = jnp.sum(weights, axis=0, keepdims=True)
        mixed = nn_dot(values_t, weights.astype(jnp.bfloat16)) / total
        lse_ref[h : h + 1, :] = top + jnp.log(total)
        heads.append(mixed.T)
    pairs = jnp.concatenate([p.astype(jnp.bfloat16) for p in join_heads(heads)], axis=1)
    for s, o_ref in enumerate((o0, o1, o2, o3)):

        @pl.when(step == s)
        def _(o_ref=o_ref):
            o_ref[...] = pairs


def attend(me, q4, before, kv, start, block):
    plane = q4.shape[1]
    whole = pl.BlockSpec((plane, 2 * LANES), lambda i, m: (0, 0))
    return pl.pallas_call(
        functools.partial(attend_kernel, plane=plane, block=block),
        grid_spec=pltpu.PrefetchScalarGridSpec(
            num_scalar_prefetch=1,
            grid=(4,),
            in_specs=[
                pl.BlockSpec((4, block, LANES), lambda i, m: (0, m[0] ^ i, 0)),
                whole,
                whole,
                pl.BlockSpec((1, block), lambda i, m: (0, m[0] ^ i)),
            ],
            out_specs=[pl.BlockSpec((block, 2 * LANES), lambda i, m: (0, 0))] * 4
            + [pl.BlockSpec((4, block), lambda i, m: (0, m[0] ^ i))],
            scratch_shapes=[pltpu.VMEM((2 * plane, 2 * LANES), jnp.bfloat16)],
        ),
        out_shape=[jax.ShapeDtypeStruct((block, 2 * LANES), jnp.bfloat16)] * 4
        + [jax.ShapeDtypeStruct((4, plane), jnp.float32)],
        compiler_params=pltpu.CompilerParams(vmem_limit_bytes=32 * MIB),
        name="attend",
    )(me, q4, before, kv, start)


def attend_back_kernel(
    me_ref,
    q_ref,
    before_ref,
    kv_ref,
    start_ref,
    lse_ref,
    do0,
    do1,
    do2,
    do3,
    cos_ref,
    sin_ref,
    dq_ref,
    dbefore_ref,
    dkv_ref,
    kv_all,
    sums,
    do_now,
    *,
    plane,
    block,
):
    window = plane + block
    step = pl.program_id(0)

    @pl.when(step == 0)
    def _():
        kv_all[:plane] = before_ref[...]
        kv_all[plane:] = kv_ref[...]
        sums[...] = jnp.zeros_like(sums)

    for s, do_ref in enumerate((do0, do1, do2, do3)):

        @pl.when(step == s)
        def _(do_ref=do_ref):
            do_now[...] = do_ref[...]

    first_key = pl.multiple_of((me_ref[0] ^ step) * block, block)
    keys = kv_all[pl.ds(first_key, window), :LANES]
    values = kv_all[pl.ds(first_key, window), LANES:]
    keys_t = keys.astype(jnp.float32).T.astype(jnp.bfloat16)
    bias = window_bias(start_ref[...], first_key, window, block, plane)
    grad = do_now[...].astype(jnp.float32)
    grads = [g.astype(jnp.bfloat16) for g in spread_heads([grad[:, :LANES], grad[:, LANES:]])]
    heads = []
    dk_total, dv_total = None, None
    for h in range(4):
        q = q_ref[h]
        weights = jnp.exp(nt_dot(keys, q) + bias - lse_ref[h : h + 1, :])
        dv = nn_dot(weights.astype(jnp.bfloat16), grads[h])
        product = weights * nt_dot(values, grads[h])
        centre = jnp.sum(product, axis=0, keepdims=True)
        ds = (product - weights * centre).astype(jnp.bfloat16)
        dk = nn_dot(ds, q)
        heads.append(nn_dot(keys_t, ds).T)
        dk_total = dk if dk_total is None else dk_total + dk
        dv_total = dv if dv_total is None else dv_total + dv
    sums[pl.ds(first_key, window), :LANES] += dk_total
    sums[pl.ds(first_key, window), LANES:] += dv_total
    scale = 1.0 / math.sqrt(HEAD_SIZE)
    for i, pair in enumerate(join_heads(heads)):
        dq_ref[:, i * LANES : (i + 1) * LANES] = turn(
            pair * scale, cos_ref[...], -sin_ref[...]
        ).astype(jnp.bfloat16)

    @pl.when(step == 3)
    def _():
        dbefore_ref[...] = sums[:plane].astype(jnp.bfloat16)
        dkv_ref[...] = sums[plane:]


def attend_back(me, q4, before, kv, start, lse, do_list, cos_table, sin_table, block):
    plane = q4.shape[1]
    whole = pl.BlockSpec((plane, 2 * LANES), lambda i, m: (0, 0))
    small = pl.BlockSpec((block, 2 * LANES), lambda i, m: (0, 0))
    table = pl.BlockSpec((block, LANES), lambda i, m: (m[0] ^ i, 0))
    return pl.pallas_call(
        functools.partial(attend_back_kernel, plane=plane, block=block),
        grid_spec=pltpu.PrefetchScalarGridSpec(
            num_scalar_prefetch=1,
            grid=(4,),
            in_specs=[
                pl.BlockSpec((4, block, LANES), lambda i, m: (0, m[0] ^ i, 0)),
                whole,
                whole,
                pl.BlockSpec((1, block), lambda i, m: (0, m[0] ^ i)),
                pl.BlockSpec((4, block), lambda i, m: (0, m[0] ^ i)),
            ]
            + [small] * 4
            + [table, table],
            out_specs=[
                pl.BlockSpec((block, 2 * LANES), lambda i, m: (m[0] ^ i, 0)),
                whole,
                whole,
            ],
            scratch_shapes=[
                pltpu.VMEM((2 * plane, 2 * LANES), jnp.bfloat16),
                pltpu.VMEM((2 * plane, 2 * LANES), jnp.float32),
                pltpu.VMEM((block, 2 * LANES), jnp.bfloat16),
            ],
        ),
        out_shape=[
            jax.ShapeDtypeStruct((plane, 2 * LANES), jnp.bfloat16),
            jax.ShapeDtypeStruct((plane, 2 * LANES), jnp.bfloat16),
            jax.ShapeDtypeStruct((plane, 2 * LANES), jnp.float32),
        ],
        compiler_params=pltpu.CompilerParams(vmem_limit_bytes=32 * MIB),
        name="attend_back",
    )(me, q4, before, kv, start, lse, *do_list, cos_table, sin_table)


def hidden_kernel(x_ref, gain_ref, o0, o1, o2, o3, w0, w1, w2, w3, hidden_ref, hn_ref):
    hidden = x_ref[...].astype(jnp.float32)
    for o_ref, w_ref in ((o0, w0), (o1, w1), (o2, w2), (o3, w3)):
        hidden = hidden + nn_dot(o_ref[...], w_ref[...])
    hidden_ref[...] = hidden
    rinv = lax.rsqrt(jnp.mean(hidden * hidden, axis=1, keepdims=True) + EPSILON)
    hn_ref[...] = (hidden * rinv * gain_ref[...]).astype(jnp.bfloat16)


def second_norm(x, gain, o_list, wo_list):
    return pl.pallas_call(
        hidden_kernel,
        out_shape=[
            jax.ShapeDtypeStruct(x.shape, jnp.float32),
            jax.ShapeDtypeStruct(x.shape, jnp.bfloat16),
        ],
        compiler_params=pltpu.CompilerParams(vmem_limit_bytes=32 * MIB),
        name="second_norm",
    )(x, gain, *o_list, *wo_list)


def masked_softmax(logits, mask):
    shown = jnp.where(mask, logits, MASKED_SCORE)
    top = jnp.max(shown, axis=0, keepdims=True)
    raised = jnp.where(mask, jnp.exp(shown - top), 0.0)
    return raised / jnp.sum(raised, axis=0, keepdims=True)


def second_norm_back_kernel(*refs, low, tok, parts):
    hidden_ref, hn_ref, go_ref, router_ref, mask_ref, gain_ref = refs[:6]
    wo_refs = refs[6:10]
    part_refs = refs[10 : 10 + parts]
    dh_ref, dattn_ref, do0, do1, do2, do3, small_ref = refs[10 + parts :]
    total = part_refs[0][:low, :] if parts == 1 else part_refs[0][0, :low]
    total = total.astype(jnp.float32)
    if parts > 1:
        total = total + part_refs[1][0, :low].astype(jnp.float32)
        total = total + part_refs[2][0].astype(jnp.float32)
        total = total + part_refs[3][...].astype(jnp.float32)
    width = hidden_ref.shape[1]
    group = EXPERTS * tok // width
    spare = total[tok : tok + group] + total[tok + group :]
    dgate = jnp.concatenate(
        [spare[:, b * tok : (b + 1) * tok] for b in range(width // tok)], axis=0
    )
    hn = hn_ref[...]
    router = router_ref[...]
    gate = masked_softmax(nt_dot(router, hn), mask_ref[...] > 0)
    dlogits = gate * (dgate - jnp.sum(gate * dgate, axis=0, keepdims=True))
    dlogits = dlogits.astype(jnp.bfloat16)
    dhn = total[:tok] + tn_dot(dlogits, router)
    small_ref[:EXPERTS, :] = nn_dot(dlogits, hn)
    hidden = hidden_ref[...]
    rinv = lax.rsqrt(jnp.mean(hidden * hidden, axis=1, keepdims=True) + EPSILON)
    unit = hidden * rinv
    small_ref[EXPERTS:, :] = jnp.broadcast_to(
        jnp.sum(dhn * unit, axis=0, keepdims=True), (8, width)
    )
    scaled = dhn * gain_ref[...]
    dh = go_ref[...].astype(jnp.float32) + rinv * (
        scaled - unit * jnp.mean(scaled * unit, axis=1, keepdims=True)
    )
    dh_ref[...] = dh
    dattn = dh.astype(jnp.bfloat16)
    dattn_ref[...] = dattn
    for w_ref, do_ref in zip(wo_refs, (do0, do1, do2, do3)):
        do_ref[...] = nt_dot(dattn, w_ref[...]).astype(jnp.bfloat16)


def second_norm_back(hidden, hn, go, router, mask, gain, wo_list, parts, low):
    tok, width = hidden.shape
    specs = [
        pl.BlockSpec(a.shape, functools.partial(lambda n, i: (0,) * n, a.ndim))
        for a in (hidden, hn, go, router, mask, gain, *wo_list)
    ]
    specs += part_specs(parts)
    cols = wo_list[0].shape[0]
    shapes = [
        jax.ShapeDtypeStruct((tok, width), jnp.float32),
        jax.ShapeDtypeStruct((tok, width), jnp.bfloat16),
    ]
    shapes += [jax.ShapeDtypeStruct((tok, cols), jnp.bfloat16)] * 4
    shapes += [jax.ShapeDtypeStruct((EXPERTS + 8, width), jnp.float32)]
    return pl.pallas_call(
        functools.partial(second_norm_back_kernel, low=low, tok=tok, parts=len(parts)),
        grid=(1,),
        in_specs=specs,
        out_specs=[pl.BlockSpec(s.shape, lambda i: (0, 0)) for s in shapes],
        out_shape=shapes,
        compiler_params=pltpu.CompilerParams(vmem_limit_bytes=32 * MIB),
        name="second_norm_back",
    )(hidden, hn, go, router, mask, gain, *wo_list, *parts)


def first_norm_back_kernel(x_ref, dh_ref, gain_ref, keep_ref, came_ref, far_ref, dx_ref, part_ref):
    x = x_ref[...].astype(jnp.float32)
    rinv = lax.rsqrt(jnp.mean(x * x, axis=1, keepdims=True) + EPSILON)
    unit = x * rinv
    dxn = keep_ref[0].astype(jnp.float32) + came_ref[0].astype(jnp.float32)
    dxn = dxn + far_ref[...].astype(jnp.float32)
    part_ref[...] = jnp.broadcast_to(jnp.sum(dxn * unit, axis=0, keepdims=True), part_ref.shape)
    scaled = dxn * gain_ref[...]
    dx_ref[...] = dh_ref[...] + rinv * (
        scaled - unit * jnp.mean(scaled * unit, axis=1, keepdims=True)
    )


def first_norm_back(x, dh, gain, keep, came, far):
    tok, width = x.shape
    flat = pl.BlockSpec((tok, width), lambda i: (0, 0))
    first = pl.BlockSpec((1, tok, width), lambda i: (0, 0, 0))
    return pl.pallas_call(
        first_norm_back_kernel,
        grid=(1,),
        in_specs=[flat, flat, pl.BlockSpec((1, width), lambda i: (0, 0)), first, first, flat],
        out_specs=[flat, pl.BlockSpec((8, width), lambda i: (0, 0))],
        out_shape=[
            jax.ShapeDtypeStruct((tok, width), jnp.float32),
            jax.ShapeDtypeStruct((8, width), jnp.float32),
        ],
        compiler_params=pltpu.CompilerParams(vmem_limit_bytes=32 * MIB),
        name="first_norm_back",
    )(x, dh, gain, keep, came, far)


def output_kernel(hidden_ref, keep_ref, came_ref, by_ref, last_ref, out_ref, *, low):
    total = hidden_ref[...] + keep_ref[0, low:].astype(jnp.float32)
    total = total + came_ref[0, low:].astype(jnp.float32)
    total = total + by_ref[0].astype(jnp.float32) + last_ref[...].astype(jnp.float32)
    out_ref[...] = total.astype(jnp.bfloat16)


def layer_output(hidden, parts, low):
    whole = pl.BlockSpec(hidden.shape, lambda i: (0, 0))
    return pl.pallas_call(
        functools.partial(output_kernel, low=low),
        grid=(1,),
        in_specs=[whole] + part_specs(parts),
        out_specs=whole,
        out_shape=jax.ShapeDtypeStruct(hidden.shape, jnp.bfloat16),
        compiler_params=pltpu.CompilerParams(vmem_limit_bytes=60 * MIB),
        name="layer_output",
    )(hidden, *parts)


def expert_kernel(me_ref, *refs, total, chunk, tok, rows, cols):
    hn_refs, go_refs = refs[:total], refs[total : 2 * total]
    pos_ref, gate_ref, wg_ref, wu_ref, wd_ref = refs[2 * total : 2 * total + 5]
    y_ref, dx_ref, dgate_ref, grad_ref = refs[2 * total + 5 : 2 * total + 9]
    x_all, go_rows, slot_gate, sums = refs[2 * total + 9 :]
    for begin in range(0, total, chunk):
        for s in range(chunk):
            at = slice((begin + s) * tok, (begin + s + 1) * tok)
            spot = lax.broadcasted_iota(jnp.int32, (CAP, tok), 0)
            hot = spot == pos_ref[0, :, at]
            hot_low = hot.astype(jnp.bfloat16)
            mine = slice(s * CAP, (s + 1) * CAP)
            x_all[mine, :] = nn_dot(hot_low, hn_refs[begin + s][...]).astype(jnp.bfloat16)
            go_rows[mine, :] = nn_dot(hot_low, go_refs[begin + s][:tok, :]).astype(jnp.bfloat16)
            slot_gate[mine, :] = jnp.sum(
                jnp.where(hot, gate_ref[0, :, at], 0.0), axis=1, keepdims=True
            )
        x = x_all[...]
        go = go_rows[...]
        gate = slot_gate[...]
        a = nn_dot(x, wg_ref[0])
        b = nn_dot(x, wu_ref[0])
        dz = nt_dot(go, wd_ref[0])
        sig = 1.0 / (1.0 + jnp.exp(-a))
        silu = a * sig
        z = silu * b
        z_low = z.astype(jnp.bfloat16)
        dgate = jnp.sum(z_low.astype(jnp.float32) * dz, axis=1, keepdims=True)
        dz = dz * gate
        da = (dz * b * sig * (1.0 + a * (1.0 - sig))).astype(jnp.bfloat16)
        db = (dz * silu).astype(jnp.bfloat16)
        gz = (z * gate).astype(jnp.bfloat16)
        y = (nn_dot(z_low, wd_ref[0]) * gate).astype(jnp.bfloat16)
        dx = (nt_dot(da, wg_ref[0]) + nt_dot(db, wu_ref[0])).astype(jnp.bfloat16)
        for s in range(chunk):
            at = slice((begin + s) * tok, (begin + s + 1) * tok)
            mine = slice(s * CAP, (s + 1) * CAP)
            y_ref[begin + s, 0] = y[mine]
            dx_ref[begin + s, 0] = dx[mine]
            spot = lax.broadcasted_iota(jnp.int32, (CAP, tok), 0)
            hot = spot == pos_ref[0, :, at]
            dgate_ref[0, :, at] = jnp.sum(
                jnp.where(hot, dgate[mine], 0.0), axis=0, keepdims=True
            )
        for i, (left, right) in enumerate(((x, da), (x, db), (go, gz))):
            term = tn_dot(left, right).reshape(sums.shape[1:])
            if begin:
                sums[i] += term
            else:
                sums[i] = term
    for s in range(cols):
        grad_ref[:, s, 0] = jnp.swapaxes(sums[:, :, me_ref[1] ^ s], 0, 1).astype(jnp.bfloat16)


def experts(me, hn_list, go_list, pos, gate, w_gate, w_up, w_down, rows, cols, first, count):
    total = len(hn_list)
    tok, width = hn_list[0].shape
    hidden = w_gate.shape[2]
    chunk = 8 if total % 8 == 0 else total
    part = width // (rows * cols)
    slots = chunk * CAP

    def weight(shape):
        return pl.BlockSpec((1,) + shape, lambda e, m: (m[0] + first + e, 0, 0))

    token = pl.BlockSpec((tok, width), lambda e, m: (0, 0), pipeline_mode=pl.Buffered(1))
    grad_token = pl.BlockSpec(go_list[0].shape, lambda e, m: (0, 0), pipeline_mode=pl.Buffered(1))
    line = pl.BlockSpec((1, 1, total * tok), lambda e, m: (first + e, 0, 0))
    slot = pl.BlockSpec((total, 1, CAP, width), lambda e, m: (0, e, 0, 0))
    return pl.pallas_call(
        functools.partial(
            expert_kernel, total=total, chunk=chunk, tok=tok, rows=rows, cols=cols
        ),
        grid_spec=pltpu.PrefetchScalarGridSpec(
            num_scalar_prefetch=1,
            grid=(count,),
            in_specs=[token] * total
            + [grad_token] * total
            + [line, line, weight((width, hidden)), weight((width, hidden)), weight((hidden, width))],
            out_specs=[
                slot,
                slot,
                pl.BlockSpec((1, 1, total * tok), lambda e, m: (e, 0, 0)),
                pl.BlockSpec(
                    (rows, cols, 1, 3, part, hidden), lambda e, m: (0, 0, e, 0, 0, 0)
                ),
            ],
            scratch_shapes=[
                pltpu.VMEM((slots, width), jnp.bfloat16),
                pltpu.VMEM((slots, width), jnp.bfloat16),
                pltpu.VMEM((slots, 1), jnp.float32),
                pltpu.VMEM((3, rows, cols, part, hidden), jnp.float32),
            ],
        ),
        out_shape=[
            jax.ShapeDtypeStruct((total, count, CAP, width), jnp.bfloat16),
            jax.ShapeDtypeStruct((total, count, CAP, width), jnp.bfloat16),
            jax.ShapeDtypeStruct((count, 1, total * tok), jnp.float32),
            jax.ShapeDtypeStruct((rows, cols, count, 3, part, hidden), jnp.bfloat16),
        ],
        compiler_params=pltpu.CompilerParams(vmem_limit_bytes=62 * MIB),
        name="experts",
    )(me, *hn_list, *go_list, pos, gate, w_gate, w_up, w_down)


def combine_kernel(me_ref, pos_ref, *refs, calls, count, tok, half, extra):
    y_refs, dx_refs, dgate_refs = refs[:calls], refs[calls : 2 * calls], refs[2 * calls : 3 * calls]
    keep_ref, away_ref = refs[3 * calls :]
    width = keep_ref.shape[2]
    low = tok + 2 * extra
    spot = lax.broadcasted_iota(jnp.int32, (CAP, tok), 0)
    hot = jnp.concatenate(
        [(spot == pos_ref[e]).astype(jnp.float32).astype(jnp.bfloat16) for e in range(count)],
        axis=0,
    )

    def rows_of(value_refs):
        return jnp.concatenate([r[0].reshape(-1, width) for r in value_refs], axis=0)

    out = tn_dot(hot, rows_of(y_refs)).astype(jnp.bfloat16)
    dhn = tn_dot(hot, rows_of(dx_refs)).astype(jnp.bfloat16)
    row = lax.broadcasted_iota(jnp.int32, (extra, width), 0)
    lane = lax.broadcasted_iota(jnp.int32, (extra, width), 1)
    per_row = width // tok
    spare = jnp.zeros((extra, width), jnp.float32)
    done = 0
    for dgate_ref in dgate_refs:
        for e in range(dgate_ref.shape[0]):
            expert = me_ref[2] + done
            here = (row == expert // per_row) & (lane // tok == expert % per_row)
            line = jnp.concatenate([dgate_ref[e]] * per_row, axis=1)
            spare = spare + jnp.where(here, line, 0.0)
            done += 1
    spare_high = spare.astype(jnp.bfloat16)
    spare_low = (spare - spare_high.astype(jnp.float32)).astype(jnp.bfloat16)

    def store(ref):
        ref[0, :tok] = dhn
        ref[0, tok:low] = jnp.concatenate([spare_high, spare_low], axis=0)
        ref[0, low:] = out

    @pl.when(pl.program_id(0) < half)
    def _():
        store(keep_ref)

    @pl.when(pl.program_id(0) >= half)
    def _():
        store(away_ref)


def combine(me, pos, y_list, dx_list, dgate_list, tok):
    total, _, _, width = y_list[0].shape
    count = pos.shape[0]
    half = total // 2
    extra = EXPERTS * tok // width
    rows = 2 * tok + 2 * extra
    slots = [
        pl.BlockSpec((1,) + y.shape[1:], lambda s, m: (s, 0, 0, 0)) for y in y_list + dx_list
    ]
    lines = [pl.BlockSpec((d.shape[0], 1, tok), lambda s, m: (0, 0, s)) for d in dgate_list]

    def keep(s, m):
        return (jnp.minimum(s, half - 1), 0, 0)

    def away(s, m):
        return (jnp.maximum(s - half, 0), 0, 0)

    return pl.pallas_call(
        functools.partial(
            combine_kernel, calls=len(y_list), count=count, tok=tok, half=half, extra=extra
        ),
        grid_spec=pltpu.PrefetchScalarGridSpec(
            num_scalar_prefetch=1,
            grid=(total,),
            in_specs=[pl.BlockSpec((count, 1, tok), lambda s, m: (0, 0, s))] + slots + lines,
            out_specs=[
                pl.BlockSpec((1, rows, width), keep),
                pl.BlockSpec((1, rows, width), away),
            ],
        ),
        out_shape=[
            jax.ShapeDtypeStruct((half, rows, width), jnp.bfloat16),
            jax.ShapeDtypeStruct((half, rows, width), jnp.bfloat16),
        ],
        compiler_params=pltpu.CompilerParams(vmem_limit_bytes=60 * MIB),
        name="combine",
    )(me, pos, *y_list, *dx_list, *dgate_list)


def finish_kernel(me_ref, *refs, calls):
    gate_ref, up_ref, down_ref = refs[4 * calls :]
    for s in range(4):

        @pl.when(pl.program_id(0) == s)
        def _(s=s):
            done = 0
            for call in range(calls):
                ref = refs[4 * call + s]
                for e in range(ref.shape[0]):
                    gate_ref[done] = ref[e, 0].astype(jnp.float32)
                    up_ref[done] = ref[e, 1].astype(jnp.float32)
                    down_ref[done] = ref[e, 2].astype(jnp.float32)
                    done += 1


def finish(me, lists):
    calls = len(lists)
    parts = [p for one in lists for p in one]
    mine = sum(one[0].shape[0] for one in lists)
    part, hidden = parts[0].shape[2:]
    whole = [pl.BlockSpec(p.shape, lambda s, m: (0, 0, 0, 0)) for p in parts]
    return pl.pallas_call(
        functools.partial(finish_kernel, calls=calls),
        grid_spec=pltpu.PrefetchScalarGridSpec(
            num_scalar_prefetch=1,
            grid=(4,),
            in_specs=whole,
            out_specs=[
                pl.BlockSpec((mine, part, hidden), lambda s, m: (m[1] ^ s, 0, 0)),
                pl.BlockSpec((mine, part, hidden), lambda s, m: (m[1] ^ s, 0, 0)),
                pl.BlockSpec((mine, part, hidden), lambda s, m: (m[1] ^ s, 0, 0)),
            ],
        ),
        out_shape=[
            jax.ShapeDtypeStruct((4 * mine, part, hidden), jnp.float32),
            jax.ShapeDtypeStruct((4 * mine, part, hidden), jnp.float32),
            jax.ShapeDtypeStruct((4 * mine, part, hidden), jnp.float32),
        ],
        compiler_params=pltpu.CompilerParams(vmem_limit_bytes=32 * MIB),
        name="finish",
    )(me, *parts)


def places(seq_lengths, first_row, total_rows):
    seq_ends = jnp.cumsum(seq_lengths)
    spots = first_row + jnp.arange(total_rows, dtype=jnp.int32)
    passed = (spots[:, None] >= seq_ends[None, :]).astype(jnp.int32)
    starts = jnp.sum(passed * seq_lengths[None, :], axis=1)
    return spots, starts


def route_mask(routes_t, ids):
    return jnp.any(routes_t[None, :, :] == ids[:, None, None], axis=1)


def on_device(
    inputs,
    lengths,
    routes,
    norm1_gain,
    w_query,
    key_weight,
    value_weight,
    w_output,
    norm2_gain,
    router,
    w_gate,
    w_up,
    w_down,
    d_output,
):
    row_count = lax.axis_size("row")
    col_count = lax.axis_size("col")
    dp_count = lax.axis_size("dp")
    my_row, my_col = lax.axis_index("row"), lax.axis_index("col")
    tok, width = inputs.shape
    plane = tok * col_count
    query_cols, key_cols = w_query.shape[1], key_weight.shape[1]
    assert col_count == 4 and plane >= MAX_LEN - 1
    assert query_cols == 2 * LANES and key_cols == LANES
    local_experts = w_gate.shape[0]
    split = local_experts % col_count == 0
    axes = ("dp", "col") if split else ("dp",)
    mine_experts = local_experts // col_count if split else local_experts
    first_local = my_col * mine_experts if split else jnp.int32(0)
    first_expert = lax.axis_index("dp") * local_experts + first_local
    sources = dp_count * (col_count if split else 1)
    ids = jnp.arange(EXPERTS, dtype=jnp.int32)
    my_half = lax.axis_index("dp") % 2
    me = jnp.stack([my_col, my_row, my_half]).astype(jnp.int32)
    me_first = jnp.stack([first_local, my_col, first_expert]).astype(jnp.int32)

    x_list = gather_col(inputs)
    w_list = gather_row(jnp.concatenate([w_query, key_weight, value_weight], axis=1))
    wo_rows = gather_row(after(w_output, w_list[0]))
    spots, starts = places(lengths[0], my_row * plane, plane)
    frequency = jnp.exp(
        -math.log(ROPE_BASE) * jnp.arange(HEAD_SIZE // 2, dtype=jnp.float32) / (HEAD_SIZE // 2)
    )
    frequency = jnp.tile(frequency, 4)
    sign = jnp.tile(jnp.repeat(jnp.array([-1.0, 1.0], jnp.float32), HEAD_SIZE // 2), 2)
    angles = (spots - starts).astype(jnp.float32)[:, None] * frequency[None, :]
    cos_table = jnp.cos(angles)
    sin_table = jnp.sin(angles) * sign[None, :]
    start = (starts - (my_row - 1) * plane)[None, :]
    route_rows = routes.astype(jnp.bfloat16).reshape(-1, width)
    extra = route_rows.shape[0]
    blank = jnp.zeros((16 - extra, width), jnp.bfloat16)
    go = jnp.concatenate([d_output, route_rows, blank], axis=0)
    xn1, q4, kv, w_joined = project(me, norm1_gain[None, :], cos_table, sin_table, x_list, w_list)
    kv_before = lax.ppermute(kv, "row", [(i, i + 1) for i in range(row_count - 1)])

    wo_rows, go_mine = lax.optimization_barrier((wo_rows, go, kv))[:2]
    wo_place = jnp.zeros((query_cols, width), jnp.bfloat16)
    for s in range(row_count):
        at = lax.rem(my_row - s + row_count, row_count) * (width // row_count)
        wo_place = lax.dynamic_update_slice_in_dim(wo_place, wo_rows[s], at, 1)
    wo_list = gather_col(wo_place)
    go_list = gather_tokens(go_mine, axes)

    *heads, lse = attend(me, q4, kv_before, kv, start, tok)
    o_list = exchange_col(heads)
    o_list, go_list = lax.optimization_barrier((o_list, go_list))
    hidden, hn = second_norm(inputs, norm2_gain[None, :], o_list, wo_list)

    routes_all = jnp.concatenate([g[tok : tok + extra] for g in go_list], axis=0)
    routes_t = routes_all.reshape(sources * tok, TOPK).astype(jnp.int32).T
    mask_all = route_mask(routes_t, ids)
    mask_mine = lax.dynamic_slice_in_dim(mask_all, first_expert, mine_experts, 0)
    before = jnp.triu(jnp.ones((tok, tok), jnp.bfloat16), 1)
    rank = jnp.dot(
        mask_mine.reshape(mine_experts * sources, tok).astype(jnp.bfloat16),
        before,
        preferred_element_type=jnp.float32,
    ).astype(jnp.int32)
    pos = jnp.where(mask_mine, rank.reshape(mine_experts, sources * tok), -1)
    pos = pos.reshape(mine_experts, 1, sources * tok)
    per_row = width // tok
    mixed_ids = ids.reshape(-1, per_row).T.reshape(-1)
    mask_own = route_mask(routes.T, mixed_ids).astype(jnp.int32)
    router_t = router.T
    router_mixed = router_t.reshape(-1, per_row, width).swapaxes(0, 1).reshape(EXPERTS, width)

    hn_list = gather_tokens(hn, axes)
    logits_t = jnp.concatenate([nt_dot(router_t, h) for h in hn_list], axis=1)
    gate_all = masked_softmax(logits_t, mask_all)
    gate_mine = lax.dynamic_slice_in_dim(gate_all, first_expert, mine_experts, 0)
    gate_mine = gate_mine.reshape(mine_experts, 1, sources * tok)
    calls = mine_experts if split else 1
    count = mine_experts // calls
    results = [
        experts(
            me_first,
            hn_list,
            go_list,
            pos,
            gate_mine,
            w_gate,
            w_up,
            w_down,
            row_count,
            col_count,
            call * count,
            count,
        )
        for call in range(calls)
    ]
    y_list, dx_list, dgate_list, grad_list = [list(r) for r in zip(*results)]
    keep, away = combine(me_first, pos, y_list, dx_list, dgate_list, tok)
    low = tok + 2 * EXPERTS * tok // width
    if two_way(axes):
        keep, came, by_x, by_y, last_low, last_high = scatter_tokens(keep, away, low)
        dhn_parts, out_parts = [keep, came, by_x, last_low], [keep, came, by_y, last_high]
    else:
        terms = jnp.concatenate([keep, away], axis=0)
        dhn_parts = [lax.psum_scatter(terms, axes, scatter_dimension=0, tiled=False)]
    dh, dattn, *do_mine, small = second_norm_back(
        hidden, hn, d_output, router_mixed, mask_own, norm2_gain[None, :], wo_list, dhn_parts, low
    )

    do_list = exchange_col(do_mine)
    dattn_late = after(dattn, do_list[2])
    dattn_list = [dattn_late] + [swap(dattn_late, "col", s) for s in (1, 2, 3)]
    dq, dbefore, dkv = attend_back(
        me, q4, kv_before, kv, start, lse, do_list, cos_table, sin_table, tok
    )
    lists, sums_list = [], []
    if split:
        sums_list = [
            lax.psum_scatter(grads, "row", scatter_dimension=0, tiled=False) for grads in grad_list
        ]

    def spread(sums):
        return exchange_col([sums[s] for s in range(col_count)])

    if split:
        lists = [spread(after(sums, do_list[2])) for sums in sums_list[: calls // 2]]
    dafter = lax.ppermute(dbefore, "row", [(i + 1, i) for i in range(row_count - 1)])
    dq, dattn_list = lax.optimization_barrier((dq, dattn_list))
    if two_way(axes):
        output = layer_output(after(hidden, dq), out_parts, low)
        dq, output, lists = lax.optimization_barrier((dq, output, lists))
    else:
        output = (hidden + dhn_parts[0][low:].astype(jnp.float32)).astype(jnp.bfloat16)
    dqkv, dx_keep, dx_away = project_back(me, dq, dkv, dafter, cos_table, sin_table, w_joined, tok)
    dx_came = swap(dx_away, "col", 1)
    grad_send, grad_keep = weight_grad(me, xn1, dqkv, heads, dattn_list, row_count)
    dx_came, grad_send = lax.optimization_barrier((dx_came, grad_send))
    grad_came = swap(grad_send, "dp", 1)
    dx_far = (dx_keep[1].astype(jnp.float32) + dx_came[1].astype(jnp.float32)).astype(jnp.bfloat16)
    dx_gone = swap(dx_far, "col", 2)

    if split:
        lists += [spread(after(sums, dx_far)) for sums in sums_list[calls // 2 : calls - 1]]
    dx_gone, lists, grad_came = lax.optimization_barrier((dx_gone, lists, grad_came))
    d_inputs, gain_one = first_norm_back(
        inputs, dh, norm1_gain[None, :], dx_keep, dx_came, dx_gone
    )
    small = jnp.concatenate([small[: EXPERTS + 1], gain_one[:1]], axis=0)
    small = sum_over(sum_over(small, "col"), "dp")

    grad_keep = after(grad_keep, d_inputs)
    pair = (grad_keep.astype(jnp.float32) + grad_came.astype(jnp.float32)).astype(jnp.bfloat16)
    mine = scatter_row([pair[s] for s in range(row_count)], small)
    mine, small = lax.optimization_barrier((mine, small))
    step = 2
    while step < dp_count:
        mine = mine + swap(mine.astype(jnp.bfloat16), "dp", step).astype(jnp.float32)
        step *= 2
    mine = mine.astype(jnp.bfloat16)
    other = swap(mine, "dp", 1)
    first, second = jnp.where(my_half == 0, mine, other), jnp.where(my_half == 0, other, mine)
    tall = width // row_count
    d_w_qkv = jnp.concatenate([first[:tall], second[:tall]], axis=1).astype(jnp.float32)
    d_w_output = jnp.concatenate([first[tall:], second[tall:]], axis=0).astype(jnp.float32)

    if split:
        lists.append(spread(after(sums_list[-1], mine)))
    small = sum_over(small, "row")
    if split:
        lists[-1] = lax.optimization_barrier((lists[-1], small, d_w_qkv))[0]
        d_w_gate, d_w_up, d_w_down = finish(me_first, lists)
        d_w_down = jnp.swapaxes(d_w_down, 1, 2)
    else:
        order = jnp.stack([my_col ^ s for s in range(col_count)])
        back = jnp.take(grad_list[0], order, axis=1)
        sums = lax.psum_scatter(
            back.reshape((row_count * col_count,) + back.shape[2:]),
            ("row", "col"),
            scatter_dimension=0,
            tiled=False,
        )
        d_w_gate = sums[:, 0].astype(jnp.float32)
        d_w_up = sums[:, 1].astype(jnp.float32)
        d_w_down = jnp.swapaxes(sums[:, 2], 1, 2).astype(jnp.float32)

    d_router = small[:EXPERTS].reshape(per_row, -1, width).swapaxes(0, 1).reshape(EXPERTS, width).T
    return (
        output,
        d_inputs,
        small[EXPERTS + 1],
        d_w_qkv[:, :query_cols],
        d_w_qkv[:, query_cols : query_cols + key_cols],
        d_w_qkv[:, query_cols + key_cols :],
        d_w_output,
        small[EXPERTS],
        d_router,
        d_w_gate,
        d_w_up,
        d_w_down,
    )


def solution(mesh):
    return jax.shard_map(
        on_device,
        mesh=mesh,
        in_specs=(
            P(("dp", "row", "col"), None),
            P("dp", None),
            P(("dp", "row", "col"), None),
            P(),
            P("row", "col"),
            P("row", "col"),
            P("row", "col"),
            P("col", "row"),
            P(),
            P(),
            P("dp", None, None),
            P("dp", None, None),
            P("dp", None, None),
            P(("dp", "row", "col"), None),
        ),
        out_specs=(
            P(("dp", "row", "col"), None),
            P(("dp", "row", "col"), None),
            P(),
            P("row", "col"),
            P("row", "col"),
            P("row", "col"),
            P("col", "row"),
            P(),
            P(),
            P("dp", ("row", "col"), None),
            P("dp", ("row", "col"), None),
            P("dp", None, ("row", "col")),
        ),
        check_vma=False,
    )
```
